32 devices in a mesh: section: 2 (over x), ctx: 4 (over y, core), tp: 4 (over z).
Axes of the slice: x: 2, y: 2, z: 4, core: 2. Of those that a mesh axis runs over, the one named last changes fastest.
Arguments:
- tokens_in: bfloat16 [8, 1024, 1, 2048], P(None, ('ctx', 'tp')), may hold values from -6 to 6
- cotangent: bfloat16 [8, 1024, 1, 2048], P(None, ('ctx', 'tp')), may hold values from -6 to 6
- plan: int32 [8], replicated, may hold values from 0 to 7, each once
- positions: int32 [1, 1024], replicated, may hold values from 0 to 2047, as said below
- norm_gain: float32 [2, 2, 2048], P('section'), may hold values from 0.5 to 1.5
- norm_shift: float32 [2, 2, 2048], P('section'), may hold values from -2 to 2
- w_qkv: bfloat16 [2, 3, 2048, 2048], P('section', None, None, 'tp'), may hold values from -0.125 to 0.125
- b_qkv: float32 [2, 3, 2048], P('section', None, 'tp'), may hold values from -2 to 2
- w_out: bfloat16 [2, 2048, 2048], P('section', 'tp'), may hold values from -1.5 to 1.5
- w_gate_up: bfloat16 [2, 2, 2048, 5632], P('section', None, None, 'tp'), may hold values from -0.125 to 0.125
- down_weight: bfloat16 [2, 5632, 2048], P('section', 'tp'), may hold values from -0.078125 to 0.078125
Outputs:
- section_ends: bfloat16 [2, 8, 1024, 1, 2048], P('section', None, ('ctx', 'tp'))
- grad_gain: float32 [2, 2, 2048], P('section', None, ('ctx', 'tp'))
- grad_shift: float32 [2, 2, 2048], P('section', None, ('ctx', 'tp'))
- grad_bias: float32 [2, 3, 2048], P('section', None, ('ctx', 'tp'))
- grad_qkv: float32 [2, 3, 2048, 2048], P('section', None, 'ctx', 'tp')
- grad_out: float32 [2, 2048, 2048], P('section', 'tp', 'ctx')
- grad_gate_up: float32 [2, 2, 2048, 5632], P('section', None, 'ctx', 'tp')
- grad_down: float32 [2, 5632, 2048], P('section', 'tp', 'ctx')
The draws below stay inside these ranges and needn't reach their ends.
Inputs may be any that keep to these rules, and one draw needn't show every extreme that they name: Each sequence's positions rise strictly from one token to the next, by 1 to 3; every sequence starts at the least and ends at the most.
All inputs are finite; a program needn't handle non-finite values.
Results may differ from the reference program's by a relative error of at most 0.02.
Values may be sent and summed in bfloat16 or wider, within the bound.
No kernel may reach another device: no remote copies, remote signals or barrier semaphores. Data moves between devices by JAX's collectives and lax.ppermute only.
A program may use at most 320 MiB of HBM per device.

```python
import jax
import jax.numpy as jnp
from jax import lax

D = 2048
HEADS = 32
HEAD_WIDTH = 64
ROT = 16
FF = 5632
SEQS = 1
MB = 8
LEN = 1024


def draw_positions(key, part):
    offsets = jax.random.randint(key, (SEQS, LEN), 0, 2)
    index_row = jnp.arange(LEN, dtype=jnp.int32)[None, :]
    offsets = jnp.where(index_row == 0, 0, offsets)
    offsets = jnp.where(index_row == LEN - 1, 1, offsets)
    return (2 * index_row + offsets).astype(jnp.int32)


def shard_levels(stream_key, extent, pieces, least, largest):
    gain = 1.0
    for dim, parts in pieces:
        heights = jax.random.uniform(jax.random.fold_in(jax.random.fold_in(stream_key, 6), dim), (parts,), jnp.float32, least / len(pieces), largest / len(pieces))
        gain = gain * jnp.repeat(jnp.exp(heights), extent[dim] // parts).reshape((-1,) + (1,) * (len(extent) - 1 - dim))
    return gain


def bell_draw(own_key, extent, deviation, limit, cuts=(), kind=jnp.bfloat16):
    level = shard_levels(own_key, extent, cuts, -0.22, 0.18) if cuts else 1.0
    entries = jax.random.normal(own_key, extent, jnp.float32) * deviation * level
    return jnp.minimum(jnp.maximum(entries, -limit), limit).astype(kind)


def setup_inputs(seed: int = 0) -> dict:
    arg_keys = jax.random.split(jax.random.key(seed), 12)
    return {
        "tokens_in": bell_draw(arg_keys[0], (MB, LEN, SEQS, D), 1.0, 6.0, ((1, 16),)),
        "cotangent": bell_draw(arg_keys[1], (MB, LEN, SEQS, D), 1.0, 6.0, ((1, 16),)),
        "plan": jax.random.permutation(arg_keys[2], MB).astype(jnp.int32),
        "positions": draw_positions(jax.random.fold_in(arg_keys[11], 71), 0),
        "norm_gain": jnp.clip(1.0 + 0.1 * jax.random.normal(arg_keys[4], (2, 2, D), jnp.float32), 0.5, 1.5),
        "norm_shift": bell_draw(arg_keys[5], (2, 2, D), 0.3, 2.0, ((0, 2),), jnp.float32),
        "w_qkv": bell_draw(arg_keys[6], (2, 3, D, D), D ** -0.5, 0.125, ((0, 2), (3, 4))),
        "b_qkv": bell_draw(arg_keys[7], (2, 3, D), 0.3, 2.0, ((0, 2), (2, 4)), jnp.float32),
        "w_out": bell_draw(arg_keys[8], (2, D, D), (D // 128) ** -0.5, 1.5, ((0, 2), (1, 4))),
        "w_gate_up": bell_draw(arg_keys[9], (2, 2, D, FF), D ** -0.5, 0.125, ((0, 2), (3, 4))),
        "down_weight": bell_draw(arg_keys[10], (2, FF, D), FF ** -0.5, 0.078125, ((0, 2), (1, 4))),
    }


@jax.custom_vjp
def low(v):
    return lax.optimization_barrier(v.astype(jnp.bfloat16)).astype(jnp.float32)

@jax.custom_vjp
def low_back(v):
    return v

def low_keep(v):
    return (low(v), None)

def low_pass(kept, grad):
    return (grad,)

def back_keep(v):
    return (v, None)

def back_low(kept, grad):
    return (low(grad),)
low.defvjp(low_keep, low_pass)
low_back.defvjp(back_keep, back_low)

def elementwise_product(form, left, right):
    return jnp.einsum(form, left, right, precision=lax.Precision.HIGHEST)

def normalize(stream, gain_vec, shift_vec):
    centre = stream - lax.optimization_barrier(jnp.mean(stream, axis=-1, keepdims=True))
    spread = lax.optimization_barrier(jnp.mean(centre * centre, axis=-1, keepdims=True))
    return centre * lax.rsqrt(spread + 1e-05) * gain_vec + shift_vec

def rotary(tensor, cosine, sine):
    half_rot = ROT // 2
    front = tensor[..., :ROT]
    turned = jnp.concatenate([-front[..., half_rot:], front[..., :half_rot]], axis=-1)
    return jnp.concatenate([front * cosine + turned * sine, tensor[..., ROT:]], axis=-1)

def tables(position_rows):
    freqs = 10000.0 ** (-jnp.arange(ROT // 2, dtype=jnp.float32) * 2.0 / ROT)
    angles = position_rows.T.astype(jnp.float32)[:, :, None] * freqs
    angles = jnp.concatenate([angles, angles], axis=-1)[:, :, None, :]
    return (jnp.cos(angles), jnp.sin(angles))

def attend(queries, key_rows, value_rows, allowed):
    scores = low_back(elementwise_product('qse,kse->sqk', queries, key_rows) * HEAD_WIDTH ** (-0.5))
    scores = jnp.where(allowed, scores, -1e+30)
    probability = jax.nn.softmax(scores, axis=-1)
    return elementwise_product('sqk,kse->qse', low(probability), value_rows)

def layer(stream, weights, index, cosine, sine, allowed):
    gain_vec = weights[0][index]
    shift_vec = weights[1][index]
    w_qkv = weights[2][index]
    b_qkv = weights[3][index]
    w_out = weights[4][index]
    w_gate_up = weights[5][index]
    down_weight = weights[6][index]
    length = stream.shape[0]
    seq_count = stream.shape[1]
    normed = low(normalize(stream, gain_vec[0], shift_vec[0]))
    mixed = low_back(elementwise_product('lsd,cde->clse', normed, w_qkv) + b_qkv[:, None, None, :])
    queries = low(rotary(mixed[0].reshape(length, seq_count, HEADS, HEAD_WIDTH), cosine, sine))
    key_rows = low(rotary(mixed[1].reshape(length, seq_count, HEADS, HEAD_WIDTH), cosine, sine))
    value_rows = low(mixed[2].reshape(length, seq_count, HEADS, HEAD_WIDTH))

    def one_head(bundle):
        return attend(bundle[0], bundle[1], bundle[2], allowed)
    per_head = lax.map(jax.checkpoint(one_head), (jnp.moveaxis(queries, 2, 0), jnp.moveaxis(key_rows, 2, 0), jnp.moveaxis(value_rows, 2, 0)))
    attended = jnp.moveaxis(per_head, 0, 2).reshape(length, seq_count, D)
    attended = low_back(low(attended))
    hidden_state = stream + low_back(elementwise_product('lse,ed->lsd', attended, w_out))
    normed_two = low(normalize(hidden_state, gain_vec[1], shift_vec[1]))
    gate_up = low_back(elementwise_product('lsd,cdf->clsf', normed_two, w_gate_up))
    gated_activation = low(jax.nn.silu(gate_up[0]) * gate_up[1])
    return hidden_state + low_back(elementwise_product('xiv,vg->xig', gated_activation, down_weight))

def reference(tokens_in, cotangent, plan, positions, norm_gain, norm_shift, w_qkv, b_qkv, w_out, w_gate_up, down_weight):
    params = tuple((array.astype(jnp.float32) for array in (norm_gain, norm_shift, w_qkv, b_qkv, w_out, w_gate_up, down_weight)))
    cosine, sine = tables(positions)
    allowed = positions[:, None, :] <= positions[:, :, None]

    def network(weights, stream):
        first_out = layer(stream, weights, 0, cosine, sine, allowed)
        middle = low_back(low(first_out))
        return layer(middle, weights, 1, cosine, sine, allowed)

    def one_micro(totals, micro):
        stream = tokens_in[plan[micro]].astype(jnp.float32)
        final_out, pull = jax.vjp(network, params, stream)
        weight_grads, input_grad = pull(cotangent[micro].astype(jnp.float32))
        totals = jax.tree.map(jnp.add, totals, weight_grads)
        return (totals, (input_grad.astype(jnp.bfloat16), final_out.astype(jnp.bfloat16)))
    start_totals = jax.tree.map(jnp.zeros_like, params)
    totals, (input_grads, final_outs) = lax.scan(one_micro, start_totals, jnp.arange(MB, dtype=jnp.int32))
    section_ends = jnp.stack([input_grads, final_outs])
    return (section_ends, totals[0], totals[1], totals[3], totals[2], totals[4], totals[5], totals[6])
```

```python
import functools

import jax
import jax.numpy as jnp
from jax import lax
from jax.experimental import pallas as pl
from jax.experimental.pallas import tpu as pltpu
from jax.sharding import PartitionSpec as P

HEAD_WIDTH = 64
ROT = 16


def pair_routes(ctx_count):
    core = [(i, i ^ 1) for i in range(ctx_count)]
    across = [(i, (i + 2) % 4) for i in range(ctx_count)]
    return core, across


def ln_stats(stream):
    mean = jnp.mean(stream, axis=-1, keepdims=True)
    centre = stream - mean
    inv_std = lax.rsqrt(jnp.mean(centre * centre, axis=-1, keepdims=True) + 1e-05)
    return centre, inv_std


def ln(stream, gain_vec, shift_vec):
    centre, inv_std = ln_stats(stream)
    return (centre * inv_std * gain_vec + shift_vec).astype(jnp.bfloat16)


def ln_back(stream, grad_in, gain_vec):
    centre, inv_std = ln_stats(stream)
    unit = centre * inv_std
    scaled = grad_in * gain_vec
    result = inv_std * (
        scaled
        - jnp.mean(scaled, axis=-1, keepdims=True)
        - unit * jnp.mean(scaled * unit, axis=-1, keepdims=True)
    )
    return result, jnp.sum(grad_in * unit, axis=0), jnp.sum(grad_in, axis=0)


def rot_tables(pos_row):
    half = ROT // 2
    freqs = 10000.0 ** (-jnp.arange(half, dtype=jnp.float32) * 2.0 / ROT)
    angles = pos_row.astype(jnp.float32)[:, None] * freqs
    cosine, sine = jnp.cos(angles), jnp.sin(angles)
    rows = pos_row.shape[0]
    rest = HEAD_WIDTH - ROT
    zeros = jnp.zeros((rows, half), jnp.float32)
    cos_head = jnp.concatenate([cosine, cosine, jnp.ones((rows, rest), jnp.float32)], 1)
    low_head = jnp.concatenate([-sine, zeros, jnp.zeros((rows, rest), jnp.float32)], 1)
    high_head = jnp.concatenate([zeros, sine, jnp.zeros((rows, rest), jnp.float32)], 1)
    return tuple(jnp.concatenate([t, t], 1) for t in (cos_head, low_head, high_head))


def dot_t(a, b):
    return lax.dot_general(a, b, (((1,), (1,)), ((), ())), preferred_element_type=jnp.float32)


def dot_0(a, b):
    return lax.dot_general(a, b, (((0,), (0,)), ((), ())), preferred_element_type=jnp.float32)


def dot_n(a, b):
    return lax.dot_general(a, b, (((1,), (0,)), ((), ())), preferred_element_type=jnp.float32)


def chunked(x, chunk):
    half = x.shape[0] // 2
    pieces = []
    for i in range(half // chunk):
        pieces.append(x[i * chunk : (i + 1) * chunk])
        pieces.append(x[half + i * chunk : half + (i + 1) * chunk])
    return jnp.concatenate(pieces, axis=0)


def attn_fwd_kernel(heads, chunk, mixed, bias, cos_t, low_t, high_t, pos_c, pos_r, qkv, out):
    rows = mixed.shape[0]
    half = rows // 2
    width = heads * HEAD_WIDTH
    half_rot = ROT // 2
    cosine, low, high = cos_t[...], low_t[...], high_t[...]
    for pair in range(heads // 2):
        parts = []
        for c in range(3):
            at = c * width + pair * 128
            x = mixed[:, at : at + 128] + bias[0, :, at : at + 128]
            if c < 2:
                x = x * cosine + pltpu.roll(x, 128 - half_rot, 1) * low + pltpu.roll(x, half_rot, 1) * high
            x = x.astype(jnp.bfloat16)
            qkv[:, at : at + 128] = x
            parts.append(chunked(x, chunk))
        query, key, value = parts
        query = query * jnp.bfloat16(HEAD_WIDTH ** (-0.5))
        for i in range(half // chunk):
            end = 2 * chunk * (i + 1)
            begin = end - 2 * chunk
            allowed = pos_r[:, begin:end] <= pos_c[begin:end, :]
            halves = []
            for h in range(2):
                lanes = slice(h * HEAD_WIDTH, (h + 1) * HEAD_WIDTH)
                q_h = query[begin:end, lanes]
                score = dot_t(q_h, key[:end, lanes])
                last = jnp.where(allowed, score[:, begin:], -1e30)
                score = last if i == 0 else jnp.concatenate([score[:, :begin], last], axis=1)
                prob = jnp.exp(score - jnp.max(score, axis=1, keepdims=True))
                total = jnp.sum(prob, axis=1, keepdims=True)
                mixed_values = dot_n(prob.astype(jnp.bfloat16), value[:end, lanes])
                halves.append(mixed_values / total)
            done = jnp.concatenate(halves, axis=1).astype(jnp.bfloat16)
            lanes = slice(pair * 128, pair * 128 + 128)
            out[i * chunk : (i + 1) * chunk, lanes] = done[:chunk]
            out[half + i * chunk : half + (i + 1) * chunk, lanes] = done[chunk:]


def attn_bwd_kernel(heads, chunk, qkv, ctx, cos_t, low_t, high_t, pos_c, pos_r, grad, bias_grad, dk_s, dv_s):
    rows = qkv.shape[0]
    half = rows // 2
    width = heads * HEAD_WIDTH
    half_rot = ROT // 2
    cosine, low, high = cos_t[...], low_t[...], high_t[...]
    scale = HEAD_WIDTH ** (-0.5)

    def finish(c, pair, x):
        at = c * width + pair * 128
        if c < 2:
            x = x * scale
            x = x * cosine + pltpu.roll(x * high, 128 - half_rot, 1) + pltpu.roll(x * low, half_rot, 1)
        x = x.astype(jnp.bfloat16)
        grad[:, at : at + 128] = x
        bias_grad[0, :, at : at + 128] = jnp.sum(x.astype(jnp.float32), axis=0, keepdims=True)

    def unchunked(x):
        steps = half // chunk
        own = [x[2 * i * chunk : (2 * i + 1) * chunk] for i in range(steps)]
        other = [x[(2 * i + 1) * chunk : (2 * i + 2) * chunk] for i in range(steps)]
        return jnp.concatenate(own + other, axis=0)

    for pair in range(heads // 2):
        lanes2 = slice(pair * 128, pair * 128 + 128)
        query, key, value = (
            chunked(qkv[:, c * width + pair * 128 : c * width + pair * 128 + 128], chunk) for c in range(3)
        )
        query_s = query * jnp.bfloat16(scale)
        ctx_grad = chunked(ctx[:, lanes2], chunk)
        dk_s[...] = jnp.zeros_like(dk_s)
        dv_s[...] = jnp.zeros_like(dv_s)
        dq_parts = []
        for i in range(half // chunk):
            end = 2 * chunk * (i + 1)
            begin = end - 2 * chunk
            allowed = pos_c[begin:end, :] <= pos_r[:, begin:end]
            dq_h, dk_h, dv_h = [], [], []
            for h in range(2):
                lanes = slice(h * HEAD_WIDTH, (h + 1) * HEAD_WIDTH)
                score = dot_t(key[:end, lanes], query_s[begin:end, lanes])
                last = jnp.where(allowed, score[begin:, :], -1e30)
                score = last if i == 0 else jnp.concatenate([score[:begin, :], last], axis=0)
                prob = jnp.exp(score - jnp.max(score, axis=0, keepdims=True))
                prob = prob * (1.0 / jnp.sum(prob, axis=0, keepdims=True))
                grad_h = ctx_grad[begin:end, lanes]
                dv_h.append(dot_n(prob.astype(jnp.bfloat16), grad_h))
                prob_grad = dot_t(value[:end, lanes], grad_h)
                delta = jnp.sum(prob * prob_grad, axis=0, keepdims=True)
                score_grad = (prob * (prob_grad - delta)).astype(jnp.bfloat16)
                dk_h.append(dot_n(score_grad, query[begin:end, lanes]))
                dq_h.append(dot_0(score_grad, key[:end, lanes]))
            dk_s[:end, :] += jnp.concatenate(dk_h, axis=1)
            dv_s[:end, :] += jnp.concatenate(dv_h, axis=1)
            dq_parts.append(jnp.concatenate(dq_h, axis=1))
        finish(0, pair, unchunked(jnp.concatenate(dq_parts, axis=0)))
        finish(1, pair, unchunked(dk_s[...]))
        finish(2, pair, unchunked(dv_s[...]))


VMEM_LIMIT = 56 * 1024 * 1024


def attn_fwd(mixed, bias, context, groups, chunk):
    rows, columns = mixed.shape
    block = columns // groups
    heads = block // (3 * HEAD_WIDTH)
    cos_t, low_t, high_t, pos_c, pos_r = context
    whole = lambda shape: pl.BlockSpec(shape, lambda g: (0, 0))
    return pl.pallas_call(
        functools.partial(attn_fwd_kernel, heads, chunk),
        grid=(groups,),
        in_specs=[
            pl.BlockSpec((rows, block), lambda g: (0, g)),
            pl.BlockSpec((1, 1, block), lambda g: (g, 0, 0)),
            whole((rows, 128)),
            whole((rows, 128)),
            whole((rows, 128)),
            whole((rows, 1)),
            whole((1, rows)),
        ],
        out_specs=[
            pl.BlockSpec((rows, block), lambda g: (0, g)),
            pl.BlockSpec((rows, block // 3), lambda g: (0, g)),
        ],
        out_shape=[
            jax.ShapeDtypeStruct((rows, columns), jnp.bfloat16),
            jax.ShapeDtypeStruct((rows, columns // 3), jnp.bfloat16),
        ],
        compiler_params=pltpu.CompilerParams(vmem_limit_bytes=VMEM_LIMIT),
        cost_estimate=pl.CostEstimate(
            flops=3 * rows * rows * columns // 3 * 4,
            bytes_accessed=rows * columns * 7,
            transcendentals=rows * rows * columns // (3 * HEAD_WIDTH),
        ),
    )(mixed, bias.reshape(groups, 1, block), cos_t, low_t, high_t, pos_c, pos_r)


def attn_bwd(qkv, ctx_grad, context, groups, chunk):
    rows, columns = qkv.shape
    block = columns // groups
    heads = block // (3 * HEAD_WIDTH)
    cos_t, low_t, high_t, pos_c, pos_r = context
    whole = lambda shape: pl.BlockSpec(shape, lambda g: (0, 0))
    return pl.pallas_call(
        functools.partial(attn_bwd_kernel, heads, chunk),
        grid=(groups,),
        in_specs=[
            pl.BlockSpec((rows, block), lambda g: (0, g)),
            pl.BlockSpec((rows, block // 3), lambda g: (0, g)),
            whole((rows, 128)),
            whole((rows, 128)),
            whole((rows, 128)),
            whole((rows, 1)),
            whole((1, rows)),
        ],
        out_specs=[
            pl.BlockSpec((rows, block), lambda g: (0, g)),
            pl.BlockSpec((1, 1, block), lambda g: (g, 0, 0)),
        ],
        out_shape=[
            jax.ShapeDtypeStruct((rows, columns), jnp.bfloat16),
            jax.ShapeDtypeStruct((groups, 1, block), jnp.float32),
        ],
        scratch_shapes=[pltpu.VMEM((rows, 128), jnp.float32), pltpu.VMEM((rows, 128), jnp.float32)],
        compiler_params=pltpu.CompilerParams(vmem_limit_bytes=VMEM_LIMIT),
        cost_estimate=pl.CostEstimate(
            flops=7 * rows * rows * columns // 3 * 4,
            bytes_accessed=rows * columns * 5,
            transcendentals=rows * rows * columns // (3 * HEAD_WIDTH),
        ),
    )(qkv, ctx_grad, cos_t, low_t, high_t, pos_c, pos_r)


def bulk_device(
    tokens_in,
    cotangent,
    plan,
    positions,
    norm_gain,
    norm_shift,
    w_qkv,
    b_qkv,
    w_out,
    w_gate_up,
    down_weight,
):
    tp_count = lax.axis_size("tp")
    ctx_count = lax.axis_size("ctx")
    section_index = lax.axis_index("section")
    ctx_index = lax.axis_index("ctx")
    side, core = ctx_index // 2, ctx_index % 2
    core_route, across_route = pair_routes(ctx_count)
    micro_count, slice_len, _, width = tokens_in.shape
    gain, shift = norm_gain[0], norm_shift[0]
    piece = slice_len // 2
    rows = micro_count * slice_len * 2
    own_rows = rows // 2
    half_width = width // 2
    columns = w_qkv.shape[3] // 2
    hidden = w_gate_up.shape[3] // 2
    first = section_index == 0

    ordered = jnp.stack(
        [lax.dynamic_index_in_dim(tokens_in, plan[m], 0, keepdims=False)[:, 0] for m in range(micro_count)]
    )
    fresh = jnp.where(first, ordered, cotangent[:, :, 0])
    fresh = fresh.reshape(ctx_count // 2, tp_count, 2, piece, width).transpose(0, 2, 1, 3, 4)
    fresh = fresh.reshape(ctx_count * tp_count, piece, width)
    inbound = lax.all_to_all(fresh, ("ctx", "tp"), 0, 0, tiled=True).reshape(own_rows, width)

    pos = positions.reshape(-1, 2, piece)
    pos = jnp.concatenate(
        [
            lax.dynamic_index_in_dim(pos, core, 1, False).reshape(-1),
            lax.dynamic_index_in_dim(pos, 1 - core, 1, False).reshape(-1),
        ]
    )
    chunk = min(128, own_rows)
    chunk_pos = chunked(pos, chunk)
    context = (*rot_tables(pos), chunk_pos[:, None], chunk_pos[None, :])

    def gathered(block):
        own = lax.all_gather(block, "tp", axis=0, tiled=True)
        other = lax.ppermute(own, "ctx", across_route)
        return jnp.where(
            side == 0, jnp.concatenate([own, other], axis=1), jnp.concatenate([other, own], axis=1)
        )

    d_from = side * half_width
    qkv_block = lax.dynamic_slice(w_qkv[0], (0, d_from, core * columns), (3, half_width, columns))
    qkv_block = qkv_block.transpose(0, 2, 1).reshape(3 * columns, half_width)
    out_block = lax.dynamic_slice(w_out[0], (core * columns, d_from), (columns, half_width))
    gu_block = lax.dynamic_slice(w_gate_up[0], (0, d_from, core * hidden), (2, half_width, hidden))
    gu_block = gu_block.transpose(0, 2, 1)
    down_block = lax.dynamic_slice(down_weight[0], (core * hidden, d_from), (hidden, half_width))
    wt_qkv = gathered(qkv_block)
    wt_out = gathered(out_block)
    wt_gu = jnp.concatenate([gathered(gu_block[0]), gathered(gu_block[1])], axis=0)
    wt_down = gathered(down_block)
    bias_all = lax.all_gather(b_qkv[0], "tp", axis=0)
    bias = lax.dynamic_slice_in_dim(bias_all, core * columns, columns, 2).reshape(tp_count, 3 * columns)
    ff = wt_down.shape[0]

    def both(own):
        return jnp.concatenate([own, lax.ppermute(own, "ctx", core_route)], axis=0)

    def summed(a, weight):
        other = dot_n(a[own_rows:], weight).astype(jnp.bfloat16)
        arriving = lax.ppermute(other, "ctx", core_route)
        return dot_n(a[:own_rows], weight) + arriving.astype(jnp.float32)

    def forward(stream):
        normed = both(ln(stream, gain[0], shift[0]))
        mixed = dot_t(normed, wt_qkv)
        qkv, attended = attn_fwd(mixed, bias, context, tp_count, chunk)
        hidden_state = stream + summed(attended, wt_out)
        normed_two = both(ln(hidden_state, gain[1], shift[1]))
        gate_up = dot_t(normed_two, wt_gu)
        gate, up = gate_up[:, :ff], gate_up[:, ff:]
        activation = (jax.nn.silu(gate) * up).astype(jnp.bfloat16)
        out = (hidden_state + summed(activation, wt_down)).astype(jnp.bfloat16)
        return out, (stream, normed, qkv, attended, hidden_state, normed_two, gate_up, activation)

    def backward(grad_out, stored):
        stream, normed, qkv, attended, hidden_state, normed_two, gate_up, activation = stored
        mlp_grad = both(grad_out)
        act_grad = dot_t(mlp_grad, wt_down)
        gate, up = gate_up[:, :ff], gate_up[:, ff:]
        sigma = jax.nn.sigmoid(gate)
        gu_grad = jnp.concatenate(
            [act_grad * up * sigma * (1.0 + gate * (1.0 - sigma)), act_grad * gate * sigma], axis=1
        ).astype(jnp.bfloat16)
        two_grad = summed(gu_grad, wt_gu)
        result, gain_two, shift_two = ln_back(hidden_state, two_grad, gain[1])
        hidden_grad = grad_out.astype(jnp.float32) + result
        attn_grad = both(hidden_grad.astype(jnp.bfloat16))
        ctx_grad = dot_t(attn_grad, wt_out).astype(jnp.bfloat16)
        qkv_grad, bias_grad = attn_bwd(qkv, ctx_grad, context, tp_count, chunk)
        one_grad = summed(qkv_grad, wt_qkv)
        result, gain_one, shift_one = ln_back(stream, one_grad, gain[0])
        input_grad = (hidden_grad + result).astype(jnp.bfloat16)
        small = (jnp.stack([gain_one, gain_two]), jnp.stack([shift_one, shift_two]), bias_grad)
        pairs = ((activation, mlp_grad), (gu_grad, normed_two), (attended, attn_grad), (qkv_grad, normed))
        return input_grad, small, pairs

    sent, _ = forward(inbound.astype(jnp.float32))
    arriving = lax.ppermute(sent, "section", [(0, 1)])
    final_out, stored = forward(jnp.where(first, inbound, arriving).astype(jnp.float32))
    sent_back, _, _ = backward(inbound, stored)
    arriving_back = lax.ppermute(sent_back, "section", [(1, 0)])
    grad_out = jnp.where(first, arriving_back, inbound)
    input_grad, small, pairs = backward(grad_out, stored)

    def weight_grad(pair):
        left, right = pair
        far = lax.dynamic_slice_in_dim(right, (1 - side) * half_width, half_width, 1)
        near = lax.dynamic_slice_in_dim(right, side * half_width, half_width, 1)
        arriving = lax.ppermute(dot_0(left, far).astype(jnp.bfloat16), "ctx", across_route)
        total = (dot_0(left, near) + arriving.astype(jnp.float32)).astype(jnp.bfloat16)
        return lax.psum_scatter(total, "tp", scatter_dimension=0, tiled=True)

    def settled(term):
        share = half_width // 2
        away = lax.dynamic_slice_in_dim(term, (1 - core) * share, share, term.ndim - 1)
        kept = lax.dynamic_slice_in_dim(term, core * share, share, term.ndim - 1)
        got = lax.ppermute(away, "ctx", core_route)
        axis = term.ndim - 2
        return jnp.where(
            core == 0, jnp.concatenate([kept, got], axis), jnp.concatenate([got, kept], axis)
        ).astype(jnp.float32)

    act_pair, gu_pair, out_pair, qkv_pair = pairs
    grad_down = settled(weight_grad(act_pair))
    gu_left, gu_right = gu_pair
    grad_gate = settled(weight_grad((gu_left[:, :ff], gu_right)))
    grad_up = settled(weight_grad((gu_left[:, ff:], gu_right)))
    grad_out_w = settled(weight_grad(out_pair))
    grad_qkv = settled(weight_grad(qkv_pair).reshape(3, columns, half_width))

    gain_terms, shift_terms, bias_terms = small
    bias_terms = bias_terms.reshape(tp_count, 3, columns).transpose(1, 0, 2)[:, :, None]
    bias_full = jnp.where(
        (jnp.arange(2) == core)[None, None, :, None], bias_terms, 0.0
    ).reshape(3, tp_count * 2 * columns)
    vectors = jnp.concatenate([gain_terms, shift_terms, bias_full], axis=0)
    vectors = lax.psum_scatter(vectors, ("ctx", "tp"), scatter_dimension=1, tiled=True)

    ends = jnp.where(first, input_grad, final_out).reshape(ctx_count * tp_count, piece, width)
    ends = lax.all_to_all(ends, ("ctx", "tp"), 0, 0, tiled=True)
    ends = ends.reshape(ctx_count // 2, 2, tp_count, piece, width).transpose(0, 2, 1, 3, 4)
    ends = ends.reshape(micro_count, slice_len, 1, width)
    return (
        ends[None],
        vectors[None, :2],
        vectors[None, 2:4],
        vectors[None, 4:],
        grad_qkv.transpose(0, 2, 1)[None],
        grad_out_w[None],
        jnp.stack([grad_gate.T, grad_up.T])[None],
        grad_down[None],
    )


def passed_along(block, axis, distance):
    devices = range(lax.axis_size(axis))
    route = [(i - distance, i) for i in devices if i - distance in devices]
    return lax.ppermute(block, axis, route)


def normalize(stream, gain_vec, shift_vec):
    centre = stream - jnp.mean(stream, axis=-1, keepdims=True)
    spread = jnp.mean(centre * centre, axis=-1, keepdims=True)
    return centre * lax.rsqrt(spread + 1e-05) * gain_vec + shift_vec


def norm_back(stream, grad_in, gain_vec):
    centre = stream - jnp.mean(stream, axis=-1, keepdims=True)
    inv_std = lax.rsqrt(jnp.mean(centre * centre, axis=-1, keepdims=True) + 1e-05)
    unit = centre * inv_std
    scaled = grad_in * gain_vec
    result = inv_std * (
        scaled
        - jnp.mean(scaled, axis=-1, keepdims=True)
        - unit * jnp.mean(scaled * unit, axis=-1, keepdims=True)
    )
    return (result, jnp.sum(grad_in * unit, axis=(0, 1)), jnp.sum(grad_in, axis=(0, 1)))


def rotary(tensor, cosine, sine):
    half_rot = ROT // 2
    front = tensor[..., :ROT]
    turned = jnp.concatenate([-front[..., half_rot:], front[..., :half_rot]], axis=-1)
    return jnp.concatenate([front * cosine + turned * sine, tensor[..., ROT:]], axis=-1)


def unrotary(tensor, cosine, sine):
    half_rot = ROT // 2
    front = tensor[..., :ROT]
    turned = jnp.concatenate([-front[..., half_rot:], front[..., :half_rot]], axis=-1)
    return jnp.concatenate([front * cosine - turned * sine, tensor[..., ROT:]], axis=-1)


def tables(position_rows):
    freqs = 10000.0 ** (-jnp.arange(ROT // 2, dtype=jnp.float32) * 2.0 / ROT)
    angles = position_rows.T.astype(jnp.float32)[:, :, None] * freqs
    angles = jnp.concatenate([angles, angles], axis=-1)[:, :, None, :]
    return (jnp.cos(angles), jnp.sin(angles))


def attention_scores(queries, key_heads, allowed):
    scores = jnp.einsum(
        "qshe,kshe->shqk", queries, key_heads, preferred_element_type=jnp.float32
    ) * HEAD_WIDTH ** (-0.5)
    return jnp.where(allowed, scores, -1e30)


def forward_layer(layer_in, weights, context_rows):
    gain_vec, shift_vec, w_qkv, b_qkv, w_out, w_gate_up, down_weight = weights
    cosine, sine, allowed = context_rows
    normed = normalize(layer_in, gain_vec[0], shift_vec[0]).astype(jnp.bfloat16)
    normed_all = lax.all_gather(normed, "tp", axis=0, tiled=True)
    block_len, seq_count, width = normed_all.shape
    columns = w_qkv.shape[2]
    head_count = columns // HEAD_WIDTH
    mixed = (
        jnp.einsum("rsd,cde->crse", normed_all, w_qkv, preferred_element_type=jnp.float32)
        + b_qkv[:, None, None, :]
    )
    queries = rotary(
        mixed[0].reshape(block_len, seq_count, head_count, HEAD_WIDTH), cosine, sine
    ).astype(jnp.bfloat16)
    key_own = rotary(
        mixed[1].reshape(block_len, seq_count, head_count, HEAD_WIDTH), cosine, sine
    ).astype(jnp.bfloat16)
    key_own = key_own.reshape(block_len, seq_count, columns)
    value_own = mixed[2].astype(jnp.bfloat16)
    key_all, value_all = (
        lax.all_gather(key_own, "ctx", axis=0, tiled=True),
        lax.all_gather(value_own, "ctx", axis=0, tiled=True),
    )
    key_heads = key_all.reshape(key_all.shape[0], seq_count, head_count, HEAD_WIDTH)
    value_heads = value_all.reshape(value_all.shape[0], seq_count, head_count, HEAD_WIDTH)
    scores = attention_scores(queries, key_heads, allowed)
    top_score = jnp.max(scores, axis=-1, keepdims=True)
    log_total = top_score + jnp.log(jnp.sum(jnp.exp(scores - top_score), axis=-1, keepdims=True))
    probability = jnp.exp(scores - log_total)
    attended = jnp.einsum(
        "shqk,kshe->qshe",
        probability.astype(jnp.bfloat16),
        value_heads,
        preferred_element_type=jnp.float32,
    )
    attended = attended.astype(jnp.bfloat16).reshape(block_len, seq_count, columns)
    piece = attended
    hidden_state = layer_in + lax.psum_scatter(
        jnp.einsum("rse,ed->rsd", piece, w_out, preferred_element_type=jnp.float32).astype(
            jnp.bfloat16
        ),
        "tp",
        scatter_dimension=0,
        tiled=True,
    ).astype(jnp.float32)
    normed_two = normalize(hidden_state, gain_vec[1], shift_vec[1]).astype(jnp.bfloat16)
    normed_two_all = lax.all_gather(normed_two, "tp", axis=0, tiled=True)
    gate_up = jnp.einsum(
        "rsd,cdf->crsf", normed_two_all, w_gate_up, preferred_element_type=jnp.float32
    )
    gated_activation = (jax.nn.silu(gate_up[0]) * gate_up[1]).astype(jnp.bfloat16)
    piece = gated_activation
    layer_out = hidden_state + lax.psum_scatter(
        jnp.einsum("rsf,fd->rsd", piece, down_weight, preferred_element_type=jnp.float32).astype(
            jnp.bfloat16
        ),
        "tp",
        scatter_dimension=0,
        tiled=True,
    ).astype(jnp.float32)
    stored = (
        layer_in,
        normed_all,
        queries,
        key_all,
        value_all,
        log_total,
        attended,
        hidden_state,
        normed_two_all,
        gate_up,
    )
    return (layer_out, stored)


def backward_layer(grad_out, stored, weights, context_rows):
    gain_vec, shift_vec, w_qkv, b_qkv, w_out, w_gate_up, down_weight = weights
    cosine, sine, allowed = context_rows
    (
        layer_in,
        normed_all,
        queries,
        key_all,
        value_all,
        log_total,
        attended,
        hidden_state,
        normed_two_all,
        gate_up,
    ) = stored
    block_len, seq_count, columns = attended.shape
    head_count = columns // HEAD_WIDTH
    mlp_grad = lax.all_gather(grad_out.astype(jnp.bfloat16), "tp", axis=0, tiled=True)
    gate_part = gate_up[0]
    up_part = gate_up[1]
    sigma = jax.nn.sigmoid(gate_part)
    swish = gate_part * sigma
    gated_activation = (swish * up_part).astype(jnp.bfloat16)
    down_grad = jnp.einsum(
        "rsf,rsd->fd", gated_activation, mlp_grad, preferred_element_type=jnp.float32
    )
    act_grad = jnp.einsum("rsd,fd->rsf", mlp_grad, down_weight, preferred_element_type=jnp.float32)
    gate_up_grad = jnp.stack(
        [act_grad * up_part * sigma * (1.0 + gate_part * (1.0 - sigma)), act_grad * swish]
    ).astype(jnp.bfloat16)
    gu_grad = jnp.einsum(
        "rsd,crsf->cdf", normed_two_all, gate_up_grad, preferred_element_type=jnp.float32
    )
    piece = gate_up_grad
    two_grad = lax.psum_scatter(
        jnp.einsum("crsf,cdf->rsd", piece, w_gate_up, preferred_element_type=jnp.float32).astype(
            jnp.bfloat16
        ),
        "tp",
        scatter_dimension=0,
        tiled=True,
    ).astype(jnp.float32)
    hidden_grad, gain_two, shift_two = norm_back(hidden_state, two_grad, gain_vec[1])
    hidden_grad = grad_out + hidden_grad
    attn_grad = lax.all_gather(hidden_grad.astype(jnp.bfloat16), "tp", axis=0, tiled=True)
    out_grad = jnp.einsum("rse,rsd->ed", attended, attn_grad, preferred_element_type=jnp.float32)
    ctx_grad = jnp.einsum("rsd,ed->rse", attn_grad, w_out, preferred_element_type=jnp.float32)
    ctx_grad = ctx_grad.astype(jnp.bfloat16).reshape(block_len, seq_count, head_count, HEAD_WIDTH)
    key_heads = key_all.reshape(key_all.shape[0], seq_count, head_count, HEAD_WIDTH)
    value_heads = value_all.reshape(value_all.shape[0], seq_count, head_count, HEAD_WIDTH)
    scores = attention_scores(queries, key_heads, allowed)
    probability = jnp.exp(scores - log_total)
    value_grad = jnp.einsum(
        "shqk,qshe->kshe",
        probability.astype(jnp.bfloat16),
        ctx_grad,
        preferred_element_type=jnp.float32,
    )
    prob_grad = jnp.einsum(
        "qshe,kshe->shqk", ctx_grad, value_heads, preferred_element_type=jnp.float32
    )
    score_grad = probability * (
        prob_grad - jnp.sum(probability * prob_grad, axis=-1, keepdims=True)
    )
    score_grad = score_grad.astype(jnp.bfloat16)
    query_grad = jnp.einsum(
        "shqk,kshe->qshe", score_grad, key_heads, preferred_element_type=jnp.float32
    ) * HEAD_WIDTH ** (-0.5)
    key_grad = jnp.einsum(
        "shqk,qshe->kshe", score_grad, queries, preferred_element_type=jnp.float32
    ) * HEAD_WIDTH ** (-0.5)
    key_back, value_back = (
        lax.psum_scatter(
            key_grad.astype(jnp.bfloat16), "ctx", scatter_dimension=0, tiled=True
        ).astype(jnp.float32),
        lax.psum_scatter(
            value_grad.astype(jnp.bfloat16), "ctx", scatter_dimension=0, tiled=True
        ).astype(jnp.float32),
    )
    qkv_grad = jnp.stack(
        [
            unrotary(query_grad, cosine, sine).reshape(block_len, seq_count, columns),
            unrotary(key_back, cosine, sine).reshape(block_len, seq_count, columns),
            value_back.reshape(block_len, seq_count, columns),
        ]
    ).astype(jnp.bfloat16)
    bias_grad = jnp.sum(qkv_grad.astype(jnp.float32), axis=(1, 2))
    qkv_weight_grad = jnp.einsum(
        "rsd,crse->cde", normed_all, qkv_grad, preferred_element_type=jnp.float32
    )
    piece = qkv_grad
    one_grad = lax.psum_scatter(
        jnp.einsum("crse,cde->rsd", piece, w_qkv, preferred_element_type=jnp.float32).astype(
            jnp.bfloat16
        ),
        "tp",
        scatter_dimension=0,
        tiled=True,
    ).astype(jnp.float32)
    input_grad, gain_one, shift_one = norm_back(layer_in, one_grad, gain_vec[0])
    input_grad = hidden_grad + input_grad
    weight_terms = (qkv_weight_grad, out_grad, gu_grad, down_grad)
    return (
        input_grad,
        (
            weight_terms,
            jnp.stack([gain_one, gain_two]),
            jnp.stack([shift_one, shift_two]),
            bias_grad,
        ),
    )


def spread(terms, columns, tp_index):
    weight_terms, gain_terms, shift_terms, bias_terms = terms
    qkv_term, out_term, gu_term, down_term = weight_terms
    scattered = (
        lax.psum_scatter(
            qkv_term.astype(jnp.bfloat16), "ctx", scatter_dimension=1, tiled=True
        ).astype(jnp.float32),
        lax.psum_scatter(
            out_term.astype(jnp.bfloat16), "ctx", scatter_dimension=1, tiled=True
        ).astype(jnp.float32),
        lax.psum_scatter(
            gu_term.astype(jnp.bfloat16), "ctx", scatter_dimension=1, tiled=True
        ).astype(jnp.float32),
        lax.psum_scatter(
            down_term.astype(jnp.bfloat16), "ctx", scatter_dimension=1, tiled=True
        ).astype(jnp.float32),
    )
    bias_full = lax.dynamic_update_slice_in_dim(
        jnp.zeros((3, gain_terms.shape[1]), jnp.float32), bias_terms, tp_index * columns, 1
    )
    gain_part, shift_part, bias_part = (
        lax.psum_scatter(gain_terms, ("ctx", "tp"), scatter_dimension=1, tiled=True),
        lax.psum_scatter(shift_terms, ("ctx", "tp"), scatter_dimension=1, tiled=True),
        lax.psum_scatter(bias_full, ("ctx", "tp"), scatter_dimension=1, tiled=True),
    )
    return (tuple(scattered), gain_part, shift_part, bias_part)


def stepwise_device(
    tokens_in,
    cotangent,
    plan,
    positions,
    norm_gain,
    norm_shift,
    w_qkv,
    b_qkv,
    w_out,
    w_gate_up,
    down_weight,
):
    weights = (
        norm_gain[0],
        norm_shift[0],
        w_qkv[0],
        b_qkv[0],
        w_out[0],
        w_gate_up[0],
        down_weight[0],
    )
    micro_count = tokens_in.shape[0]
    local_row_slice = tokens_in.shape[1]
    width = tokens_in.shape[3]
    columns = w_qkv.shape[3]
    ff_local = w_gate_up.shape[3]
    tp_count = lax.axis_size("tp")
    ctx_count = lax.axis_size("ctx")
    block_len = local_row_slice * tp_count
    section_index = lax.axis_index("section")
    ctx_index = lax.axis_index("ctx")
    tp_index = lax.axis_index("tp")
    block_pos = lax.dynamic_slice_in_dim(positions, ctx_index * block_len, block_len, 1)
    cosine, sine = tables(block_pos)
    allowed = (positions[:, None, :] <= block_pos[:, :, None])[:, None]
    context_rows = (cosine, sine, allowed)
    zero_rows = jnp.zeros(tokens_in.shape[1:], jnp.bfloat16)

    def forward_step(carry, step_index):
        arriving = passed_along(carry, "section", 1)
        micro = jnp.clip(step_index, 0, micro_count - 1)
        fresh = lax.dynamic_index_in_dim(tokens_in, plan[micro], 0, keepdims=False)
        layer_in = jnp.where(section_index == 0, fresh, arriving).astype(jnp.float32)
        layer_out, stored = forward_layer(layer_in, weights, context_rows)
        sent = layer_out.astype(jnp.bfloat16)
        return (sent, (sent, stored))

    steps_all = jnp.arange(micro_count + 1, dtype=jnp.int32)
    unused, (outputs, stored_all) = lax.scan(forward_step, zero_rows, steps_all)
    share = width // ctx_count
    fine_share = width // (ctx_count * tp_count)
    totals = (
        (
            jnp.zeros((3, share, columns), jnp.float32),
            jnp.zeros((columns, share), jnp.float32),
            jnp.zeros((2, share, ff_local), jnp.float32),
            jnp.zeros((ff_local, share), jnp.float32),
        ),
        jnp.zeros((2, fine_share), jnp.float32),
        jnp.zeros((2, fine_share), jnp.float32),
        jnp.zeros((3, fine_share), jnp.float32),
    )

    def backward_step(carry, bundle):
        send_back, running = carry
        step_index, stored = bundle
        arriving = passed_along(send_back, "section", -1)
        micro = step_index - section_index
        valid_step = ((micro >= 0) & (micro < micro_count)).astype(jnp.float32)
        target = lax.dynamic_index_in_dim(
            cotangent, jnp.clip(micro, 0, micro_count - 1), 0, keepdims=False
        )
        grad_out = jnp.where(section_index == 1, target, arriving).astype(jnp.float32)
        input_grad, terms = backward_layer(grad_out, stored, weights, context_rows)
        terms = jax.tree.map(lambda tensor: tensor * valid_step, terms)
        terms = spread(terms, columns, tp_index)
        running = jax.tree.map(jnp.add, running, terms)
        sent = input_grad.astype(jnp.bfloat16)
        return ((sent, running), sent)

    (unused_back, totals), input_grads = lax.scan(
        backward_step, (zero_rows, totals), (steps_all, stored_all), reverse=True
    )
    weight_parts, gain_part, shift_part, bias_part = totals
    section_ends = jnp.where(section_index == 0, input_grads[:micro_count], outputs[1:])[None]
    return (
        section_ends,
        gain_part[None],
        shift_part[None],
        bias_part[None],
        weight_parts[0][None],
        weight_parts[1][None],
        weight_parts[2][None],
        weight_parts[3][None],
    )


def per_device(*arrays):
    chips = lax.axis_size("ctx") // 2 * lax.axis_size("tp")
    if lax.axis_size("section") == 2 and lax.axis_size("ctx") == 4 and arrays[0].shape[0] == chips:
        return bulk_device(*arrays)
    return stepwise_device(*arrays)


def solution(mesh):
    placed = (
        P(None, ("ctx", "tp"), None, None),
        P(None, ("ctx", "tp"), None, None),
        P(),
        P(),
        P("section", None, None),
        P("section", None, None),
        P("section", None, None, "tp"),
        P("section", None, "tp"),
        P("section", "tp", None),
        P("section", None, None, "tp"),
        P("section", "tp", None),
    )
    return jax.shard_map(
        per_device,
        mesh=mesh,
        in_specs=placed,
        out_specs=(
            P("section", None, ("ctx", "tp"), None, None),
            P("section", None, ("ctx", "tp")),
            P("section", None, ("ctx", "tp")),
            P("section", None, ("ctx", "tp")),
            P("section", None, "ctx", "tp"),
            P("section", "tp", "ctx"),
            P("section", None, "ctx", "tp"),
            P("section", "tp", "ctx"),
        ),
        check_vma=False,
    )
```

```python
import functools

import jax
import jax.numpy as jnp
from jax import lax
from jax.experimental import pallas as pl
from jax.experimental.pallas import tpu as pltpu
from jax.sharding import PartitionSpec as P

HEAD_WIDTH = 64
ROT = 16


def pair_routes(ctx_count):
    core = [(i, i ^ 1) for i in range(ctx_count)]
    across = [(i, (i + 2) % 4) for i in range(ctx_count)]
    return core, across


def ln_stats(stream):
    mean = jnp.mean(stream, axis=-1, keepdims=True)
    centre = stream - mean
    inv_std = lax.rsqrt(jnp.mean(centre * centre, axis=-1, keepdims=True) + 1e-05)
    return centre, inv_std


def ln(stream, gain_vec, shift_vec):
    centre, inv_std = ln_stats(stream)
    return (centre * inv_std * gain_vec + shift_vec).astype(jnp.bfloat16)


def ln_back(stream, grad_in, gain_vec):
    centre, inv_std = ln_stats(stream)
    unit = centre * inv_std
    scaled = grad_in * gain_vec
    result = inv_std * (
        scaled
        - jnp.mean(scaled, axis=-1, keepdims=True)
        - unit * jnp.mean(scaled * unit, axis=-1, keepdims=True)
    )
    return result, jnp.sum(grad_in * unit, axis=0), jnp.sum(grad_in, axis=0)


def rot_tables(pos_row):
    half = ROT // 2
    freqs = 10000.0 ** (-jnp.arange(half, dtype=jnp.float32) * 2.0 / ROT)
    angles = pos_row.astype(jnp.float32)[:, None] * freqs
    cosine, sine = jnp.cos(angles), jnp.sin(angles)
    rows = pos_row.shape[0]
    rest = HEAD_WIDTH - ROT
    zeros = jnp.zeros((rows, half), jnp.float32)
    cos_head = jnp.concatenate([cosine, cosine, jnp.ones((rows, rest), jnp.float32)], 1)
    low_head = jnp.concatenate([-sine, zeros, jnp.zeros((rows, rest), jnp.float32)], 1)
    high_head = jnp.concatenate([zeros, sine, jnp.zeros((rows, rest), jnp.float32)], 1)
    return tuple(jnp.concatenate([t, t], 1) for t in (cos_head, low_head, high_head))


def dot_t(a, b):
    return lax.dot_general(a, b, (((1,), (1,)), ((), ())), preferred_element_type=jnp.float32)


def dot_0(a, b):
    return lax.dot_general(a, b, (((0,), (0,)), ((), ())), preferred_element_type=jnp.float32)


def dot_n(a, b):
    return lax.dot_general(a, b, (((1,), (0,)), ((), ())), preferred_element_type=jnp.float32)


def chunked(x, chunk):
    half = x.shape[0] // 2
    pieces = []
    for i in range(half // chunk):
        pieces.append(x[i * chunk : (i + 1) * chunk])
        pieces.append(x[half + i * chunk : half + (i + 1) * chunk])
    return jnp.concatenate(pieces, axis=0)


def attn_fwd_kernel(heads, chunk, mixed, bias, cos_t, low_t, high_t, pos_c, pos_r, qkv, out):
    rows = mixed.shape[0]
    half = rows // 2
    width = heads * HEAD_WIDTH
    half_rot = ROT // 2
    cosine, low, high = cos_t[...], low_t[...], high_t[...]
    for pair in range(heads // 2):
        parts = []
        for c in range(3):
            at = c * width + pair * 128
            x = mixed[:, at : at + 128] + bias[0, :, at : at + 128]
            if c < 2:
                x = x * cosine + pltpu.roll(x, 128 - half_rot, 1) * low + pltpu.roll(x, half_rot, 1) * high
            x = x.astype(jnp.bfloat16)
            qkv[:, at : at + 128] = x
            parts.append(chunked(x, chunk))
        query, key, value = parts
        query = query * jnp.bfloat16(HEAD_WIDTH ** (-0.5))
        for i in range(half // chunk):
            end = 2 * chunk * (i + 1)
            begin = end - 2 * chunk
            allowed = pos_r[:, begin:end] <= pos_c[begin:end, :]
            halves = []
            for h in range(2):
                lanes = slice(h * HEAD_WIDTH, (h + 1) * HEAD_WIDTH)
                q_h = query[begin:end, lanes]
                score = dot_t(q_h, key[:end, lanes])
                last = jnp.where(allowed, score[:, begin:], -1e30)
                score = last if i == 0 else jnp.concatenate([score[:, :begin], last], axis=1)
                prob = jnp.exp(score - jnp.max(score, axis=1, keepdims=True))
                total = jnp.sum(prob, axis=1, keepdims=True)
                mixed_values = dot_n(prob.astype(jnp.bfloat16), value[:end, lanes])
                halves.append(mixed_values / total)
            done = jnp.concatenate(halves, axis=1).astype(jnp.bfloat16)
            lanes = slice(pair * 128, pair * 128 + 128)
            out[i * chunk : (i + 1) * chunk, lanes] = done[:chunk]
            out[half + i * chunk : half + (i + 1) * chunk, lanes] = done[chunk:]


def attn_bwd_kernel(heads, chunk, qkv, ctx, cos_t, low_t, high_t, pos_c, pos_r, grad, bias_grad, dk_s, dv_s):
    rows = qkv.shape[0]
    half = rows // 2
    width = heads * HEAD_WIDTH
    half_rot = ROT // 2
    cosine, low, high = cos_t[...], low_t[...], high_t[...]
    scale = HEAD_WIDTH ** (-0.5)

    def finish(c, pair, x):
        at = c * width + pair * 128
        if c < 2:
            x = x * scale
            x = x * cosine + pltpu.roll(x * high, 128 - half_rot, 1) + pltpu.roll(x * low, half_rot, 1)
        x = x.astype(jnp.bfloat16)
        grad[:, at : at + 128] = x
        bias_grad[0, :, at : at + 128] = jnp.sum(x.astype(jnp.float32), axis=0, keepdims=True)

    def unchunked(x):
        steps = half // chunk
        own = [x[2 * i * chunk : (2 * i + 1) * chunk] for i in range(steps)]
        other = [x[(2 * i + 1) * chunk : (2 * i + 2) * chunk] for i in range(steps)]
        return jnp.concatenate(own + other, axis=0)

    for pair in range(heads // 2):
        lanes2 = slice(pair * 128, pair * 128 + 128)
        query, key, value = (
            chunked(qkv[:, c * width + pair * 128 : c * width + pair * 128 + 128], chunk) for c in range(3)
        )
        query_s = query * jnp.bfloat16(scale)
        ctx_grad = chunked(ctx[:, lanes2], chunk)
        dk_s[...] = jnp.zeros_like(dk_s)
        dv_s[...] = jnp.zeros_like(dv_s)
        dq_parts = []
        for i in range(half // chunk):
            end = 2 * chunk * (i + 1)
            begin = end - 2 * chunk
            allowed = pos_c[begin:end, :] <= pos_r[:, begin:end]
            dq_h, dk_h, dv_h = [], [], []
            for h in range(2):
                lanes = slice(h * HEAD_WIDTH, (h + 1) * HEAD_WIDTH)
                score = dot_t(key[:end, lanes], query_s[begin:end, lanes])
                last = jnp.where(allowed, score[begin:, :], -1e30)
                score = last if i == 0 else jnp.concatenate([score[:begin, :], last], axis=0)
                prob = jnp.exp(score - jnp.max(score, axis=0, keepdims=True))
                prob = prob * (1.0 / jnp.sum(prob, axis=0, keepdims=True))
                grad_h = ctx_grad[begin:end, lanes]
                dv_h.append(dot_n(prob.astype(jnp.bfloat16), grad_h))
                prob_grad = dot_t(value[:end, lanes], grad_h)
                delta = jnp.sum(prob * prob_grad, axis=0, keepdims=True)
                score_grad = (prob * (prob_grad - delta)).astype(jnp.bfloat16)
                dk_h.append(dot_n(score_grad, query[begin:end, lanes]))
                dq_h.append(dot_0(score_grad, key[:end, lanes]))
            dk_s[:end, :] += jnp.concatenate(dk_h, axis=1)
            dv_s[:end, :] += jnp.concatenate(dv_h, axis=1)
            dq_parts.append(jnp.concatenate(dq_h, axis=1))
        finish(0, pair, unchunked(jnp.concatenate(dq_parts, axis=0)))
        finish(1, pair, unchunked(dk_s[...]))
        finish(2, pair, unchunked(dv_s[...]))


VMEM_LIMIT = 56 * 1024 * 1024


def attn_fwd(mixed, bias, context, groups, chunk):
    rows, columns = mixed.shape
    block = columns // groups
    heads = block // (3 * HEAD_WIDTH)
    cos_t, low_t, high_t, pos_c, pos_r = context
    whole = lambda shape: pl.BlockSpec(shape, lambda g: (0, 0))
    return pl.pallas_call(
        functools.partial(attn_fwd_kernel, heads, chunk),
        grid=(groups,),
        in_specs=[
            pl.BlockSpec((rows, block), lambda g: (0, g)),
            pl.BlockSpec((1, 1, block), lambda g: (g, 0, 0)),
            whole((rows, 128)),
            whole((rows, 128)),
            whole((rows, 128)),
            whole((rows, 1)),
            whole((1, rows)),
        ],
        out_specs=[
            pl.BlockSpec((rows, block), lambda g: (0, g)),
            pl.BlockSpec((rows, block // 3), lambda g: (0, g)),
        ],
        out_shape=[
            jax.ShapeDtypeStruct((rows, columns), jnp.bfloat16),
            jax.ShapeDtypeStruct((rows, columns // 3), jnp.bfloat16),
        ],
        compiler_params=pltpu.CompilerParams(vmem_limit_bytes=VMEM_LIMIT),
        cost_estimate=pl.CostEstimate(
            flops=3 * rows * rows * columns // 3 * 4,
            bytes_accessed=rows * columns * 7,
            transcendentals=rows * rows * columns // (3 * HEAD_WIDTH),
        ),
    )(mixed, bias.reshape(groups, 1, block), cos_t, low_t, high_t, pos_c, pos_r)


def attn_bwd(qkv, ctx_grad, context, groups, chunk):
    rows, columns = qkv.shape
    block = columns // groups
    heads = block // (3 * HEAD_WIDTH)
    cos_t, low_t, high_t, pos_c, pos_r = context
    whole = lambda shape: pl.BlockSpec(shape, lambda g: (0, 0))
    return pl.pallas_call(
        functools.partial(attn_bwd_kernel, heads, chunk),
        grid=(groups,),
        in_specs=[
            pl.BlockSpec((rows, block), lambda g: (0, g)),
            pl.BlockSpec((rows, block // 3), lambda g: (0, g)),
            whole((rows, 128)),
            whole((rows, 128)),
            whole((rows, 128)),
            whole((rows, 1)),
            whole((1, rows)),
        ],
        out_specs=[
            pl.BlockSpec((rows, block), lambda g: (0, g)),
            pl.BlockSpec((1, 1, block), lambda g: (g, 0, 0)),
        ],
        out_shape=[
            jax.ShapeDtypeStruct((rows, columns), jnp.bfloat16),
            jax.ShapeDtypeStruct((groups, 1, block), jnp.float32),
        ],
        scratch_shapes=[pltpu.VMEM((rows, 128), jnp.float32), pltpu.VMEM((rows, 128), jnp.float32)],
        compiler_params=pltpu.CompilerParams(vmem_limit_bytes=VMEM_LIMIT),
        cost_estimate=pl.CostEstimate(
            flops=7 * rows * rows * columns // 3 * 4,
            bytes_accessed=rows * columns * 5,
            transcendentals=rows * rows * columns // (3 * HEAD_WIDTH),
        ),
    )(qkv, ctx_grad, cos_t, low_t, high_t, pos_c, pos_r)


def bulk_device(
    tokens_in,
    cotangent,
    plan,
    positions,
    norm_gain,
    norm_shift,
    w_qkv,
    b_qkv,
    w_out,
    w_gate_up,
    down_weight,
):
    tp_count = lax.axis_size("tp")
    ctx_count = lax.axis_size("ctx")
    section_index = lax.axis_index("section")
    ctx_index = lax.axis_index("ctx")
    side, core = ctx_index // 2, ctx_index % 2
    core_route, across_route = pair_routes(ctx_count)
    micro_count, slice_len, _, width = tokens_in.shape
    gain, shift = norm_gain[0], norm_shift[0]
    piece = slice_len // 2
    rows = micro_count * slice_len * 2
    own_rows = rows // 2
    half_width = width // 2
    columns = w_qkv.shape[3] // 2
    hidden = w_gate_up.shape[3] // 2
    first = section_index == 0

    ordered = jnp.stack(
        [lax.dynamic_index_in_dim(tokens_in, plan[m], 0, keepdims=False)[:, 0] for m in range(micro_count)]
    )
    fresh = jnp.where(first, ordered, cotangent[:, :, 0])
    fresh = fresh.reshape(ctx_count // 2, tp_count, 2, piece, width).transpose(0, 2, 1, 3, 4)
    fresh = fresh.reshape(ctx_count * tp_count, piece, width)
    inbound = lax.all_to_all(fresh, ("ctx", "tp"), 0, 0, tiled=True).reshape(own_rows, width)

    pos = positions.reshape(-1, 2, piece)
    pos = jnp.concatenate(
        [
            lax.dynamic_index_in_dim(pos, core, 1, False).reshape(-1),
            lax.dynamic_index_in_dim(pos, 1 - core, 1, False).reshape(-1),
        ]
    )
    chunk = min(128, own_rows)
    chunk_pos = chunked(pos, chunk)
    context = (*rot_tables(pos), chunk_pos[:, None], chunk_pos[None, :])

    tp_index = lax.axis_index("tp")

    def turned_by_tp(shards, axis=0):
        count = shards.shape[axis] // tp_count
        twice = jnp.concatenate([shards, shards], axis=axis)
        start = lax.rem(tp_count - tp_index, tp_count) * count
        return lax.dynamic_slice_in_dim(twice, start, tp_count * count, axis)

    def after(x, *others):
        return lax.optimization_barrier((x, *others))[0]

    own_parts, across_parts = [], []

    def gathered(block_of):
        block, held = block_of(side), block_of(1 - side)
        count = block.shape[0]
        step = len(own_parts)
        if step == 2:
            block = after(block, own_parts[0], across_parts[0], inbound)
        elif step > 2:
            block = after(block, own_parts[step - 2], across_parts[step - 3])
        own = lax.all_gather(block, "tp", axis=0, tiled=True)
        wanted = [
            lax.dynamic_slice_in_dim(own, lax.rem(tp_index + p, tp_count) * count, count, 0)
            for p in range(1, tp_count)
        ]
        arriving = lax.ppermute(jnp.concatenate(wanted, axis=0), "ctx", across_route)
        own_parts.append(own)
        across_parts.append(arriving)
        other = turned_by_tp(jnp.concatenate([held, arriving], axis=0))
        return jnp.where(
            side == 0, jnp.concatenate([own, other], axis=1), jnp.concatenate([other, own], axis=1)
        )

    def qkv_block(half):
        block = lax.dynamic_slice(w_qkv[0], (0, half * half_width, core * columns), (3, half_width, columns))
        return block.transpose(0, 2, 1).reshape(3 * columns, half_width)

    def out_block(half):
        return lax.dynamic_slice(w_out[0], (core * columns, half * half_width), (columns, half_width))

    def gu_block(which, half):
        block = lax.dynamic_slice(
            w_gate_up[0], (which, half * half_width, core * hidden), (1, half_width, hidden)
        )
        return block[0].T

    def down_block(part, half):
        start = core * hidden + part * (hidden // 2)
        return lax.dynamic_slice(down_weight[0], (start, half * half_width), (hidden // 2, half_width))

    wt_out = gathered(out_block)
    wt_qkv = gathered(qkv_block)
    wt_gu = jnp.concatenate([gathered(functools.partial(gu_block, w)) for w in range(2)], axis=0)
    wt_down = jnp.concatenate(
        [
            gathered(functools.partial(down_block, part)).reshape(tp_count, hidden // 2, width)
            for part in range(2)
        ],
        axis=1,
    ).reshape(tp_count * hidden, width)
    bias_own = lax.dynamic_slice_in_dim(b_qkv[0], core * columns, columns, 1).reshape(1, 3 * columns)
    bias = [bias_own]
    for p in range(1, tp_count):
        ring = [((i + p) % tp_count, i) for i in range(tp_count)]
        bias.append(lax.ppermute(bias_own, "tp", ring))
    bias = turned_by_tp(jnp.concatenate(bias, axis=0))
    ff = wt_down.shape[0]

    def both(own):
        return jnp.concatenate([own, lax.ppermute(own, "ctx", core_route)], axis=0)

    def summed(a, weight, parts=1):
        step = own_rows // parts
        spans = [slice(i * step, (i + 1) * step) for i in range(parts)]
        others = [dot_n(a[own_rows:][span], weight).astype(jnp.bfloat16) for span in spans]
        arriving = [lax.ppermute(other, "ctx", core_route) for other in others]
        own = [dot_n(a[:own_rows][span], weight) for span in spans]
        return [x + y.astype(jnp.float32) for x, y in zip(own, arriving)]

    def split(x, parts):
        step = x.shape[0] // parts
        return [x[i * step : (i + 1) * step] for i in range(parts)]

    def over_x(parts, route):
        return jnp.concatenate([lax.ppermute(part, "section", route) for part in parts], axis=0)

    def forward(stream):
        normed = both(ln(stream, gain[0], shift[0]))
        mixed = dot_t(normed, wt_qkv)
        qkv, attended = attn_fwd(mixed, bias, context, tp_count, chunk)
        hidden_state = stream + summed(attended, wt_out)[0]
        normed_two = both(ln(hidden_state, gain[1], shift[1]))
        gate_up = dot_t(normed_two, wt_gu)
        gate, up = gate_up[:, :ff], gate_up[:, ff:]
        activation = (jax.nn.silu(gate) * up).astype(jnp.bfloat16)
        out = [
            (x + y).astype(jnp.bfloat16)
            for x, y in zip(split(hidden_state, 2), summed(activation, wt_down, 2))
        ]
        return out, (stream, normed, qkv, attended, hidden_state, normed_two, gate_up, activation)

    def far_near(right):
        far = lax.dynamic_slice_in_dim(right, (1 - side) * half_width, half_width, 1)
        near = lax.dynamic_slice_in_dim(right, side * half_width, half_width, 1)
        return far, near

    def far_term(left, right):
        return dot_0(left, far_near(right)[0]).astype(jnp.bfloat16)

    def near_total(left, right, arriving, *others):
        near = far_near(right)[1]
        if others:
            near = after(near, *others)
        return (dot_0(left, near) + arriving.astype(jnp.float32)).astype(jnp.bfloat16)

    def across(term, *others):
        return lax.ppermute(after(term, *others) if others else term, "ctx", across_route)

    def over_tp(term):
        return lax.psum_scatter(term, "tp", scatter_dimension=0, tiled=True)

    together = lax.optimization_barrier

    def part_of(x, i, parts, axis):
        shard = x.shape[axis] // tp_count
        step = shard // parts
        return jnp.concatenate(
            [
                lax.slice_in_dim(x, z * shard + i * step, z * shard + (i + 1) * step, axis=axis)
                for z in range(tp_count)
            ],
            axis=axis,
        )

    def mlp_back(act_grad, gate_up):
        gate, up = gate_up[:, :ff], gate_up[:, ff:]
        sigma = jax.nn.sigmoid(gate)
        gate_grad = (act_grad * up * sigma * (1.0 + gate * (1.0 - sigma))).astype(jnp.bfloat16)
        up_grad = (act_grad * gate * sigma).astype(jnp.bfloat16)
        return gate_grad, up_grad, jnp.concatenate([gate_grad, up_grad], axis=1)

    def backward(grad_out, stored):
        stream, normed, qkv, attended, hidden_state, normed_two, gate_up, activation = stored
        gu_grad = mlp_back(dot_t(both(grad_out), wt_down), gate_up)[2]
        result = ln_back(hidden_state, summed(gu_grad, wt_gu)[0], gain[1])[0]
        hidden_grad = grad_out.astype(jnp.float32) + result
        ctx_grad = dot_t(both(hidden_grad.astype(jnp.bfloat16)), wt_out).astype(jnp.bfloat16)
        qkv_grad, _ = attn_bwd(qkv, ctx_grad, context, tp_count, chunk)
        one_grad = jnp.concatenate(summed(qkv_grad, wt_qkv, 2), axis=0)
        result = ln_back(stream, one_grad, gain[0])[0]
        return split((hidden_grad + result).astype(jnp.bfloat16), 2)

    def last_backward(grad_out, stored, final_out):
        stream, normed, qkv, attended, hidden_state, normed_two, gate_up, activation, act_a, act_b = stored
        grad_f32 = grad_out.astype(jnp.float32)
        mlp_grad = both(grad_out)
        far_a, far_b = far_term(act_a, mlp_grad), far_term(act_b, mlp_grad)

        mlp_in, far_a, far_b = together((mlp_grad, far_a, far_b))
        arriving = across(far_a)
        gate_grad, up_grad, gu_grad = mlp_back(dot_t(mlp_in, wt_down), gate_up)

        arriving, far_b, gate_grad, up_grad, act_a = together((arriving, far_b, gate_grad, up_grad, act_a))
        arriving_b = across(far_b)
        sum_a = over_tp(near_total(act_a, mlp_grad, arriving))
        gu_grad = jnp.concatenate([gate_grad, up_grad], axis=1)
        two_other = dot_n(gu_grad[own_rows:], wt_gu).astype(jnp.bfloat16)
        far_gate = far_term(gate_grad, normed_two)

        arriving_b, far_gate, gu_grad, two_other, act_b, up_grad = together(
            (arriving_b, far_gate, gu_grad, two_other, act_b, up_grad)
        )
        arriving_gate = across(far_gate)
        sum_b = over_tp(near_total(act_b, mlp_grad, arriving_b))
        two_grad = dot_n(gu_grad[:own_rows], wt_gu) + lax.ppermute(two_other, "ctx", core_route).astype(jnp.float32)
        result, gain_two, shift_two = ln_back(hidden_state, two_grad, gain[1])
        hidden_grad = grad_f32 + result
        attn_grad = both(hidden_grad.astype(jnp.bfloat16))
        far_up = far_term(up_grad, normed_two)

        arriving_gate, far_up, gate_grad, attn_grad, hidden_grad = together(
            (arriving_gate, far_up, gate_grad, attn_grad, hidden_grad)
        )
        far_up_a, far_up_b = split(far_up, 2)
        arriving = across(far_up_a)
        sum_gate = over_tp(near_total(gate_grad, normed_two, arriving_gate))
        ctx_grad = dot_t(attn_grad, wt_out).astype(jnp.bfloat16)

        arriving, far_up_b, ctx_grad = together((arriving, far_up_b, ctx_grad))
        arriving_up = jnp.concatenate([arriving, across(far_up_b)], axis=0)
        qkv_grad, bias_grad = attn_bwd(qkv, ctx_grad, context, tp_count, chunk)
        qkv_a, qkv_b = (part_of(qkv_grad, i, 2, 1) for i in range(2))
        far_a = far_term(qkv_a, normed)

        arriving_up, far_a, qkv_a, qkv_b, qkv_grad, up_grad, attn_grad = together(
            (arriving_up, far_a, qkv_a, qkv_b, qkv_grad, up_grad, attn_grad)
        )
        arriving = across(far_a)
        sum_up = over_tp(near_total(up_grad, normed_two, arriving_up))
        one_other = dot_n(qkv_grad[own_rows:], wt_qkv).astype(jnp.bfloat16)
        far_b = far_term(qkv_b, normed)

        arriving, far_b, one_other, qkv_grad, qkv_a, qkv_b = together(
            (arriving, far_b, one_other, qkv_grad, qkv_a, qkv_b)
        )
        arriving_b = across(far_b)
        sum_qkv_a = over_tp(near_total(qkv_a, normed, arriving))
        one_grad = dot_n(qkv_grad[:own_rows], wt_qkv) + lax.ppermute(one_other, "ctx", core_route).astype(jnp.float32)
        result, gain_one, shift_one = ln_back(stream, one_grad, gain[0])
        input_grad = (hidden_grad + result).astype(jnp.bfloat16)
        ends = jnp.where(first, input_grad, final_out)
        far_out = far_term(attended, attn_grad)

        arriving_b, far_out, ends, qkv_b = together((arriving_b, far_out, ends, qkv_b))
        arriving_out = across(far_out)
        ends = lax.all_to_all(
            ends.reshape(ctx_count * tp_count, piece, width), ("ctx", "tp"), 0, 0, tiled=True
        )
        sum_qkv_b = over_tp(near_total(qkv_b, normed, arriving_b))
        sum_out = over_tp(near_total(attended, attn_grad, arriving_out))
        small = (jnp.stack([gain_one, gain_two]), jnp.stack([shift_one, shift_two]), bias_grad)
        sum_down = jnp.concatenate([sum_a, sum_b], axis=0)
        sum_qkv = jnp.concatenate([sum_qkv_a, sum_qkv_b], axis=0)
        return ends, small, (sum_down, sum_gate, sum_up, sum_out, sum_qkv)

    sent, _ = forward(inbound.astype(jnp.float32))
    arriving = over_x(sent, [(0, 1)])
    final_out, stored = forward(jnp.where(first, inbound, arriving).astype(jnp.float32))
    arriving_back = over_x(backward(inbound, stored), [(1, 0)])
    halves = tuple(part_of(stored[-1], i, 2, 1) for i in range(2))
    arriving_back, final_out, *halves = together((arriving_back, jnp.concatenate(final_out, axis=0), *halves))
    stored = (*stored, *halves)
    grad_out = jnp.where(first, arriving_back, inbound)
    ends, small, sums = last_backward(grad_out, stored, final_out)
    down_sum, gate_sum, up_sum, out_sum, qkv_sum = sums

    def settled(term):
        share = half_width // 2
        away = lax.dynamic_slice_in_dim(term, (1 - core) * share, share, term.ndim - 1)
        kept = lax.dynamic_slice_in_dim(term, core * share, share, term.ndim - 1)
        got = lax.ppermute(away, "ctx", core_route)
        axis = term.ndim - 2
        return jnp.where(
            core == 0, jnp.concatenate([kept, got], axis), jnp.concatenate([got, kept], axis)
        ).astype(jnp.float32)

    grad_down = settled(down_sum)
    grad_gate = settled(gate_sum)
    grad_up = settled(up_sum)
    grad_out_w = settled(out_sum)
    grad_qkv = settled(qkv_sum.reshape(3, columns, half_width))

    gain_terms, shift_terms, bias_terms = small
    bias_terms = bias_terms.reshape(tp_count, 3, columns).transpose(1, 0, 2)[:, :, None]
    bias_full = jnp.where(
        (jnp.arange(2) == core)[None, None, :, None], bias_terms, 0.0
    ).reshape(3, tp_count * 2 * columns)
    vectors = jnp.concatenate([gain_terms, shift_terms, bias_full], axis=0)
    share = width // (ctx_count * tp_count)
    vectors = vectors.reshape(-1, ctx_count * tp_count, share).transpose(1, 0, 2)
    vectors = jnp.sum(lax.all_to_all(vectors, ("ctx", "tp"), 0, 0, tiled=True), axis=0).reshape(-1, share)

    ends = ends.reshape(ctx_count // 2, 2, tp_count, piece, width).transpose(0, 2, 1, 3, 4)
    ends = ends.reshape(micro_count, slice_len, 1, width)
    return (
        ends[None],
        vectors[None, :2],
        vectors[None, 2:4],
        vectors[None, 4:],
        grad_qkv.transpose(0, 2, 1)[None],
        grad_out_w[None],
        jnp.stack([grad_gate.T, grad_up.T])[None],
        grad_down[None],
    )


def passed_along(block, axis, distance):
    devices = range(lax.axis_size(axis))
    route = [(i - distance, i) for i in devices if i - distance in devices]
    return lax.ppermute(block, axis, route)


def normalize(stream, gain_vec, shift_vec):
    centre = stream - jnp.mean(stream, axis=-1, keepdims=True)
    spread = jnp.mean(centre * centre, axis=-1, keepdims=True)
    return centre * lax.rsqrt(spread + 1e-05) * gain_vec + shift_vec


def norm_back(stream, grad_in, gain_vec):
    centre = stream - jnp.mean(stream, axis=-1, keepdims=True)
    inv_std = lax.rsqrt(jnp.mean(centre * centre, axis=-1, keepdims=True) + 1e-05)
    unit = centre * inv_std
    scaled = grad_in * gain_vec
    result = inv_std * (
        scaled
        - jnp.mean(scaled, axis=-1, keepdims=True)
        - unit * jnp.mean(scaled * unit, axis=-1, keepdims=True)
    )
    return (result, jnp.sum(grad_in * unit, axis=(0, 1)), jnp.sum(grad_in, axis=(0, 1)))


def rotary(tensor, cosine, sine):
    half_rot = ROT // 2
    front = tensor[..., :ROT]
    turned = jnp.concatenate([-front[..., half_rot:], front[..., :half_rot]], axis=-1)
    return jnp.concatenate([front * cosine + turned * sine, tensor[..., ROT:]], axis=-1)


def unrotary(tensor, cosine, sine):
    half_rot = ROT // 2
    front = tensor[..., :ROT]
    turned = jnp.concatenate([-front[..., half_rot:], front[..., :half_rot]], axis=-1)
    return jnp.concatenate([front * cosine - turned * sine, tensor[..., ROT:]], axis=-1)


def tables(position_rows):
    freqs = 10000.0 ** (-jnp.arange(ROT // 2, dtype=jnp.float32) * 2.0 / ROT)
    angles = position_rows.T.astype(jnp.float32)[:, :, None] * freqs
    angles = jnp.concatenate([angles, angles], axis=-1)[:, :, None, :]
    return (jnp.cos(angles), jnp.sin(angles))


def attention_scores(queries, key_heads, allowed):
    scores = jnp.einsum(
        "qshe,kshe->shqk", queries, key_heads, preferred_element_type=jnp.float32
    ) * HEAD_WIDTH ** (-0.5)
    return jnp.where(allowed, scores, -1e30)


def forward_layer(layer_in, weights, context_rows):
    gain_vec, shift_vec, w_qkv, b_qkv, w_out, w_gate_up, down_weight = weights
    cosine, sine, allowed = context_rows
    normed = normalize(layer_in, gain_vec[0], shift_vec[0]).astype(jnp.bfloat16)
    normed_all = lax.all_gather(normed, "tp", axis=0, tiled=True)
    block_len, seq_count, width = normed_all.shape
    columns = w_qkv.shape[2]
    head_count = columns // HEAD_WIDTH
    mixed = (
        jnp.einsum("rsd,cde->crse", normed_all, w_qkv, preferred_element_type=jnp.float32)
        + b_qkv[:, None, None, :]
    )
    queries = rotary(
        mixed[0].reshape(block_len, seq_count, head_count, HEAD_WIDTH), cosine, sine
    ).astype(jnp.bfloat16)
    key_own = rotary(
        mixed[1].reshape(block_len, seq_count, head_count, HEAD_WIDTH), cosine, sine
    ).astype(jnp.bfloat16)
    key_own = key_own.reshape(block_len, seq_count, columns)
    value_own = mixed[2].astype(jnp.bfloat16)
    key_all, value_all = (
        lax.all_gather(key_own, "ctx", axis=0, tiled=True),
        lax.all_gather(value_own, "ctx", axis=0, tiled=True),
    )
    key_heads = key_all.reshape(key_all.shape[0], seq_count, head_count, HEAD_WIDTH)
    value_heads = value_all.reshape(value_all.shape[0], seq_count, head_count, HEAD_WIDTH)
    scores = attention_scores(queries, key_heads, allowed)
    top_score = jnp.max(scores, axis=-1, keepdims=True)
    log_total = top_score + jnp.log(jnp.sum(jnp.exp(scores - top_score), axis=-1, keepdims=True))
    probability = jnp.exp(scores - log_total)
    attended = jnp.einsum(
        "shqk,kshe->qshe",
        probability.astype(jnp.bfloat16),
        value_heads,
        preferred_element_type=jnp.float32,
    )
    attended = attended.astype(jnp.bfloat16).reshape(block_len, seq_count, columns)
    piece = attended
    hidden_state = layer_in + lax.psum_scatter(
        jnp.einsum("rse,ed->rsd", piece, w_out, preferred_element_type=jnp.float32).astype(
            jnp.bfloat16
        ),
        "tp",
        scatter_dimension=0,
        tiled=True,
    ).astype(jnp.float32)
    normed_two = normalize(hidden_state, gain_vec[1], shift_vec[1]).astype(jnp.bfloat16)
    normed_two_all = lax.all_gather(normed_two, "tp", axis=0, tiled=True)
    gate_up = jnp.einsum(
        "rsd,cdf->crsf", normed_two_all, w_gate_up, preferred_element_type=jnp.float32
    )
    gated_activation = (jax.nn.silu(gate_up[0]) * gate_up[1]).astype(jnp.bfloat16)
    piece = gated_activation
    layer_out = hidden_state + lax.psum_scatter(
        jnp.einsum("rsf,fd->rsd", piece, down_weight, preferred_element_type=jnp.float32).astype(
            jnp.bfloat16
        ),
        "tp",
        scatter_dimension=0,
        tiled=True,
    ).astype(jnp.float32)
    stored = (
        layer_in,
        normed_all,
        queries,
        key_all,
        value_all,
        log_total,
        attended,
        hidden_state,
        normed_two_all,
        gate_up,
    )
    return (layer_out, stored)


def backward_layer(grad_out, stored, weights, context_rows):
    gain_vec, shift_vec, w_qkv, b_qkv, w_out, w_gate_up, down_weight = weights
    cosine, sine, allowed = context_rows
    (
        layer_in,
        normed_all,
        queries,
        key_all,
        value_all,
        log_total,
        attended,
        hidden_state,
        normed_two_all,
        gate_up,
    ) = stored
    block_len, seq_count, columns = attended.shape
    head_count = columns // HEAD_WIDTH
    mlp_grad = lax.all_gather(grad_out.astype(jnp.bfloat16), "tp", axis=0, tiled=True)
    gate_part = gate_up[0]
    up_part = gate_up[1]
    sigma = jax.nn.sigmoid(gate_part)
    swish = gate_part * sigma
    gated_activation = (swish * up_part).astype(jnp.bfloat16)
    down_grad = jnp.einsum(
        "rsf,rsd->fd", gated_activation, mlp_grad, preferred_element_type=jnp.float32
    )
    act_grad = jnp.einsum("rsd,fd->rsf", mlp_grad, down_weight, preferred_element_type=jnp.float32)
    gate_up_grad = jnp.stack(
        [act_grad * up_part * sigma * (1.0 + gate_part * (1.0 - sigma)), act_grad * swish]
    ).astype(jnp.bfloat16)
    gu_grad = jnp.einsum(
        "rsd,crsf->cdf", normed_two_all, gate_up_grad, preferred_element_type=jnp.float32
    )
    piece = gate_up_grad
    two_grad = lax.psum_scatter(
        jnp.einsum("crsf,cdf->rsd", piece, w_gate_up, preferred_element_type=jnp.float32).astype(
            jnp.bfloat16
        ),
        "tp",
        scatter_dimension=0,
        tiled=True,
    ).astype(jnp.float32)
    hidden_grad, gain_two, shift_two = norm_back(hidden_state, two_grad, gain_vec[1])
    hidden_grad = grad_out + hidden_grad
    attn_grad = lax.all_gather(hidden_grad.astype(jnp.bfloat16), "tp", axis=0, tiled=True)
    out_grad = jnp.einsum("rse,rsd->ed", attended, attn_grad, preferred_element_type=jnp.float32)
    ctx_grad = jnp.einsum("rsd,ed->rse", attn_grad, w_out, preferred_element_type=jnp.float32)
    ctx_grad = ctx_grad.astype(jnp.bfloat16).reshape(block_len, seq_count, head_count, HEAD_WIDTH)
    key_heads = key_all.reshape(key_all.shape[0], seq_count, head_count, HEAD_WIDTH)
    value_heads = value_all.reshape(value_all.shape[0], seq_count, head_count, HEAD_WIDTH)
    scores = attention_scores(queries, key_heads, allowed)
    probability = jnp.exp(scores - log_total)
    value_grad = jnp.einsum(
        "shqk,qshe->kshe",
        probability.astype(jnp.bfloat16),
        ctx_grad,
        preferred_element_type=jnp.float32,
    )
    prob_grad = jnp.einsum(
        "qshe,kshe->shqk", ctx_grad, value_heads, preferred_element_type=jnp.float32
    )
    score_grad = probability * (
        prob_grad - jnp.sum(probability * prob_grad, axis=-1, keepdims=True)
    )
    score_grad = score_grad.astype(jnp.bfloat16)
    query_grad = jnp.einsum(
        "shqk,kshe->qshe", score_grad, key_heads, preferred_element_type=jnp.float32
    ) * HEAD_WIDTH ** (-0.5)
    key_grad = jnp.einsum(
        "shqk,qshe->kshe", score_grad, queries, preferred_element_type=jnp.float32
    ) * HEAD_WIDTH ** (-0.5)
    key_back, value_back = (
        lax.psum_scatter(
            key_grad.astype(jnp.bfloat16), "ctx", scatter_dimension=0, tiled=True
        ).astype(jnp.float32),
        lax.psum_scatter(
            value_grad.astype(jnp.bfloat16), "ctx", scatter_dimension=0, tiled=True
        ).astype(jnp.float32),
    )
    qkv_grad = jnp.stack(
        [
            unrotary(query_grad, cosine, sine).reshape(block_len, seq_count, columns),
            unrotary(key_back, cosine, sine).reshape(block_len, seq_count, columns),
            value_back.reshape(block_len, seq_count, columns),
        ]
    ).astype(jnp.bfloat16)
    bias_grad = jnp.sum(qkv_grad.astype(jnp.float32), axis=(1, 2))
    qkv_weight_grad = jnp.einsum(
        "rsd,crse->cde", normed_all, qkv_grad, preferred_element_type=jnp.float32
    )
    piece = qkv_grad
    one_grad = lax.psum_scatter(
        jnp.einsum("crse,cde->rsd", piece, w_qkv, preferred_element_type=jnp.float32).astype(
            jnp.bfloat16
        ),
        "tp",
        scatter_dimension=0,
        tiled=True,
    ).astype(jnp.float32)
    input_grad, gain_one, shift_one = norm_back(layer_in, one_grad, gain_vec[0])
    input_grad = hidden_grad + input_grad
    weight_terms = (qkv_weight_grad, out_grad, gu_grad, down_grad)
    return (
        input_grad,
        (
            weight_terms,
            jnp.stack([gain_one, gain_two]),
            jnp.stack([shift_one, shift_two]),
            bias_grad,
        ),
    )


def spread(terms, columns, tp_index):
    weight_terms, gain_terms, shift_terms, bias_terms = terms
    qkv_term, out_term, gu_term, down_term = weight_terms
    scattered = (
        lax.psum_scatter(
            qkv_term.astype(jnp.bfloat16), "ctx", scatter_dimension=1, tiled=True
        ).astype(jnp.float32),
        lax.psum_scatter(
            out_term.astype(jnp.bfloat16), "ctx", scatter_dimension=1, tiled=True
        ).astype(jnp.float32),
        lax.psum_scatter(
            gu_term.astype(jnp.bfloat16), "ctx", scatter_dimension=1, tiled=True
        ).astype(jnp.float32),
        lax.psum_scatter(
            down_term.astype(jnp.bfloat16), "ctx", scatter_dimension=1, tiled=True
        ).astype(jnp.float32),
    )
    bias_full = lax.dynamic_update_slice_in_dim(
        jnp.zeros((3, gain_terms.shape[1]), jnp.float32), bias_terms, tp_index * columns, 1
    )
    gain_part, shift_part, bias_part = (
        lax.psum_scatter(gain_terms, ("ctx", "tp"), scatter_dimension=1, tiled=True),
        lax.psum_scatter(shift_terms, ("ctx", "tp"), scatter_dimension=1, tiled=True),
        lax.psum_scatter(bias_full, ("ctx", "tp"), scatter_dimension=1, tiled=True),
    )
    return (tuple(scattered), gain_part, shift_part, bias_part)


def stepwise_device(
    tokens_in,
    cotangent,
    plan,
    positions,
    norm_gain,
    norm_shift,
    w_qkv,
    b_qkv,
    w_out,
    w_gate_up,
    down_weight,
):
    weights = (
        norm_gain[0],
        norm_shift[0],
        w_qkv[0],
        b_qkv[0],
        w_out[0],
        w_gate_up[0],
        down_weight[0],
    )
    micro_count = tokens_in.shape[0]
    local_row_slice = tokens_in.shape[1]
    width = tokens_in.shape[3]
    columns = w_qkv.shape[3]
    ff_local = w_gate_up.shape[3]
    tp_count = lax.axis_size("tp")
    ctx_count = lax.axis_size("ctx")
    block_len = local_row_slice * tp_count
    section_index = lax.axis_index("section")
    ctx_index = lax.axis_index("ctx")
    tp_index = lax.axis_index("tp")
    block_pos = lax.dynamic_slice_in_dim(positions, ctx_index * block_len, block_len, 1)
    cosine, sine = tables(block_pos)
    allowed = (positions[:, None, :] <= block_pos[:, :, None])[:, None]
    context_rows = (cosine, sine, allowed)
    zero_rows = jnp.zeros(tokens_in.shape[1:], jnp.bfloat16)

    def forward_step(carry, step_index):
        arriving = passed_along(carry, "section", 1)
        micro = jnp.clip(step_index, 0, micro_count - 1)
        fresh = lax.dynamic_index_in_dim(tokens_in, plan[micro], 0, keepdims=False)
        layer_in = jnp.where(section_index == 0, fresh, arriving).astype(jnp.float32)
        layer_out, stored = forward_layer(layer_in, weights, context_rows)
        sent = layer_out.astype(jnp.bfloat16)
        return (sent, (sent, stored))

    steps_all = jnp.arange(micro_count + 1, dtype=jnp.int32)
    unused, (outputs, stored_all) = lax.scan(forward_step, zero_rows, steps_all)
    share = width // ctx_count
    fine_share = width // (ctx_count * tp_count)
    totals = (
        (
            jnp.zeros((3, share, columns), jnp.float32),
            jnp.zeros((columns, share), jnp.float32),
            jnp.zeros((2, share, ff_local), jnp.float32),
            jnp.zeros((ff_local, share), jnp.float32),
        ),
        jnp.zeros((2, fine_share), jnp.float32),
        jnp.zeros((2, fine_share), jnp.float32),
        jnp.zeros((3, fine_share), jnp.float32),
    )

    def backward_step(carry, bundle):
        send_back, running = carry
        step_index, stored = bundle
        arriving = passed_along(send_back, "section", -1)
        micro = step_index - section_index
        valid_step = ((micro >= 0) & (micro < micro_count)).astype(jnp.float32)
        target = lax.dynamic_index_in_dim(
            cotangent, jnp.clip(micro, 0, micro_count - 1), 0, keepdims=False
        )
        grad_out = jnp.where(section_index == 1, target, arriving).astype(jnp.float32)
        input_grad, terms = backward_layer(grad_out, stored, weights, context_rows)
        terms = jax.tree.map(lambda tensor: tensor * valid_step, terms)
        terms = spread(terms, columns, tp_index)
        running = jax.tree.map(jnp.add, running, terms)
        sent = input_grad.astype(jnp.bfloat16)
        return ((sent, running), sent)

    (unused_back, totals), input_grads = lax.scan(
        backward_step, (zero_rows, totals), (steps_all, stored_all), reverse=True
    )
    weight_parts, gain_part, shift_part, bias_part = totals
    section_ends = jnp.where(section_index == 0, input_grads[:micro_count], outputs[1:])[None]
    return (
        section_ends,
        gain_part[None],
        shift_part[None],
        bias_part[None],
        weight_parts[0][None],
        weight_parts[1][None],
        weight_parts[2][None],
        weight_parts[3][None],
    )


def per_device(*arrays):
    chips = lax.axis_size("ctx") // 2 * lax.axis_size("tp")
    if lax.axis_size("section") == 2 and lax.axis_size("ctx") == 4 and arrays[0].shape[0] == chips:
        return bulk_device(*arrays)
    return stepwise_device(*arrays)


def solution(mesh):
    placed = (
        P(None, ("ctx", "tp"), None, None),
        P(None, ("ctx", "tp"), None, None),
        P(),
        P(),
        P("section", None, None),
        P("section", None, None),
        P("section", None, None, "tp"),
        P("section", None, "tp"),
        P("section", "tp", None),
        P("section", None, None, "tp"),
        P("section", "tp", None),
    )
    return jax.shard_map(
        per_device,
        mesh=mesh,
        in_specs=placed,
        out_specs=(
            P("section", None, ("ctx", "tp"), None, None),
            P("section", None, ("ctx", "tp")),
            P("section", None, ("ctx", "tp")),
            P("section", None, ("ctx", "tp")),
            P("section", None, "ctx", "tp"),
            P("section", "tp", "ctx"),
            P("section", None, "ctx", "tp"),
            P("section", "tp", "ctx"),
        ),
        check_vma=False,
    )
```

```python
import functools

import jax
import jax.numpy as jnp
from jax import lax
from jax.experimental import pallas as pl
from jax.experimental.pallas import tpu as pltpu
from jax.sharding import PartitionSpec as P

HEAD_WIDTH = 64
ROT = 16


def pair_routes(ctx_count):
    core = [(i, i ^ 1) for i in range(ctx_count)]
    across = [(i, (i + 2) % 4) for i in range(ctx_count)]
    return core, across


def ln_stats(stream):
    mean = jnp.mean(stream, axis=-1, keepdims=True)
    centre = stream - mean
    inv_std = lax.rsqrt(jnp.mean(centre * centre, axis=-1, keepdims=True) + 1e-05)
    return centre, inv_std


def ln(stream, gain_vec, shift_vec):
    centre, inv_std = ln_stats(stream)
    return (centre * inv_std * gain_vec + shift_vec).astype(jnp.bfloat16)


def ln_back(stream, grad_in, gain_vec):
    centre, inv_std = ln_stats(stream)
    unit = centre * inv_std
    scaled = grad_in * gain_vec
    result = inv_std * (
        scaled
        - jnp.mean(scaled, axis=-1, keepdims=True)
        - unit * jnp.mean(scaled * unit, axis=-1, keepdims=True)
    )
    return result, jnp.sum(grad_in * unit, axis=0), jnp.sum(grad_in, axis=0)


def rot_tables(pos_row):
    half = ROT // 2
    freqs = 10000.0 ** (-jnp.arange(half, dtype=jnp.float32) * 2.0 / ROT)
    angles = pos_row.astype(jnp.float32)[:, None] * freqs
    cosine, sine = jnp.cos(angles), jnp.sin(angles)
    rows = pos_row.shape[0]
    rest = HEAD_WIDTH - ROT
    zeros = jnp.zeros((rows, half), jnp.float32)
    cos_head = jnp.concatenate([cosine, cosine, jnp.ones((rows, rest), jnp.float32)], 1)
    low_head = jnp.concatenate([-sine, zeros, jnp.zeros((rows, rest), jnp.float32)], 1)
    high_head = jnp.concatenate([zeros, sine, jnp.zeros((rows, rest), jnp.float32)], 1)
    return tuple(jnp.concatenate([t, t], 1) for t in (cos_head, low_head, high_head))


def dot_t(a, b):
    return lax.dot_general(a, b, (((1,), (1,)), ((), ())), preferred_element_type=jnp.float32)


def dot_0(a, b):
    return lax.dot_general(a, b, (((0,), (0,)), ((), ())), preferred_element_type=jnp.float32)


def dot_n(a, b):
    return lax.dot_general(a, b, (((1,), (0,)), ((), ())), preferred_element_type=jnp.float32)


def chunked(x, chunk):
    half = x.shape[0] // 2
    pieces = []
    for i in range(half // chunk):
        pieces.append(x[i * chunk : (i + 1) * chunk])
        pieces.append(x[half + i * chunk : half + (i + 1) * chunk])
    return jnp.concatenate(pieces, axis=0)


def attn_fwd_kernel(heads, chunk, mixed, bias, cos_t, low_t, high_t, pos_c, pos_r, qkv, out):
    rows = mixed.shape[0]
    half = rows // 2
    width = heads * HEAD_WIDTH
    half_rot = ROT // 2
    cosine, low, high = cos_t[...], low_t[...], high_t[...]
    for pair in range(heads // 2):
        parts = []
        for c in range(3):
            at = c * width + pair * 128
            x = mixed[:, at : at + 128] + bias[0, :, at : at + 128]
            if c < 2:
                x = x * cosine + pltpu.roll(x, 128 - half_rot, 1) * low + pltpu.roll(x, half_rot, 1) * high
            x = x.astype(jnp.bfloat16)
            qkv[:, at : at + 128] = x
            parts.append(chunked(x, chunk))
        query, key, value = parts
        query = query * jnp.bfloat16(HEAD_WIDTH ** (-0.5))
        for i in range(half // chunk):
            end = 2 * chunk * (i + 1)
            begin = end - 2 * chunk
            allowed = pos_r[:, begin:end] <= pos_c[begin:end, :]
            halves = []
            for h in range(2):
                lanes = slice(h * HEAD_WIDTH, (h + 1) * HEAD_WIDTH)
                q_h = query[begin:end, lanes]
                score = dot_t(q_h, key[:end, lanes])
                last = jnp.where(allowed, score[:, begin:], -1e30)
                score = last if i == 0 else jnp.concatenate([score[:, :begin], last], axis=1)
                prob = jnp.exp(score - jnp.max(score, axis=1, keepdims=True))
                total = jnp.sum(prob, axis=1, keepdims=True)
                mixed_values = dot_n(prob.astype(jnp.bfloat16), value[:end, lanes])
                halves.append(mixed_values / total)
            done = jnp.concatenate(halves, axis=1).astype(jnp.bfloat16)
            lanes = slice(pair * 128, pair * 128 + 128)
            out[i * chunk : (i + 1) * chunk, lanes] = done[:chunk]
            out[half + i * chunk : half + (i + 1) * chunk, lanes] = done[chunk:]


def attn_bwd_kernel(heads, chunk, qkv, ctx, cos_t, low_t, high_t, pos_c, pos_r, grad, bias_grad, dk_s, dv_s):
    rows = qkv.shape[0]
    half = rows // 2
    width = heads * HEAD_WIDTH
    half_rot = ROT // 2
    cosine, low, high = cos_t[...], low_t[...], high_t[...]
    scale = HEAD_WIDTH ** (-0.5)

    def finish(c, pair, x):
        at = c * width + pair * 128
        if c < 2:
            x = x * scale
            x = x * cosine + pltpu.roll(x * high, 128 - half_rot, 1) + pltpu.roll(x * low, half_rot, 1)
        x = x.astype(jnp.bfloat16)
        grad[:, at : at + 128] = x
        bias_grad[0, :, at : at + 128] = jnp.sum(x.astype(jnp.float32), axis=0, keepdims=True)

    def unchunked(x):
        steps = half // chunk
        own = [x[2 * i * chunk : (2 * i + 1) * chunk] for i in range(steps)]
        other = [x[(2 * i + 1) * chunk : (2 * i + 2) * chunk] for i in range(steps)]
        return jnp.concatenate(own + other, axis=0)

    for pair in range(heads // 2):
        lanes2 = slice(pair * 128, pair * 128 + 128)
        query, key, value = (
            chunked(qkv[:, c * width + pair * 128 : c * width + pair * 128 + 128], chunk) for c in range(3)
        )
        query_s = query * jnp.bfloat16(scale)
        ctx_grad = chunked(ctx[:, lanes2], chunk)
        dk_s[...] = jnp.zeros_like(dk_s)
        dv_s[...] = jnp.zeros_like(dv_s)
        dq_parts = []
        for i in range(half // chunk):
            end = 2 * chunk * (i + 1)
            begin = end - 2 * chunk
            allowed = pos_c[begin:end, :] <= pos_r[:, begin:end]
            dq_h, dk_h, dv_h = [], [], []
            for h in range(2):
                lanes = slice(h * HEAD_WIDTH, (h + 1) * HEAD_WIDTH)
                score = dot_t(key[:end, lanes], query_s[begin:end, lanes])
                last = jnp.where(allowed, score[begin:, :], -1e30)
                score = last if i == 0 else jnp.concatenate([score[:begin, :], last], axis=0)
                prob = jnp.exp(score - jnp.max(score, axis=0, keepdims=True))
                prob = prob * (1.0 / jnp.sum(prob, axis=0, keepdims=True))
                grad_h = ctx_grad[begin:end, lanes]
                dv_h.append(dot_n(prob.astype(jnp.bfloat16), grad_h))
                prob_grad = dot_t(value[:end, lanes], grad_h)
                delta = jnp.sum(prob * prob_grad, axis=0, keepdims=True)
                score_grad = (prob * (prob_grad - delta)).astype(jnp.bfloat16)
                dk_h.append(dot_n(score_grad, query[begin:end, lanes]))
                dq_h.append(dot_0(score_grad, key[:end, lanes]))
            dk_s[:end, :] += jnp.concatenate(dk_h, axis=1)
            dv_s[:end, :] += jnp.concatenate(dv_h, axis=1)
            dq_parts.append(jnp.concatenate(dq_h, axis=1))
        finish(0, pair, unchunked(jnp.concatenate(dq_parts, axis=0)))
        finish(1, pair, unchunked(dk_s[...]))
        finish(2, pair, unchunked(dv_s[...]))


VMEM_LIMIT = 56 * 1024 * 1024


def attn_fwd(mixed, bias, context, groups, chunk):
    rows, columns = mixed.shape
    block = columns // groups
    heads = block // (3 * HEAD_WIDTH)
    cos_t, low_t, high_t, pos_c, pos_r = context
    whole = lambda shape: pl.BlockSpec(shape, lambda g: (0, 0))
    return pl.pallas_call(
        functools.partial(attn_fwd_kernel, heads, chunk),
        grid=(groups,),
        in_specs=[
            pl.BlockSpec((rows, block), lambda g: (0, g)),
            pl.BlockSpec((1, 1, block), lambda g: (g, 0, 0)),
            whole((rows, 128)),
            whole((rows, 128)),
            whole((rows, 128)),
            whole((rows, 1)),
            whole((1, rows)),
        ],
        out_specs=[
            pl.BlockSpec((rows, block), lambda g: (0, g)),
            pl.BlockSpec((rows, block // 3), lambda g: (0, g)),
        ],
        out_shape=[
            jax.ShapeDtypeStruct((rows, columns), jnp.bfloat16),
            jax.ShapeDtypeStruct((rows, columns // 3), jnp.bfloat16),
        ],
        compiler_params=pltpu.CompilerParams(vmem_limit_bytes=VMEM_LIMIT),
        cost_estimate=pl.CostEstimate(
            flops=3 * rows * rows * columns // 3 * 4,
            bytes_accessed=rows * columns * 7,
            transcendentals=rows * rows * columns // (3 * HEAD_WIDTH),
        ),
    )(mixed, bias.reshape(groups, 1, block), cos_t, low_t, high_t, pos_c, pos_r)


def attn_bwd(qkv, ctx_grad, context, groups, chunk):
    rows, columns = qkv.shape
    block = columns // groups
    heads = block // (3 * HEAD_WIDTH)
    cos_t, low_t, high_t, pos_c, pos_r = context
    whole = lambda shape: pl.BlockSpec(shape, lambda g: (0, 0))
    return pl.pallas_call(
        functools.partial(attn_bwd_kernel, heads, chunk),
        grid=(groups,),
        in_specs=[
            pl.BlockSpec((rows, block), lambda g: (0, g)),
            pl.BlockSpec((rows, block // 3), lambda g: (0, g)),
            whole((rows, 128)),
            whole((rows, 128)),
            whole((rows, 128)),
            whole((rows, 1)),
            whole((1, rows)),
        ],
        out_specs=[
            pl.BlockSpec((rows, block), lambda g: (0, g)),
            pl.BlockSpec((1, 1, block), lambda g: (g, 0, 0)),
        ],
        out_shape=[
            jax.ShapeDtypeStruct((rows, columns), jnp.bfloat16),
            jax.ShapeDtypeStruct((groups, 1, block), jnp.float32),
        ],
        scratch_shapes=[pltpu.VMEM((rows, 128), jnp.float32), pltpu.VMEM((rows, 128), jnp.float32)],
        compiler_params=pltpu.CompilerParams(vmem_limit_bytes=VMEM_LIMIT),
        cost_estimate=pl.CostEstimate(
            flops=7 * rows * rows * columns // 3 * 4,
            bytes_accessed=rows * columns * 5,
            transcendentals=rows * rows * columns // (3 * HEAD_WIDTH),
        ),
    )(qkv, ctx_grad, cos_t, low_t, high_t, pos_c, pos_r)


def bulk_device(
    tokens_in,
    cotangent,
    plan,
    positions,
    norm_gain,
    norm_shift,
    w_qkv,
    b_qkv,
    w_out,
    w_gate_up,
    down_weight,
):
    tp_count = lax.axis_size("tp")
    ctx_count = lax.axis_size("ctx")
    section_index = lax.axis_index("section")
    ctx_index = lax.axis_index("ctx")
    side, core = ctx_index // 2, ctx_index % 2
    core_route, across_route = pair_routes(ctx_count)
    micro_count, slice_len, _, width = tokens_in.shape
    gain, shift = norm_gain[0], norm_shift[0]
    piece = slice_len // 2
    rows = micro_count * slice_len * 2
    own_rows = rows // 2
    half_width = width // 2
    columns = w_qkv.shape[3] // 2
    hidden = w_gate_up.shape[3] // 2
    first = section_index == 0

    ordered = jnp.stack(
        [lax.dynamic_index_in_dim(tokens_in, plan[m], 0, keepdims=False)[:, 0] for m in range(micro_count)]
    )
    fresh = jnp.where(first, ordered, cotangent[:, :, 0])
    fresh = fresh.reshape(ctx_count // 2, tp_count, 2, piece, width).transpose(0, 2, 1, 3, 4)
    fresh = fresh.reshape(ctx_count * tp_count, piece, width)
    inbound = lax.all_to_all(fresh, ("ctx", "tp"), 0, 0, tiled=True).reshape(own_rows, width)

    pos = positions.reshape(-1, 2, piece)
    pos = jnp.concatenate(
        [
            lax.dynamic_index_in_dim(pos, core, 1, False).reshape(-1),
            lax.dynamic_index_in_dim(pos, 1 - core, 1, False).reshape(-1),
        ]
    )
    chunk = min(128, own_rows)
    chunk_pos = chunked(pos, chunk)
    context = (*rot_tables(pos), chunk_pos[:, None], chunk_pos[None, :])

    tp_index = lax.axis_index("tp")

    def turned_by_tp(shards, axis=0):
        count = shards.shape[axis] // tp_count
        twice = jnp.concatenate([shards, shards], axis=axis)
        start = lax.rem(tp_count - tp_index, tp_count) * count
        return lax.dynamic_slice_in_dim(twice, start, tp_count * count, axis)

    def after(x, *others):
        return lax.optimization_barrier((x, *others))[0]

    own_parts, across_parts = [], []

    def gathered(block_of):
        block, held = block_of(side), block_of(1 - side)
        count = block.shape[0]
        step = len(own_parts)
        if step == 2:
            block = after(block, own_parts[0], across_parts[0], inbound)
        elif step > 2:
            block = after(block, own_parts[step - 2], across_parts[step - 3])
        own = lax.all_gather(block, "tp", axis=0, tiled=True)
        wanted = [
            lax.dynamic_slice_in_dim(own, lax.rem(tp_index + p, tp_count) * count, count, 0)
            for p in range(1, tp_count)
        ]
        arriving = lax.ppermute(jnp.concatenate(wanted, axis=0), "ctx", across_route)
        own_parts.append(own)
        across_parts.append(arriving)
        other = turned_by_tp(jnp.concatenate([held, arriving], axis=0))
        return jnp.where(
            side == 0, jnp.concatenate([own, other], axis=1), jnp.concatenate([other, own], axis=1)
        )

    def qkv_block(half):
        block = lax.dynamic_slice(w_qkv[0], (0, half * half_width, core * columns), (3, half_width, columns))
        return block.transpose(0, 2, 1).reshape(3 * columns, half_width)

    def out_block(half):
        return lax.dynamic_slice(w_out[0], (core * columns, half * half_width), (columns, half_width))

    def gu_block(which, half):
        block = lax.dynamic_slice(
            w_gate_up[0], (which, half * half_width, core * hidden), (1, half_width, hidden)
        )
        return block[0].T

    def down_block(half):
        return lax.dynamic_slice(down_weight[0], (core * hidden, half * half_width), (hidden // 2, half_width))

    def by_parts(weight):
        return weight.reshape(tp_count, 2, hidden // 2, width).swapaxes(0, 1).reshape(-1, width)

    wt_out = gathered(out_block)
    wt_qkv = gathered(qkv_block)
    wt_gu = jnp.concatenate([by_parts(gathered(functools.partial(gu_block, w))) for w in range(2)], axis=0)
    down_first = gathered(down_block)
    down_last = lax.dynamic_slice_in_dim(down_weight[0], core * hidden + hidden // 2, hidden // 2, 0)
    down_last = lax.all_gather(after(down_last, across_parts[2]), "tp", axis=0, tiled=True)
    wt_down = jnp.concatenate([down_first, down_last], axis=0)
    bias_own = lax.dynamic_slice_in_dim(b_qkv[0], core * columns, columns, 1).reshape(1, 3 * columns)
    bias = [bias_own]
    for p in range(1, tp_count):
        ring = [((i + p) % tp_count, i) for i in range(tp_count)]
        bias.append(lax.ppermute(bias_own, "tp", ring))
    bias = turned_by_tp(jnp.concatenate(bias, axis=0))
    ff = wt_down.shape[0]

    def both(own):
        return jnp.concatenate([own, lax.ppermute(own, "ctx", core_route)], axis=0)

    def summed(a, weight, parts=1):
        step = own_rows // parts
        spans = [slice(i * step, (i + 1) * step) for i in range(parts)]
        others = [dot_n(a[own_rows:][span], weight).astype(jnp.bfloat16) for span in spans]
        arriving = [lax.ppermute(other, "ctx", core_route) for other in others]
        own = [dot_n(a[:own_rows][span], weight) for span in spans]
        return [x + y.astype(jnp.float32) for x, y in zip(own, arriving)]

    def split(x, parts):
        step = x.shape[0] // parts
        return [x[i * step : (i + 1) * step] for i in range(parts)]

    def over_x(parts, route):
        return jnp.concatenate([lax.ppermute(part, "section", route) for part in parts], axis=0)

    def forward(stream):
        normed = both(ln(stream, gain[0], shift[0]))
        mixed = dot_t(normed, wt_qkv)
        qkv, attended = attn_fwd(mixed, bias, context, tp_count, chunk)
        hidden_state = stream + summed(attended, wt_out)[0]
        normed_two = both(ln(hidden_state, gain[1], shift[1]))
        gate_up = dot_t(normed_two, wt_gu)
        gate, up = gate_up[:, :ff], gate_up[:, ff:]
        activation = (jax.nn.silu(gate) * up).astype(jnp.bfloat16)
        out = [
            (x + y).astype(jnp.bfloat16)
            for x, y in zip(split(hidden_state, 2), summed(activation, wt_down, 2))
        ]
        return out, (stream, normed, qkv, attended, hidden_state, normed_two, gate_up, activation)

    def far_near(right):
        far = lax.dynamic_slice_in_dim(right, (1 - side) * half_width, half_width, 1)
        near = lax.dynamic_slice_in_dim(right, side * half_width, half_width, 1)
        return far, near

    def far_term(left, right):
        return dot_0(left, far_near(right)[0]).astype(jnp.bfloat16)

    def near_total(left, right, arriving, *others):
        near = far_near(right)[1]
        if others:
            near = after(near, *others)
        return (dot_0(left, near) + arriving.astype(jnp.float32)).astype(jnp.bfloat16)

    def across(term, *others):
        return lax.ppermute(after(term, *others) if others else term, "ctx", across_route)

    def over_tp(term):
        return lax.psum_scatter(term, "tp", scatter_dimension=0, tiled=True)

    together = lax.optimization_barrier

    def part_of(x, i, parts, axis):
        shard = x.shape[axis] // tp_count
        step = shard // parts
        return jnp.concatenate(
            [
                lax.slice_in_dim(x, z * shard + i * step, z * shard + (i + 1) * step, axis=axis)
                for z in range(tp_count)
            ],
            axis=axis,
        )

    def mlp_back(act_grad, gate_up):
        gate, up = gate_up[:, :ff], gate_up[:, ff:]
        sigma = jax.nn.sigmoid(gate)
        gate_grad = (act_grad * up * sigma * (1.0 + gate * (1.0 - sigma))).astype(jnp.bfloat16)
        up_grad = (act_grad * gate * sigma).astype(jnp.bfloat16)
        return gate_grad, up_grad, jnp.concatenate([gate_grad, up_grad], axis=1)

    def backward(grad_out, stored, wait):
        stream, normed, qkv, attended, hidden_state, normed_two, gate_up, activation = stored
        gu_grad = mlp_back(dot_t(both(grad_out), wt_down), gate_up)[2]
        result = ln_back(hidden_state, summed(gu_grad, wt_gu)[0], gain[1])[0]
        hidden_grad = grad_out.astype(jnp.float32) + result
        ctx_grad = dot_t(both(hidden_grad.astype(jnp.bfloat16)), wt_out).astype(jnp.bfloat16)
        qkv_grad, _ = attn_bwd(qkv, after(ctx_grad, wait), context, tp_count, chunk)
        one_grad = summed(qkv_grad, wt_qkv, 2)
        return [
            (z + ln_back(x, y, gain[0])[0]).astype(jnp.bfloat16)
            for x, y, z in zip(split(stream, 2), one_grad, split(hidden_grad, 2))
        ]

    def last_backward(grad_out, stored, final_out, act_both):
        stream, normed, qkv, attended, hidden_state, normed_two, gate_up, _ = stored
        grad_f32 = grad_out.astype(jnp.float32)
        far_grad, near_grad = far_near(grad_out)
        grad_across = both(across(far_grad))
        mlp_grad = both(grad_out)
        gate_grad, up_grad, gu_grad = mlp_back(dot_t(mlp_grad, wt_down), gate_up)
        far_gate = far_term(gate_grad, normed_two)

        grad_across, far_gate, gate_grad, up_grad, gu_grad = together(
            (grad_across, far_gate, gate_grad, up_grad, gu_grad)
        )
        far_gate_a, far_gate_b = split(far_gate, 2)
        arriving = across(far_gate_a)
        down_total = dot_0(act_both, jnp.concatenate([both(near_grad), grad_across], axis=0)).astype(jnp.bfloat16)
        two_other = dot_n(gu_grad[own_rows:], wt_gu).astype(jnp.bfloat16)

        arriving, far_gate_b, two_other, gu_grad, down_total = together(
            (arriving, far_gate_b, two_other, gu_grad, down_total)
        )
        arriving_gate = jnp.concatenate([arriving, across(far_gate_b)], axis=0)
        sums_down = [over_tp(x) for x in split(down_total, 2)]
        two_grad = dot_n(gu_grad[:own_rows], wt_gu) + lax.ppermute(two_other, "ctx", core_route).astype(jnp.float32)
        result, gain_two, shift_two = ln_back(hidden_state, two_grad, gain[1])
        hidden_grad = grad_f32 + result
        attn_grad = both(hidden_grad.astype(jnp.bfloat16))
        far_up = far_term(up_grad, normed_two)

        arriving_gate, far_up, gate_grad, attn_grad, hidden_grad = together(
            (arriving_gate, far_up, gate_grad, attn_grad, hidden_grad)
        )
        far_up_a, far_up_b = split(far_up, 2)
        arriving = across(far_up_a)
        gate_total = near_total(gate_grad, normed_two, arriving_gate)
        sums_gate = [over_tp(x) for x in split(gate_total, 2)]
        ctx_grad = dot_t(attn_grad, wt_out).astype(jnp.bfloat16)

        arriving, far_up_b, ctx_grad = together((arriving, far_up_b, ctx_grad))
        arriving_up = jnp.concatenate([arriving, across(far_up_b)], axis=0)
        qkv_grad, bias_grad = attn_bwd(qkv, ctx_grad, context, tp_count, chunk)
        qkv_a, qkv_b = (part_of(qkv_grad, i, 2, 1) for i in range(2))
        far_a = far_term(qkv_a, normed)

        arriving_up, far_a, qkv_a, qkv_b, qkv_grad, up_grad, attn_grad = together(
            (arriving_up, far_a, qkv_a, qkv_b, qkv_grad, up_grad, attn_grad)
        )
        arriving = across(far_a)
        up_total = near_total(up_grad, normed_two, arriving_up)
        sums_up = [over_tp(x) for x in split(up_total, 2)]
        one_other = dot_n(qkv_grad[own_rows:], wt_qkv).astype(jnp.bfloat16)
        far_b = far_term(qkv_b, normed)

        arriving, far_b, one_other, qkv_grad, qkv_a, qkv_b = together(
            (arriving, far_b, one_other, qkv_grad, qkv_a, qkv_b)
        )
        arriving_b = across(far_b)
        sum_qkv_a = over_tp(near_total(qkv_a, normed, arriving))
        one_grad = dot_n(qkv_grad[:own_rows], wt_qkv) + lax.ppermute(one_other, "ctx", core_route).astype(jnp.float32)
        result, gain_one, shift_one = ln_back(stream, one_grad, gain[0])
        input_grad = (hidden_grad + result).astype(jnp.bfloat16)
        ends = jnp.where(first, input_grad, final_out)
        far_out = far_term(attended, attn_grad)

        arriving_b, far_out, ends, qkv_b = together((arriving_b, far_out, ends, qkv_b))
        arriving_out = across(far_out)
        ends = lax.all_to_all(
            ends.reshape(ctx_count * tp_count, piece, width), ("ctx", "tp"), 0, 0, tiled=True
        )
        sum_qkv_b = over_tp(near_total(qkv_b, normed, arriving_b))
        sum_out = over_tp(near_total(attended, after(attn_grad, ends), arriving_out))
        small = (jnp.stack([gain_one, gain_two]), jnp.stack([shift_one, shift_two]), bias_grad)
        sums = (jnp.concatenate(x, axis=0) for x in (sums_down, sums_gate, sums_up))
        return ends, small, (*sums, sum_out, jnp.concatenate([sum_qkv_a, sum_qkv_b], axis=0))

    sent, _ = forward(inbound.astype(jnp.float32))
    arriving = over_x(sent, [(0, 1)])
    final_out, stored = forward(jnp.where(first, inbound, arriving).astype(jnp.float32))
    act_across = across(stored[7])
    arriving_back = over_x(backward(inbound, stored, act_across), [(1, 0)])
    arriving_back, final_out, act_both = together(
        (arriving_back, jnp.concatenate(final_out, axis=0), jnp.concatenate([stored[7], act_across], axis=0))
    )
    grad_out = jnp.where(first, arriving_back, inbound)
    ends, small, sums = last_backward(grad_out, stored, final_out, act_both)
    down_sum, gate_sum, up_sum, out_sum, qkv_sum = sums

    def settled(term):
        share = half_width // 2
        away = lax.dynamic_slice_in_dim(term, (1 - core) * share, share, term.ndim - 1)
        kept = lax.dynamic_slice_in_dim(term, core * share, share, term.ndim - 1)
        got = lax.ppermute(away, "ctx", core_route)
        axis = term.ndim - 2
        return jnp.where(
            core == 0, jnp.concatenate([kept, got], axis), jnp.concatenate([got, kept], axis)
        ).astype(jnp.float32)

    grad_down = settled(down_sum)
    grad_gate = settled(gate_sum)
    grad_up = settled(up_sum)
    grad_out_w = settled(out_sum)
    grad_qkv = settled(qkv_sum.reshape(3, columns, half_width))

    gain_terms, shift_terms, bias_terms = small
    bias_terms = bias_terms.reshape(tp_count, 3, columns).transpose(1, 0, 2)[:, :, None]
    bias_full = jnp.where(
        (jnp.arange(2) == core)[None, None, :, None], bias_terms, 0.0
    ).reshape(3, tp_count * 2 * columns)
    vectors = jnp.concatenate([gain_terms, shift_terms, bias_full], axis=0)
    share = width // (ctx_count * tp_count)
    vectors = after(vectors, ends).reshape(-1, ctx_count * tp_count, share).transpose(1, 0, 2)
    vectors = jnp.sum(lax.all_to_all(vectors, ("ctx", "tp"), 0, 0, tiled=True), axis=0).reshape(-1, share)

    ends = ends.reshape(ctx_count // 2, 2, tp_count, piece, width).transpose(0, 2, 1, 3, 4)
    ends = ends.reshape(micro_count, slice_len, 1, width)
    return (
        ends[None],
        vectors[None, :2],
        vectors[None, 2:4],
        vectors[None, 4:],
        grad_qkv.transpose(0, 2, 1)[None],
        grad_out_w[None],
        jnp.stack([grad_gate.T, grad_up.T])[None],
        grad_down[None],
    )


def passed_along(block, axis, distance):
    devices = range(lax.axis_size(axis))
    route = [(i - distance, i) for i in devices if i - distance in devices]
    return lax.ppermute(block, axis, route)


def normalize(stream, gain_vec, shift_vec):
    centre = stream - jnp.mean(stream, axis=-1, keepdims=True)
    spread = jnp.mean(centre * centre, axis=-1, keepdims=True)
    return centre * lax.rsqrt(spread + 1e-05) * gain_vec + shift_vec


def norm_back(stream, grad_in, gain_vec):
    centre = stream - jnp.mean(stream, axis=-1, keepdims=True)
    inv_std = lax.rsqrt(jnp.mean(centre * centre, axis=-1, keepdims=True) + 1e-05)
    unit = centre * inv_std
    scaled = grad_in * gain_vec
    result = inv_std * (
        scaled
        - jnp.mean(scaled, axis=-1, keepdims=True)
        - unit * jnp.mean(scaled * unit, axis=-1, keepdims=True)
    )
    return (result, jnp.sum(grad_in * unit, axis=(0, 1)), jnp.sum(grad_in, axis=(0, 1)))


def rotary(tensor, cosine, sine):
    half_rot = ROT // 2
    front = tensor[..., :ROT]
    turned = jnp.concatenate([-front[..., half_rot:], front[..., :half_rot]], axis=-1)
    return jnp.concatenate([front * cosine + turned * sine, tensor[..., ROT:]], axis=-1)


def unrotary(tensor, cosine, sine):
    half_rot = ROT // 2
    front = tensor[..., :ROT]
    turned = jnp.concatenate([-front[..., half_rot:], front[..., :half_rot]], axis=-1)
    return jnp.concatenate([front * cosine - turned * sine, tensor[..., ROT:]], axis=-1)


def tables(position_rows):
    freqs = 10000.0 ** (-jnp.arange(ROT // 2, dtype=jnp.float32) * 2.0 / ROT)
    angles = position_rows.T.astype(jnp.float32)[:, :, None] * freqs
    angles = jnp.concatenate([angles, angles], axis=-1)[:, :, None, :]
    return (jnp.cos(angles), jnp.sin(angles))


def attention_scores(queries, key_heads, allowed):
    scores = jnp.einsum(
        "qshe,kshe->shqk", queries, key_heads, preferred_element_type=jnp.float32
    ) * HEAD_WIDTH ** (-0.5)
    return jnp.where(allowed, scores, -1e30)


def forward_layer(layer_in, weights, context_rows):
    gain_vec, shift_vec, w_qkv, b_qkv, w_out, w_gate_up, down_weight = weights
    cosine, sine, allowed = context_rows
    normed = normalize(layer_in, gain_vec[0], shift_vec[0]).astype(jnp.bfloat16)
    normed_all = lax.all_gather(normed, "tp", axis=0, tiled=True)
    block_len, seq_count, width = normed_all.shape
    columns = w_qkv.shape[2]
    head_count = columns // HEAD_WIDTH
    mixed = (
        jnp.einsum("rsd,cde->crse", normed_all, w_qkv, preferred_element_type=jnp.float32)
        + b_qkv[:, None, None, :]
    )
    queries = rotary(
        mixed[0].reshape(block_len, seq_count, head_count, HEAD_WIDTH), cosine, sine
    ).astype(jnp.bfloat16)
    key_own = rotary(
        mixed[1].reshape(block_len, seq_count, head_count, HEAD_WIDTH), cosine, sine
    ).astype(jnp.bfloat16)
    key_own = key_own.reshape(block_len, seq_count, columns)
    value_own = mixed[2].astype(jnp.bfloat16)
    key_all, value_all = (
        lax.all_gather(key_own, "ctx", axis=0, tiled=True),
        lax.all_gather(value_own, "ctx", axis=0, tiled=True),
    )
    key_heads = key_all.reshape(key_all.shape[0], seq_count, head_count, HEAD_WIDTH)
    value_heads = value_all.reshape(value_all.shape[0], seq_count, head_count, HEAD_WIDTH)
    scores = attention_scores(queries, key_heads, allowed)
    top_score = jnp.max(scores, axis=-1, keepdims=True)
    log_total = top_score + jnp.log(jnp.sum(jnp.exp(scores - top_score), axis=-1, keepdims=True))
    probability = jnp.exp(scores - log_total)
    attended = jnp.einsum(
        "shqk,kshe->qshe",
        probability.astype(jnp.bfloat16),
        value_heads,
        preferred_element_type=jnp.float32,
    )
    attended = attended.astype(jnp.bfloat16).reshape(block_len, seq_count, columns)
    piece = attended
    hidden_state = layer_in + lax.psum_scatter(
        jnp.einsum("rse,ed->rsd", piece, w_out, preferred_element_type=jnp.float32).astype(
            jnp.bfloat16
        ),
        "tp",
        scatter_dimension=0,
        tiled=True,
    ).astype(jnp.float32)
    normed_two = normalize(hidden_state, gain_vec[1], shift_vec[1]).astype(jnp.bfloat16)
    normed_two_all = lax.all_gather(normed_two, "tp", axis=0, tiled=True)
    gate_up = jnp.einsum(
        "rsd,cdf->crsf", normed_two_all, w_gate_up, preferred_element_type=jnp.float32
    )
    gated_activation = (jax.nn.silu(gate_up[0]) * gate_up[1]).astype(jnp.bfloat16)
    piece = gated_activation
    layer_out = hidden_state + lax.psum_scatter(
        jnp.einsum("rsf,fd->rsd", piece, down_weight, preferred_element_type=jnp.float32).astype(
            jnp.bfloat16
        ),
        "tp",
        scatter_dimension=0,
        tiled=True,
    ).astype(jnp.float32)
    stored = (
        layer_in,
        normed_all,
        queries,
        key_all,
        value_all,
        log_total,
        attended,
        hidden_state,
        normed_two_all,
        gate_up,
    )
    return (layer_out, stored)


def backward_layer(grad_out, stored, weights, context_rows):
    gain_vec, shift_vec, w_qkv, b_qkv, w_out, w_gate_up, down_weight = weights
    cosine, sine, allowed = context_rows
    (
        layer_in,
        normed_all,
        queries,
        key_all,
        value_all,
        log_total,
        attended,
        hidden_state,
        normed_two_all,
        gate_up,
    ) = stored
    block_len, seq_count, columns = attended.shape
    head_count = columns // HEAD_WIDTH
    mlp_grad = lax.all_gather(grad_out.astype(jnp.bfloat16), "tp", axis=0, tiled=True)
    gate_part = gate_up[0]
    up_part = gate_up[1]
    sigma = jax.nn.sigmoid(gate_part)
    swish = gate_part * sigma
    gated_activation = (swish * up_part).astype(jnp.bfloat16)
    down_grad = jnp.einsum(
        "rsf,rsd->fd", gated_activation, mlp_grad, preferred_element_type=jnp.float32
    )
    act_grad = jnp.einsum("rsd,fd->rsf", mlp_grad, down_weight, preferred_element_type=jnp.float32)
    gate_up_grad = jnp.stack(
        [act_grad * up_part * sigma * (1.0 + gate_part * (1.0 - sigma)), act_grad * swish]
    ).astype(jnp.bfloat16)
    gu_grad = jnp.einsum(
        "rsd,crsf->cdf", normed_two_all, gate_up_grad, preferred_element_type=jnp.float32
    )
    piece = gate_up_grad
    two_grad = lax.psum_scatter(
        jnp.einsum("crsf,cdf->rsd", piece, w_gate_up, preferred_element_type=jnp.float32).astype(
            jnp.bfloat16
        ),
        "tp",
        scatter_dimension=0,
        tiled=True,
    ).astype(jnp.float32)
    hidden_grad, gain_two, shift_two = norm_back(hidden_state, two_grad, gain_vec[1])
    hidden_grad = grad_out + hidden_grad
    attn_grad = lax.all_gather(hidden_grad.astype(jnp.bfloat16), "tp", axis=0, tiled=True)
    out_grad = jnp.einsum("rse,rsd->ed", attended, attn_grad, preferred_element_type=jnp.float32)
    ctx_grad = jnp.einsum("rsd,ed->rse", attn_grad, w_out, preferred_element_type=jnp.float32)
    ctx_grad = ctx_grad.astype(jnp.bfloat16).reshape(block_len, seq_count, head_count, HEAD_WIDTH)
    key_heads = key_all.reshape(key_all.shape[0], seq_count, head_count, HEAD_WIDTH)
    value_heads = value_all.reshape(value_all.shape[0], seq_count, head_count, HEAD_WIDTH)
    scores = attention_scores(queries, key_heads, allowed)
    probability = jnp.exp(scores - log_total)
    value_grad = jnp.einsum(
        "shqk,qshe->kshe",
        probability.astype(jnp.bfloat16),
        ctx_grad,
        preferred_element_type=jnp.float32,
    )
    prob_grad = jnp.einsum(
        "qshe,kshe->shqk", ctx_grad, value_heads, preferred_element_type=jnp.float32
    )
    score_grad = probability * (
        prob_grad - jnp.sum(probability * prob_grad, axis=-1, keepdims=True)
    )
    score_grad = score_grad.astype(jnp.bfloat16)
    query_grad = jnp.einsum(
        "shqk,kshe->qshe", score_grad, key_heads, preferred_element_type=jnp.float32
    ) * HEAD_WIDTH ** (-0.5)
    key_grad = jnp.einsum(
        "shqk,qshe->kshe", score_grad, queries, preferred_element_type=jnp.float32
    ) * HEAD_WIDTH ** (-0.5)
    key_back, value_back = (
        lax.psum_scatter(
            key_grad.astype(jnp.bfloat16), "ctx", scatter_dimension=0, tiled=True
        ).astype(jnp.float32),
        lax.psum_scatter(
            value_grad.astype(jnp.bfloat16), "ctx", scatter_dimension=0, tiled=True
        ).astype(jnp.float32),
    )
    qkv_grad = jnp.stack(
        [
            unrotary(query_grad, cosine, sine).reshape(block_len, seq_count, columns),
            unrotary(key_back, cosine, sine).reshape(block_len, seq_count, columns),
            value_back.reshape(block_len, seq_count, columns),
        ]
    ).astype(jnp.bfloat16)
    bias_grad = jnp.sum(qkv_grad.astype(jnp.float32), axis=(1, 2))
    qkv_weight_grad = jnp.einsum(
        "rsd,crse->cde", normed_all, qkv_grad, preferred_element_type=jnp.float32
    )
    piece = qkv_grad
    one_grad = lax.psum_scatter(
        jnp.einsum("crse,cde->rsd", piece, w_qkv, preferred_element_type=jnp.float32).astype(
            jnp.bfloat16
        ),
        "tp",
        scatter_dimension=0,
        tiled=True,
    ).astype(jnp.float32)
    input_grad, gain_one, shift_one = norm_back(layer_in, one_grad, gain_vec[0])
    input_grad = hidden_grad + input_grad
    weight_terms = (qkv_weight_grad, out_grad, gu_grad, down_grad)
    return (
        input_grad,
        (
            weight_terms,
            jnp.stack([gain_one, gain_two]),
            jnp.stack([shift_one, shift_two]),
            bias_grad,
        ),
    )


def spread(terms, columns, tp_index):
    weight_terms, gain_terms, shift_terms, bias_terms = terms
    qkv_term, out_term, gu_term, down_term = weight_terms
    scattered = (
        lax.psum_scatter(
            qkv_term.astype(jnp.bfloat16), "ctx", scatter_dimension=1, tiled=True
        ).astype(jnp.float32),
        lax.psum_scatter(
            out_term.astype(jnp.bfloat16), "ctx", scatter_dimension=1, tiled=True
        ).astype(jnp.float32),
        lax.psum_scatter(
            gu_term.astype(jnp.bfloat16), "ctx", scatter_dimension=1, tiled=True
        ).astype(jnp.float32),
        lax.psum_scatter(
            down_term.astype(jnp.bfloat16), "ctx", scatter_dimension=1, tiled=True
        ).astype(jnp.float32),
    )
    bias_full = lax.dynamic_update_slice_in_dim(
        jnp.zeros((3, gain_terms.shape[1]), jnp.float32), bias_terms, tp_index * columns, 1
    )
    gain_part, shift_part, bias_part = (
        lax.psum_scatter(gain_terms, ("ctx", "tp"), scatter_dimension=1, tiled=True),
        lax.psum_scatter(shift_terms, ("ctx", "tp"), scatter_dimension=1, tiled=True),
        lax.psum_scatter(bias_full, ("ctx", "tp"), scatter_dimension=1, tiled=True),
    )
    return (tuple(scattered), gain_part, shift_part, bias_part)


def stepwise_device(
    tokens_in,
    cotangent,
    plan,
    positions,
    norm_gain,
    norm_shift,
    w_qkv,
    b_qkv,
    w_out,
    w_gate_up,
    down_weight,
):
    weights = (
        norm_gain[0],
        norm_shift[0],
        w_qkv[0],
        b_qkv[0],
        w_out[0],
        w_gate_up[0],
        down_weight[0],
    )
    micro_count = tokens_in.shape[0]
    local_row_slice = tokens_in.shape[1]
    width = tokens_in.shape[3]
    columns = w_qkv.shape[3]
    ff_local = w_gate_up.shape[3]
    tp_count = lax.axis_size("tp")
    ctx_count = lax.axis_size("ctx")
    block_len = local_row_slice * tp_count
    section_index = lax.axis_index("section")
    ctx_index = lax.axis_index("ctx")
    tp_index = lax.axis_index("tp")
    block_pos = lax.dynamic_slice_in_dim(positions, ctx_index * block_len, block_len, 1)
    cosine, sine = tables(block_pos)
    allowed = (positions[:, None, :] <= block_pos[:, :, None])[:, None]
    context_rows = (cosine, sine, allowed)
    zero_rows = jnp.zeros(tokens_in.shape[1:], jnp.bfloat16)

    def forward_step(carry, step_index):
        arriving = passed_along(carry, "section", 1)
        micro = jnp.clip(step_index, 0, micro_count - 1)
        fresh = lax.dynamic_index_in_dim(tokens_in, plan[micro], 0, keepdims=False)
        layer_in = jnp.where(section_index == 0, fresh, arriving).astype(jnp.float32)
        layer_out, stored = forward_layer(layer_in, weights, context_rows)
        sent = layer_out.astype(jnp.bfloat16)
        return (sent, (sent, stored))

    steps_all = jnp.arange(micro_count + 1, dtype=jnp.int32)
    unused, (outputs, stored_all) = lax.scan(forward_step, zero_rows, steps_all)
    share = width // ctx_count
    fine_share = width // (ctx_count * tp_count)
    totals = (
        (
            jnp.zeros((3, share, columns), jnp.float32),
            jnp.zeros((columns, share), jnp.float32),
            jnp.zeros((2, share, ff_local), jnp.float32),
            jnp.zeros((ff_local, share), jnp.float32),
        ),
        jnp.zeros((2, fine_share), jnp.float32),
        jnp.zeros((2, fine_share), jnp.float32),
        jnp.zeros((3, fine_share), jnp.float32),
    )

    def backward_step(carry, bundle):
        send_back, running = carry
        step_index, stored = bundle
        arriving = passed_along(send_back, "section", -1)
        micro = step_index - section_index
        valid_step = ((micro >= 0) & (micro < micro_count)).astype(jnp.float32)
        target = lax.dynamic_index_in_dim(
            cotangent, jnp.clip(micro, 0, micro_count - 1), 0, keepdims=False
        )
        grad_out = jnp.where(section_index == 1, target, arriving).astype(jnp.float32)
        input_grad, terms = backward_layer(grad_out, stored, weights, context_rows)
        terms = jax.tree.map(lambda tensor: tensor * valid_step, terms)
        terms = spread(terms, columns, tp_index)
        running = jax.tree.map(jnp.add, running, terms)
        sent = input_grad.astype(jnp.bfloat16)
        return ((sent, running), sent)

    (unused_back, totals), input_grads = lax.scan(
        backward_step, (zero_rows, totals), (steps_all, stored_all), reverse=True
    )
    weight_parts, gain_part, shift_part, bias_part = totals
    section_ends = jnp.where(section_index == 0, input_grads[:micro_count], outputs[1:])[None]
    return (
        section_ends,
        gain_part[None],
        shift_part[None],
        bias_part[None],
        weight_parts[0][None],
        weight_parts[1][None],
        weight_parts[2][None],
        weight_parts[3][None],
    )


def per_device(*arrays):
    chips = lax.axis_size("ctx") // 2 * lax.axis_size("tp")
    if lax.axis_size("section") == 2 and lax.axis_size("ctx") == 4 and arrays[0].shape[0] == chips:
        return bulk_device(*arrays)
    return stepwise_device(*arrays)


def solution(mesh):
    placed = (
        P(None, ("ctx", "tp"), None, None),
        P(None, ("ctx", "tp"), None, None),
        P(),
        P(),
        P("section", None, None),
        P("section", None, None),
        P("section", None, None, "tp"),
        P("section", None, "tp"),
        P("section", "tp", None),
        P("section", None, None, "tp"),
        P("section", "tp", None),
    )
    return jax.shard_map(
        per_device,
        mesh=mesh,
        in_specs=placed,
        out_specs=(
            P("section", None, ("ctx", "tp"), None, None),
            P("section", None, ("ctx", "tp")),
            P("section", None, ("ctx", "tp")),
            P("section", None, ("ctx", "tp")),
            P("section", None, "ctx", "tp"),
            P("section", "tp", "ctx"),
            P("section", None, "ctx", "tp"),
            P("section", "tp", "ctx"),
        ),
        check_vma=False,
    )
```

```python
import functools

import jax
import jax.numpy as jnp
from jax import lax
from jax.experimental import pallas as pl
from jax.experimental.pallas import tpu as pltpu
from jax.sharding import PartitionSpec as P

HEAD_WIDTH = 64
ROT = 16


def pair_routes(ctx_count):
    core = [(i, i ^ 1) for i in range(ctx_count)]
    across = [(i, (i + 2) % 4) for i in range(ctx_count)]
    return core, across


def ln_stats(stream):
    mean = jnp.mean(stream, axis=-1, keepdims=True)
    centre = stream - mean
    inv_std = lax.rsqrt(jnp.mean(centre * centre, axis=-1, keepdims=True) + 1e-05)
    return centre, inv_std


def ln(stream, gain_vec, shift_vec):
    centre, inv_std = ln_stats(stream)
    return (centre * inv_std * gain_vec + shift_vec).astype(jnp.bfloat16)


def ln_back(stream, grad_in, gain_vec):
    centre, inv_std = ln_stats(stream)
    unit = centre * inv_std
    scaled = grad_in * gain_vec
    result = inv_std * (
        scaled
        - jnp.mean(scaled, axis=-1, keepdims=True)
        - unit * jnp.mean(scaled * unit, axis=-1, keepdims=True)
    )
    return result, jnp.sum(grad_in * unit, axis=0), jnp.sum(grad_in, axis=0)


def rot_tables(pos_row):
    half = ROT // 2
    freqs = 10000.0 ** (-jnp.arange(half, dtype=jnp.float32) * 2.0 / ROT)
    angles = pos_row.astype(jnp.float32)[:, None] * freqs
    cosine, sine = jnp.cos(angles), jnp.sin(angles)
    rows = pos_row.shape[0]
    rest = HEAD_WIDTH - ROT
    zeros = jnp.zeros((rows, half), jnp.float32)
    cos_head = jnp.concatenate([cosine, cosine, jnp.ones((rows, rest), jnp.float32)], 1)
    low_head = jnp.concatenate([-sine, zeros, jnp.zeros((rows, rest), jnp.float32)], 1)
    high_head = jnp.concatenate([zeros, sine, jnp.zeros((rows, rest), jnp.float32)], 1)
    return tuple(jnp.concatenate([t, t], 1) for t in (cos_head, low_head, high_head))


def dot_t(a, b):
    return lax.dot_general(a, b, (((1,), (1,)), ((), ())), preferred_element_type=jnp.float32)


def dot_0(a, b):
    return lax.dot_general(a, b, (((0,), (0,)), ((), ())), preferred_element_type=jnp.float32)


def dot_n(a, b):
    return lax.dot_general(a, b, (((1,), (0,)), ((), ())), preferred_element_type=jnp.float32)


def chunked(x, chunk):
    half = x.shape[0] // 2
    pieces = []
    for i in range(half // chunk):
        pieces.append(x[i * chunk : (i + 1) * chunk])
        pieces.append(x[half + i * chunk : half + (i + 1) * chunk])
    return jnp.concatenate(pieces, axis=0)


def attn_fwd_kernel(heads, chunk, mixed, bias, cos_t, low_t, high_t, pos_c, pos_r, qkv, out):
    rows = mixed.shape[0]
    half = rows // 2
    width = heads * HEAD_WIDTH
    half_rot = ROT // 2
    cosine, low, high = cos_t[...], low_t[...], high_t[...]
    for pair in range(heads // 2):
        parts = []
        for c in range(3):
            at = c * width + pair * 128
            x = mixed[:, at : at + 128] + bias[0, :, at : at + 128]
            if c < 2:
                x = x * cosine + pltpu.roll(x, 128 - half_rot, 1) * low + pltpu.roll(x, half_rot, 1) * high
            x = x.astype(jnp.bfloat16)
            qkv[:, at : at + 128] = x
            parts.append(chunked(x, chunk))
        query, key, value = parts
        query = query * jnp.bfloat16(HEAD_WIDTH ** (-0.5))
        for i in range(half // chunk):
            end = 2 * chunk * (i + 1)
            begin = end - 2 * chunk
            allowed = pos_r[:, begin:end] <= pos_c[begin:end, :]
            halves = []
            for h in range(2):
                lanes = slice(h * HEAD_WIDTH, (h + 1) * HEAD_WIDTH)
                q_h = query[begin:end, lanes]
                score = dot_t(q_h, key[:end, lanes])
                last = jnp.where(allowed, score[:, begin:], -1e30)
                score = last if i == 0 else jnp.concatenate([score[:, :begin], last], axis=1)
                prob = jnp.exp(score - jnp.max(score, axis=1, keepdims=True))
                total = jnp.sum(prob, axis=1, keepdims=True)
                mixed_values = dot_n(prob.astype(jnp.bfloat16), value[:end, lanes])
                halves.append(mixed_values / total)
            done = jnp.concatenate(halves, axis=1).astype(jnp.bfloat16)
            lanes = slice(pair * 128, pair * 128 + 128)
            out[i * chunk : (i + 1) * chunk, lanes] = done[:chunk]
            out[half + i * chunk : half + (i + 1) * chunk, lanes] = done[chunk:]


def attn_bwd_kernel(heads, chunk, qkv, ctx, cos_t, low_t, high_t, pos_c, pos_r, grad, bias_grad, dk_s, dv_s):
    rows = qkv.shape[0]
    half = rows // 2
    width = heads * HEAD_WIDTH
    half_rot = ROT // 2
    cosine, low, high = cos_t[...], low_t[...], high_t[...]
    scale = HEAD_WIDTH ** (-0.5)

    def finish(c, pair, x):
        at = c * width + pair * 128
        if c < 2:
            x = x * scale
            x = x * cosine + pltpu.roll(x * high, 128 - half_rot, 1) + pltpu.roll(x * low, half_rot, 1)
        x = x.astype(jnp.bfloat16)
        grad[:, at : at + 128] = x
        bias_grad[0, :, at : at + 128] = jnp.sum(x.astype(jnp.float32), axis=0, keepdims=True)

    def unchunked(x):
        steps = half // chunk
        own = [x[2 * i * chunk : (2 * i + 1) * chunk] for i in range(steps)]
        other = [x[(2 * i + 1) * chunk : (2 * i + 2) * chunk] for i in range(steps)]
        return jnp.concatenate(own + other, axis=0)

    for pair in range(heads // 2):
        lanes2 = slice(pair * 128, pair * 128 + 128)
        query, key, value = (
            chunked(qkv[:, c * width + pair * 128 : c * width + pair * 128 + 128], chunk) for c in range(3)
        )
        query_s = query * jnp.bfloat16(scale)
        ctx_grad = chunked(ctx[:, lanes2], chunk)
        dk_s[...] = jnp.zeros_like(dk_s)
        dv_s[...] = jnp.zeros_like(dv_s)
        dq_parts = []
        for i in range(half // chunk):
            end = 2 * chunk * (i + 1)
            begin = end - 2 * chunk
            allowed = pos_c[begin:end, :] <= pos_r[:, begin:end]
            dq_h, dk_h, dv_h = [], [], []
            for h in range(2):
                lanes = slice(h * HEAD_WIDTH, (h + 1) * HEAD_WIDTH)
                score = dot_t(key[:end, lanes], query_s[begin:end, lanes])
                last = jnp.where(allowed, score[begin:, :], -1e30)
                score = last if i == 0 else jnp.concatenate([score[:begin, :], last], axis=0)
                prob = jnp.exp(score - jnp.max(score, axis=0, keepdims=True))
                prob = prob * (1.0 / jnp.sum(prob, axis=0, keepdims=True))
                grad_h = ctx_grad[begin:end, lanes]
                dv_h.append(dot_n(prob.astype(jnp.bfloat16), grad_h))
                prob_grad = dot_t(value[:end, lanes], grad_h)
                delta = jnp.sum(prob * prob_grad, axis=0, keepdims=True)
                score_grad = (prob * (prob_grad - delta)).astype(jnp.bfloat16)
                dk_h.append(dot_n(score_grad, query[begin:end, lanes]))
                dq_h.append(dot_0(score_grad, key[:end, lanes]))
            dk_s[:end, :] += jnp.concatenate(dk_h, axis=1)
            dv_s[:end, :] += jnp.concatenate(dv_h, axis=1)
            dq_parts.append(jnp.concatenate(dq_h, axis=1))
        finish(0, pair, unchunked(jnp.concatenate(dq_parts, axis=0)))
        finish(1, pair, unchunked(dk_s[...]))
        finish(2, pair, unchunked(dv_s[...]))


VMEM_LIMIT = 56 * 1024 * 1024


def attn_fwd(mixed, bias, context, groups, chunk):
    rows, columns = mixed.shape
    block = columns // groups
    heads = block // (3 * HEAD_WIDTH)
    cos_t, low_t, high_t, pos_c, pos_r = context
    whole = lambda shape: pl.BlockSpec(shape, lambda g: (0, 0))
    return pl.pallas_call(
        functools.partial(attn_fwd_kernel, heads, chunk),
        grid=(groups,),
        in_specs=[
            pl.BlockSpec((rows, block), lambda g: (0, g)),
            pl.BlockSpec((1, 1, block), lambda g: (g, 0, 0)),
            whole((rows, 128)),
            whole((rows, 128)),
            whole((rows, 128)),
            whole((rows, 1)),
            whole((1, rows)),
        ],
        out_specs=[
            pl.BlockSpec((rows, block), lambda g: (0, g)),
            pl.BlockSpec((rows, block // 3), lambda g: (0, g)),
        ],
        out_shape=[
            jax.ShapeDtypeStruct((rows, columns), jnp.bfloat16),
            jax.ShapeDtypeStruct((rows, columns // 3), jnp.bfloat16),
        ],
        compiler_params=pltpu.CompilerParams(vmem_limit_bytes=VMEM_LIMIT),
        cost_estimate=pl.CostEstimate(
            flops=3 * rows * rows * columns // 3 * 4,
            bytes_accessed=rows * columns * 7,
            transcendentals=rows * rows * columns // (3 * HEAD_WIDTH),
        ),
    )(mixed, bias.reshape(groups, 1, block), cos_t, low_t, high_t, pos_c, pos_r)


def attn_bwd(qkv, ctx_grad, context, groups, chunk):
    rows, columns = qkv.shape
    block = columns // groups
    heads = block // (3 * HEAD_WIDTH)
    cos_t, low_t, high_t, pos_c, pos_r = context
    whole = lambda shape: pl.BlockSpec(shape, lambda g: (0, 0))
    return pl.pallas_call(
        functools.partial(attn_bwd_kernel, heads, chunk),
        grid=(groups,),
        in_specs=[
            pl.BlockSpec((rows, block), lambda g: (0, g)),
            pl.BlockSpec((rows, block // 3), lambda g: (0, g)),
            whole((rows, 128)),
            whole((rows, 128)),
            whole((rows, 128)),
            whole((rows, 1)),
            whole((1, rows)),
        ],
        out_specs=[
            pl.BlockSpec((rows, block), lambda g: (0, g)),
            pl.BlockSpec((1, 1, block), lambda g: (g, 0, 0)),
        ],
        out_shape=[
            jax.ShapeDtypeStruct((rows, columns), jnp.bfloat16),
            jax.ShapeDtypeStruct((groups, 1, block), jnp.float32),
        ],
        scratch_shapes=[pltpu.VMEM((rows, 128), jnp.float32), pltpu.VMEM((rows, 128), jnp.float32)],
        compiler_params=pltpu.CompilerParams(vmem_limit_bytes=VMEM_LIMIT),
        cost_estimate=pl.CostEstimate(
            flops=rows * columns,
            bytes_accessed=rows * columns,
            transcendentals=0,
        ),
    )(qkv, ctx_grad, cos_t, low_t, high_t, pos_c, pos_r)


def bulk_device(
    tokens_in,
    cotangent,
    plan,
    positions,
    norm_gain,
    norm_shift,
    w_qkv,
    b_qkv,
    w_out,
    w_gate_up,
    down_weight,
):
    tp_count = lax.axis_size("tp")
    ctx_count = lax.axis_size("ctx")
    section_index = lax.axis_index("section")
    ctx_index = lax.axis_index("ctx")
    side, core = ctx_index // 2, ctx_index % 2
    core_route, across_route = pair_routes(ctx_count)
    micro_count, slice_len, _, width = tokens_in.shape
    gain, shift = norm_gain[0], norm_shift[0]
    piece = slice_len // 2
    rows = micro_count * slice_len * 2
    own_rows = rows // 2
    half_width = width // 2
    columns = w_qkv.shape[3] // 2
    hidden = w_gate_up.shape[3] // 2
    first = section_index == 0

    ordered = jnp.stack(
        [lax.dynamic_index_in_dim(tokens_in, plan[m], 0, keepdims=False)[:, 0] for m in range(micro_count)]
    )
    fresh = jnp.where(first, ordered, cotangent[:, :, 0])
    fresh = fresh.reshape(ctx_count // 2, tp_count, 2, piece, width).transpose(0, 2, 1, 3, 4)
    fresh = fresh.reshape(ctx_count * tp_count, piece, width)
    inbound = lax.all_to_all(fresh, ("ctx", "tp"), 0, 0, tiled=True).reshape(own_rows, width)

    pos = positions.reshape(-1, 2, piece)
    pos = jnp.concatenate(
        [
            lax.dynamic_index_in_dim(pos, core, 1, False).reshape(-1),
            lax.dynamic_index_in_dim(pos, 1 - core, 1, False).reshape(-1),
        ]
    )
    chunk = min(128, own_rows)
    chunk_pos = chunked(pos, chunk)
    context = (*rot_tables(pos), chunk_pos[:, None], chunk_pos[None, :])

    tp_index = lax.axis_index("tp")

    def turned_by_tp(shards, axis=0):
        count = shards.shape[axis] // tp_count
        twice = jnp.concatenate([shards, shards], axis=axis)
        start = lax.rem(tp_count - tp_index, tp_count) * count
        return lax.dynamic_slice_in_dim(twice, start, tp_count * count, axis)

    def after(x, *others):
        return lax.optimization_barrier((x, *others))[0]

    own_parts, across_parts = [], []

    def gathered(block_of):
        block, held = block_of(side), block_of(1 - side)
        count = block.shape[0]
        step = len(own_parts)
        if step == 2:
            block = after(block, own_parts[0], across_parts[0], inbound)
        elif step > 2:
            block = after(block, own_parts[step - 2], across_parts[step - 3])
        own = lax.all_gather(block, "tp", axis=0, tiled=True)
        wanted = [
            lax.dynamic_slice_in_dim(own, lax.rem(tp_index + p, tp_count) * count, count, 0)
            for p in range(1, tp_count)
        ]
        arriving = lax.ppermute(jnp.concatenate(wanted, axis=0), "ctx", across_route)
        own_parts.append(own)
        across_parts.append(arriving)
        other = turned_by_tp(jnp.concatenate([held, arriving], axis=0))
        return jnp.where(
            side == 0, jnp.concatenate([own, other], axis=1), jnp.concatenate([other, own], axis=1)
        )

    def qkv_block(half):
        block = lax.dynamic_slice(w_qkv[0], (0, half * half_width, core * columns), (3, half_width, columns))
        return block.transpose(0, 2, 1).reshape(3 * columns, half_width)

    def out_block(half):
        return lax.dynamic_slice(w_out[0], (core * columns, half * half_width), (columns, half_width))

    def gu_block(which, half):
        block = lax.dynamic_slice(
            w_gate_up[0], (which, half * half_width, core * hidden), (1, half_width, hidden)
        )
        return block[0].T

    def down_block(part, half):
        start = core * hidden + part * (hidden // 2)
        return lax.dynamic_slice(down_weight[0], (start, half * half_width), (hidden // 2, half_width))

    wt_out = gathered(out_block)
    wt_qkv = gathered(qkv_block)
    wt_gu = jnp.concatenate([gathered(functools.partial(gu_block, w)) for w in range(2)], axis=0)
    wt_down = jnp.concatenate(
        [
            gathered(functools.partial(down_block, part)).reshape(tp_count, hidden // 2, width)
            for part in range(2)
        ],
        axis=1,
    ).reshape(tp_count * hidden, width)
    bias_own = lax.dynamic_slice_in_dim(b_qkv[0], core * columns, columns, 1).reshape(1, 3 * columns)
    bias = [bias_own]
    for p in range(1, tp_count):
        ring = [((i + p) % tp_count, i) for i in range(tp_count)]
        bias.append(lax.ppermute(bias_own, "tp", ring))
    bias = turned_by_tp(jnp.concatenate(bias, axis=0))
    ff = wt_down.shape[0]

    def both(own):
        return jnp.concatenate([own, lax.ppermute(own, "ctx", core_route)], axis=0)

    def summed(a, weight, parts=1):
        step = own_rows // parts
        spans = [slice(i * step, (i + 1) * step) for i in range(parts)]
        others = [dot_n(a[own_rows:][span], weight).astype(jnp.bfloat16) for span in spans]
        arriving = [lax.ppermute(other, "ctx", core_route) for other in others]
        own = [dot_n(a[:own_rows][span], weight) for span in spans]
        return [x + y.astype(jnp.float32) for x, y in zip(own, arriving)]

    def split(x, parts):
        step = x.shape[0] // parts
        return [x[i * step : (i + 1) * step] for i in range(parts)]

    def over_x(parts, route):
        return jnp.concatenate([lax.ppermute(part, "section", route) for part in parts], axis=0)

    def forward(stream):
        normed = both(ln(stream, gain[0], shift[0]))
        mixed = dot_t(normed, wt_qkv)
        qkv, attended = attn_fwd(mixed, bias, context, tp_count, chunk)
        hidden_state = stream + summed(attended, wt_out)[0]
        normed_two = both(ln(hidden_state, gain[1], shift[1]))
        gate_up = dot_t(normed_two, wt_gu)
        gate, up = gate_up[:, :ff], gate_up[:, ff:]
        activation = (jax.nn.silu(gate) * up).astype(jnp.bfloat16)
        out = [
            (x + y).astype(jnp.bfloat16)
            for x, y in zip(split(hidden_state, 2), summed(activation, wt_down, 2))
        ]
        return out, (stream, normed, qkv, attended, hidden_state, normed_two, gate_up, activation)

    def far_near(right):
        far = lax.dynamic_slice_in_dim(right, (1 - side) * half_width, half_width, 1)
        near = lax.dynamic_slice_in_dim(right, side * half_width, half_width, 1)
        return far, near

    def far_term(left, right):
        return dot_0(left, far_near(right)[0]).astype(jnp.bfloat16)

    def near_total(left, right, arriving, *others):
        near = far_near(right)[1]
        if others:
            near = after(near, *others)
        return (dot_0(left, near) + arriving.astype(jnp.float32)).astype(jnp.bfloat16)

    def across(term, *others):
        return lax.ppermute(after(term, *others) if others else term, "ctx", across_route)

    def over_tp(term):
        return lax.psum_scatter(term, "tp", scatter_dimension=0, tiled=True)

    together = lax.optimization_barrier

    def part_of(x, i, parts, axis):
        shard = x.shape[axis] // tp_count
        step = shard // parts
        return jnp.concatenate(
            [
                lax.slice_in_dim(x, z * shard + i * step, z * shard + (i + 1) * step, axis=axis)
                for z in range(tp_count)
            ],
            axis=axis,
        )

    def mlp_back(act_grad, gate_up):
        gate, up = gate_up[:, :ff], gate_up[:, ff:]
        sigma = jax.nn.sigmoid(gate)
        gate_grad = (act_grad * up * sigma * (1.0 + gate * (1.0 - sigma))).astype(jnp.bfloat16)
        up_grad = (act_grad * gate * sigma).astype(jnp.bfloat16)
        return gate_grad, up_grad

    def two_dot(gate_grad, up_grad):
        return dot_n(jnp.concatenate([gate_grad, up_grad], axis=1), wt_gu)

    def from_core(term):
        return lax.ppermute(term.astype(jnp.bfloat16), "ctx", core_route).astype(jnp.float32)

    def backward(grad_out, stored, wait):
        stream, normed, qkv, attended, hidden_state, normed_two, gate_up, activation = stored
        gate_grad, up_grad = mlp_back(dot_t(both(grad_out), wt_down), gate_up)
        gu_grad = jnp.concatenate([gate_grad, up_grad], axis=1)
        two_grad = summed(gu_grad, wt_gu)[0]
        hidden_grad = grad_out.astype(jnp.float32) + ln_back(hidden_state, two_grad, gain[1])[0]
        ctx_grad = dot_t(both(hidden_grad.astype(jnp.bfloat16)), wt_out).astype(jnp.bfloat16)
        qkv_grad, _ = attn_bwd(qkv, ctx_grad, context, tp_count, chunk)
        one_grad = summed(after(qkv_grad, wait), wt_qkv, 2)
        return [
            (z + ln_back(x, y, gain[0])[0]).astype(jnp.bfloat16)
            for x, y, z in zip(split(stream, 2), one_grad, split(hidden_grad, 2))
        ]

    def last_backward(grad_out, stored, final_out, act_both):
        stream, normed, qkv, attended, hidden_state, normed_two, gate_up, _ = stored
        grad_f32 = grad_out.astype(jnp.float32)
        far_grad, near_grad = far_near(grad_out)
        grad_across = across(far_grad)
        mlp_grad = both(grad_out)
        gate_grad, up_grad = mlp_back(dot_t(mlp_grad, wt_down), gate_up)
        far_gate = far_term(gate_grad, normed_two)

        grad_across, far_gate, gate_grad, up_grad = together((grad_across, far_gate, gate_grad, up_grad))
        arriving_gate = across(far_gate)
        grad_both = jnp.concatenate([both(near_grad), both(grad_across)], axis=0)
        down_total = dot_0(act_both, grad_both).astype(jnp.bfloat16)
        down_total, gate_other, up_other = together((down_total, gate_grad[own_rows:], up_grad[own_rows:]))
        sum_down = over_tp(down_total)
        arriving = from_core(two_dot(gate_other, up_other))
        two_grad = two_dot(gate_grad[:own_rows], up_grad[:own_rows]) + arriving
        far_up_a, far_up_b = (far_term(x, normed_two) for x in jnp.split(up_grad, 2, axis=1))

        arriving_gate, far_up_a, far_up_b, gate_grad, two_grad = together(
            (arriving_gate, far_up_a, far_up_b, gate_grad, two_grad)
        )
        arriving = across(far_up_a)
        gate_total = near_total(gate_grad, normed_two, arriving_gate)
        gate_total, two_grad = together((gate_total, two_grad))
        sum_gate = over_tp(gate_total)
        result, gain_two, shift_two = ln_back(hidden_state, two_grad, gain[1])
        hidden_grad = grad_f32 + result
        attn_grad = both(hidden_grad.astype(jnp.bfloat16))
        ctx_grad = dot_t(attn_grad, wt_out).astype(jnp.bfloat16)

        arriving, far_up_b, ctx_grad = together((arriving, far_up_b, ctx_grad))
        arriving_up = jnp.concatenate([arriving, across(far_up_b)], axis=0)
        qkv_grad, bias_grad = attn_bwd(qkv, ctx_grad, context, tp_count, chunk)
        far_out = far_term(attended, attn_grad)

        arriving_up, far_out, qkv_grad, up_grad, attn_grad = together(
            (arriving_up, far_out, qkv_grad, up_grad, attn_grad)
        )
        arriving_out = across(far_out)
        sum_up = over_tp(near_total(up_grad, normed_two, arriving_up))
        qkv_a, qkv_b = (part_of(qkv_grad, i, 2, 1) for i in range(2))
        far_a = far_term(qkv_a, normed)

        arriving_out, far_a, qkv_a, qkv_b, qkv_grad, attn_grad = together(
            (arriving_out, far_a, qkv_a, qkv_b, qkv_grad, attn_grad)
        )
        arriving = across(far_a)
        sum_out = over_tp(near_total(attended, attn_grad, arriving_out))
        one_grad = summed(qkv_grad, wt_qkv)[0]
        far_b = far_term(qkv_b, normed)

        arriving, far_b, one_grad, qkv_a, qkv_b = together((arriving, far_b, one_grad, qkv_a, qkv_b))
        arriving_b = across(far_b)
        sum_qkv_a = over_tp(near_total(qkv_a, normed, arriving))
        result, gain_one, shift_one = ln_back(stream, one_grad, gain[0])
        input_grad = (hidden_grad + result).astype(jnp.bfloat16)
        ends = jnp.where(first, input_grad, final_out)

        arriving_b, ends, qkv_b = together((arriving_b, ends, qkv_b))
        ends = lax.all_to_all(
            ends.reshape(ctx_count * tp_count, piece, width), ("ctx", "tp"), 0, 0, tiled=True
        )
        sum_qkv_b = over_tp(near_total(qkv_b, normed, arriving_b))
        small = (jnp.stack([gain_one, gain_two]), jnp.stack([shift_one, shift_two]), bias_grad)
        sum_qkv = jnp.concatenate([sum_qkv_a, sum_qkv_b], axis=0)

        return ends, small, (sum_down, sum_gate, sum_up, sum_out, sum_qkv)

    sent, _ = forward(inbound.astype(jnp.float32))
    arriving = over_x(sent, [(0, 1)])
    final_out, stored = forward(jnp.where(first, inbound, arriving).astype(jnp.float32))
    act_across = across(stored[7])
    arriving_back = over_x(backward(inbound, stored, act_across), [(1, 0)])
    arriving_back, final_out, act_both = together(
        (arriving_back, jnp.concatenate(final_out, axis=0), jnp.concatenate([stored[7], act_across], axis=0))
    )
    grad_out = jnp.where(first, arriving_back, inbound)
    ends, small, sums = last_backward(grad_out, stored, final_out, act_both)
    down_sum, gate_sum, up_sum, out_sum, qkv_sum = sums

    def settled(term):
        share = half_width // 2
        away = lax.dynamic_slice_in_dim(term, (1 - core) * share, share, term.ndim - 1)
        kept = lax.dynamic_slice_in_dim(term, core * share, share, term.ndim - 1)
        got = lax.ppermute(away, "ctx", core_route)
        axis = term.ndim - 2
        return jnp.where(
            core == 0, jnp.concatenate([kept, got], axis), jnp.concatenate([got, kept], axis)
        ).astype(jnp.float32)

    grad_down = settled(down_sum)
    grad_gate = settled(gate_sum)
    grad_up = settled(up_sum)
    grad_out_w = settled(out_sum)
    grad_qkv = settled(qkv_sum.reshape(3, columns, half_width))

    gain_terms, shift_terms, bias_terms = small
    bias_terms = bias_terms.reshape(tp_count, 3, columns).transpose(1, 0, 2)[:, :, None]
    bias_full = jnp.where(
        (jnp.arange(2) == core)[None, None, :, None], bias_terms, 0.0
    ).reshape(3, tp_count * 2 * columns)
    vectors = jnp.concatenate([gain_terms, shift_terms, bias_full], axis=0)
    share = width // (ctx_count * tp_count)
    vectors = after(vectors, ends).reshape(-1, ctx_count * tp_count, share).transpose(1, 0, 2)
    vectors = jnp.sum(lax.all_to_all(vectors, ("ctx", "tp"), 0, 0, tiled=True), axis=0).reshape(-1, share)

    ends = ends.reshape(ctx_count // 2, 2, tp_count, piece, width).transpose(0, 2, 1, 3, 4)
    ends = ends.reshape(micro_count, slice_len, 1, width)
    return (
        ends[None],
        vectors[None, :2],
        vectors[None, 2:4],
        vectors[None, 4:],
        grad_qkv.transpose(0, 2, 1)[None],
        grad_out_w[None],
        jnp.stack([grad_gate.T, grad_up.T])[None],
        grad_down[None],
    )


def passed_along(block, axis, distance):
    devices = range(lax.axis_size(axis))
    route = [(i - distance, i) for i in devices if i - distance in devices]
    return lax.ppermute(block, axis, route)


def normalize(stream, gain_vec, shift_vec):
    centre = stream - jnp.mean(stream, axis=-1, keepdims=True)
    spread = jnp.mean(centre * centre, axis=-1, keepdims=True)
    return centre * lax.rsqrt(spread + 1e-05) * gain_vec + shift_vec


def norm_back(stream, grad_in, gain_vec):
    centre = stream - jnp.mean(stream, axis=-1, keepdims=True)
    inv_std = lax.rsqrt(jnp.mean(centre * centre, axis=-1, keepdims=True) + 1e-05)
    unit = centre * inv_std
    scaled = grad_in * gain_vec
    result = inv_std * (
        scaled
        - jnp.mean(scaled, axis=-1, keepdims=True)
        - unit * jnp.mean(scaled * unit, axis=-1, keepdims=True)
    )
    return (result, jnp.sum(grad_in * unit, axis=(0, 1)), jnp.sum(grad_in, axis=(0, 1)))


def rotary(tensor, cosine, sine):
    half_rot = ROT // 2
    front = tensor[..., :ROT]
    turned = jnp.concatenate([-front[..., half_rot:], front[..., :half_rot]], axis=-1)
    return jnp.concatenate([front * cosine + turned * sine, tensor[..., ROT:]], axis=-1)


def unrotary(tensor, cosine, sine):
    half_rot = ROT // 2
    front = tensor[..., :ROT]
    turned = jnp.concatenate([-front[..., half_rot:], front[..., :half_rot]], axis=-1)
    return jnp.concatenate([front * cosine - turned * sine, tensor[..., ROT:]], axis=-1)


def tables(position_rows):
    freqs = 10000.0 ** (-jnp.arange(ROT // 2, dtype=jnp.float32) * 2.0 / ROT)
    angles = position_rows.T.astype(jnp.float32)[:, :, None] * freqs
    angles = jnp.concatenate([angles, angles], axis=-1)[:, :, None, :]
    return (jnp.cos(angles), jnp.sin(angles))


def attention_scores(queries, key_heads, allowed):
    scores = jnp.einsum(
        "qshe,kshe->shqk", queries, key_heads, preferred_element_type=jnp.float32
    ) * HEAD_WIDTH ** (-0.5)
    return jnp.where(allowed, scores, -1e30)


def forward_layer(layer_in, weights, context_rows):
    gain_vec, shift_vec, w_qkv, b_qkv, w_out, w_gate_up, down_weight = weights
    cosine, sine, allowed = context_rows
    normed = normalize(layer_in, gain_vec[0], shift_vec[0]).astype(jnp.bfloat16)
    normed_all = lax.all_gather(normed, "tp", axis=0, tiled=True)
    block_len, seq_count, width = normed_all.shape
    columns = w_qkv.shape[2]
    head_count = columns // HEAD_WIDTH
    mixed = (
        jnp.einsum("rsd,cde->crse", normed_all, w_qkv, preferred_element_type=jnp.float32)
        + b_qkv[:, None, None, :]
    )
    queries = rotary(
        mixed[0].reshape(block_len, seq_count, head_count, HEAD_WIDTH), cosine, sine
    ).astype(jnp.bfloat16)
    key_own = rotary(
        mixed[1].reshape(block_len, seq_count, head_count, HEAD_WIDTH), cosine, sine
    ).astype(jnp.bfloat16)
    key_own = key_own.reshape(block_len, seq_count, columns)
    value_own = mixed[2].astype(jnp.bfloat16)
    key_all, value_all = (
        lax.all_gather(key_own, "ctx", axis=0, tiled=True),
        lax.all_gather(value_own, "ctx", axis=0, tiled=True),
    )
    key_heads = key_all.reshape(key_all.shape[0], seq_count, head_count, HEAD_WIDTH)
    value_heads = value_all.reshape(value_all.shape[0], seq_count, head_count, HEAD_WIDTH)
    scores = attention_scores(queries, key_heads, allowed)
    top_score = jnp.max(scores, axis=-1, keepdims=True)
    log_total = top_score + jnp.log(jnp.sum(jnp.exp(scores - top_score), axis=-1, keepdims=True))
    probability = jnp.exp(scores - log_total)
    attended = jnp.einsum(
        "shqk,kshe->qshe",
        probability.astype(jnp.bfloat16),
        value_heads,
        preferred_element_type=jnp.float32,
    )
    attended = attended.astype(jnp.bfloat16).reshape(block_len, seq_count, columns)
    piece = attended
    hidden_state = layer_in + lax.psum_scatter(
        jnp.einsum("rse,ed->rsd", piece, w_out, preferred_element_type=jnp.float32).astype(
            jnp.bfloat16
        ),
        "tp",
        scatter_dimension=0,
        tiled=True,
    ).astype(jnp.float32)
    normed_two = normalize(hidden_state, gain_vec[1], shift_vec[1]).astype(jnp.bfloat16)
    normed_two_all = lax.all_gather(normed_two, "tp", axis=0, tiled=True)
    gate_up = jnp.einsum(
        "rsd,cdf->crsf", normed_two_all, w_gate_up, preferred_element_type=jnp.float32
    )
    gated_activation = (jax.nn.silu(gate_up[0]) * gate_up[1]).astype(jnp.bfloat16)
    piece = gated_activation
    layer_out = hidden_state + lax.psum_scatter(
        jnp.einsum("rsf,fd->rsd", piece, down_weight, preferred_element_type=jnp.float32).astype(
            jnp.bfloat16
        ),
        "tp",
        scatter_dimension=0,
        tiled=True,
    ).astype(jnp.float32)
    stored = (
        layer_in,
        normed_all,
        queries,
        key_all,
        value_all,
        log_total,
        attended,
        hidden_state,
        normed_two_all,
        gate_up,
    )
    return (layer_out, stored)


def backward_layer(grad_out, stored, weights, context_rows):
    gain_vec, shift_vec, w_qkv, b_qkv, w_out, w_gate_up, down_weight = weights
    cosine, sine, allowed = context_rows
    (
        layer_in,
        normed_all,
        queries,
        key_all,
        value_all,
        log_total,
        attended,
        hidden_state,
        normed_two_all,
        gate_up,
    ) = stored
    block_len, seq_count, columns = attended.shape
    head_count = columns // HEAD_WIDTH
    mlp_grad = lax.all_gather(grad_out.astype(jnp.bfloat16), "tp", axis=0, tiled=True)
    gate_part = gate_up[0]
    up_part = gate_up[1]
    sigma = jax.nn.sigmoid(gate_part)
    swish = gate_part * sigma
    gated_activation = (swish * up_part).astype(jnp.bfloat16)
    down_grad = jnp.einsum(
        "rsf,rsd->fd", gated_activation, mlp_grad, preferred_element_type=jnp.float32
    )
    act_grad = jnp.einsum("rsd,fd->rsf", mlp_grad, down_weight, preferred_element_type=jnp.float32)
    gate_up_grad = jnp.stack(
        [act_grad * up_part * sigma * (1.0 + gate_part * (1.0 - sigma)), act_grad * swish]
    ).astype(jnp.bfloat16)
    gu_grad = jnp.einsum(
        "rsd,crsf->cdf", normed_two_all, gate_up_grad, preferred_element_type=jnp.float32
    )
    piece = gate_up_grad
    two_grad = lax.psum_scatter(
        jnp.einsum("crsf,cdf->rsd", piece, w_gate_up, preferred_element_type=jnp.float32).astype(
            jnp.bfloat16
        ),
        "tp",
        scatter_dimension=0,
        tiled=True,
    ).astype(jnp.float32)
    hidden_grad, gain_two, shift_two = norm_back(hidden_state, two_grad, gain_vec[1])
    hidden_grad = grad_out + hidden_grad
    attn_grad = lax.all_gather(hidden_grad.astype(jnp.bfloat16), "tp", axis=0, tiled=True)
    out_grad = jnp.einsum("rse,rsd->ed", attended, attn_grad, preferred_element_type=jnp.float32)
    ctx_grad = jnp.einsum("rsd,ed->rse", attn_grad, w_out, preferred_element_type=jnp.float32)
    ctx_grad = ctx_grad.astype(jnp.bfloat16).reshape(block_len, seq_count, head_count, HEAD_WIDTH)
    key_heads = key_all.reshape(key_all.shape[0], seq_count, head_count, HEAD_WIDTH)
    value_heads = value_all.reshape(value_all.shape[0], seq_count, head_count, HEAD_WIDTH)
    scores = attention_scores(queries, key_heads, allowed)
    probability = jnp.exp(scores - log_total)
    value_grad = jnp.einsum(
        "shqk,qshe->kshe",
        probability.astype(jnp.bfloat16),
        ctx_grad,
        preferred_element_type=jnp.float32,
    )
    prob_grad = jnp.einsum(
        "qshe,kshe->shqk", ctx_grad, value_heads, preferred_element_type=jnp.float32
    )
    score_grad = probability * (
        prob_grad - jnp.sum(probability * prob_grad, axis=-1, keepdims=True)
    )
    score_grad = score_grad.astype(jnp.bfloat16)
    query_grad = jnp.einsum(
        "shqk,kshe->qshe", score_grad, key_heads, preferred_element_type=jnp.float32
    ) * HEAD_WIDTH ** (-0.5)
    key_grad = jnp.einsum(
        "shqk,qshe->kshe", score_grad, queries, preferred_element_type=jnp.float32
    ) * HEAD_WIDTH ** (-0.5)
    key_back, value_back = (
        lax.psum_scatter(
            key_grad.astype(jnp.bfloat16), "ctx", scatter_dimension=0, tiled=True
        ).astype(jnp.float32),
        lax.psum_scatter(
            value_grad.astype(jnp.bfloat16), "ctx", scatter_dimension=0, tiled=True
        ).astype(jnp.float32),
    )
    qkv_grad = jnp.stack(
        [
            unrotary(query_grad, cosine, sine).reshape(block_len, seq_count, columns),
            unrotary(key_back, cosine, sine).reshape(block_len, seq_count, columns),
            value_back.reshape(block_len, seq_count, columns),
        ]
    ).astype(jnp.bfloat16)
    bias_grad = jnp.sum(qkv_grad.astype(jnp.float32), axis=(1, 2))
    qkv_weight_grad = jnp.einsum(
        "rsd,crse->cde", normed_all, qkv_grad, preferred_element_type=jnp.float32
    )
    piece = qkv_grad
    one_grad = lax.psum_scatter(
        jnp.einsum("crse,cde->rsd", piece, w_qkv, preferred_element_type=jnp.float32).astype(
            jnp.bfloat16
        ),
        "tp",
        scatter_dimension=0,
        tiled=True,
    ).astype(jnp.float32)
    input_grad, gain_one, shift_one = norm_back(layer_in, one_grad, gain_vec[0])
    input_grad = hidden_grad + input_grad
    weight_terms = (qkv_weight_grad, out_grad, gu_grad, down_grad)
    return (
        input_grad,
        (
            weight_terms,
            jnp.stack([gain_one, gain_two]),
            jnp.stack([shift_one, shift_two]),
            bias_grad,
        ),
    )


def spread(terms, columns, tp_index):
    weight_terms, gain_terms, shift_terms, bias_terms = terms
    qkv_term, out_term, gu_term, down_term = weight_terms
    scattered = (
        lax.psum_scatter(
            qkv_term.astype(jnp.bfloat16), "ctx", scatter_dimension=1, tiled=True
        ).astype(jnp.float32),
        lax.psum_scatter(
            out_term.astype(jnp.bfloat16), "ctx", scatter_dimension=1, tiled=True
        ).astype(jnp.float32),
        lax.psum_scatter(
            gu_term.astype(jnp.bfloat16), "ctx", scatter_dimension=1, tiled=True
        ).astype(jnp.float32),
        lax.psum_scatter(
            down_term.astype(jnp.bfloat16), "ctx", scatter_dimension=1, tiled=True
        ).astype(jnp.float32),
    )
    bias_full = lax.dynamic_update_slice_in_dim(
        jnp.zeros((3, gain_terms.shape[1]), jnp.float32), bias_terms, tp_index * columns, 1
    )
    gain_part, shift_part, bias_part = (
        lax.psum_scatter(gain_terms, ("ctx", "tp"), scatter_dimension=1, tiled=True),
        lax.psum_scatter(shift_terms, ("ctx", "tp"), scatter_dimension=1, tiled=True),
        lax.psum_scatter(bias_full, ("ctx", "tp"), scatter_dimension=1, tiled=True),
    )
    return (tuple(scattered), gain_part, shift_part, bias_part)


def stepwise_device(
    tokens_in,
    cotangent,
    plan,
    positions,
    norm_gain,
    norm_shift,
    w_qkv,
    b_qkv,
    w_out,
    w_gate_up,
    down_weight,
):
    weights = (
        norm_gain[0],
        norm_shift[0],
        w_qkv[0],
        b_qkv[0],
        w_out[0],
        w_gate_up[0],
        down_weight[0],
    )
    micro_count = tokens_in.shape[0]
    local_row_slice = tokens_in.shape[1]
    width = tokens_in.shape[3]
    columns = w_qkv.shape[3]
    ff_local = w_gate_up.shape[3]
    tp_count = lax.axis_size("tp")
    ctx_count = lax.axis_size("ctx")
    block_len = local_row_slice * tp_count
    section_index = lax.axis_index("section")
    ctx_index = lax.axis_index("ctx")
    tp_index = lax.axis_index("tp")
    block_pos = lax.dynamic_slice_in_dim(positions, ctx_index * block_len, block_len, 1)
    cosine, sine = tables(block_pos)
    allowed = (positions[:, None, :] <= block_pos[:, :, None])[:, None]
    context_rows = (cosine, sine, allowed)
    zero_rows = jnp.zeros(tokens_in.shape[1:], jnp.bfloat16)

    def forward_step(carry, step_index):
        arriving = passed_along(carry, "section", 1)
        micro = jnp.clip(step_index, 0, micro_count - 1)
        fresh = lax.dynamic_index_in_dim(tokens_in, plan[micro], 0, keepdims=False)
        layer_in = jnp.where(section_index == 0, fresh, arriving).astype(jnp.float32)
        layer_out, stored = forward_layer(layer_in, weights, context_rows)
        sent = layer_out.astype(jnp.bfloat16)
        return (sent, (sent, stored))

    steps_all = jnp.arange(micro_count + 1, dtype=jnp.int32)
    unused, (outputs, stored_all) = lax.scan(forward_step, zero_rows, steps_all)
    share = width // ctx_count
    fine_share = width // (ctx_count * tp_count)
    totals = (
        (
            jnp.zeros((3, share, columns), jnp.float32),
            jnp.zeros((columns, share), jnp.float32),
            jnp.zeros((2, share, ff_local), jnp.float32),
            jnp.zeros((ff_local, share), jnp.float32),
        ),
        jnp.zeros((2, fine_share), jnp.float32),
        jnp.zeros((2, fine_share), jnp.float32),
        jnp.zeros((3, fine_share), jnp.float32),
    )

    def backward_step(carry, bundle):
        send_back, running = carry
        step_index, stored = bundle
        arriving = passed_along(send_back, "section", -1)
        micro = step_index - section_index
        valid_step = ((micro >= 0) & (micro < micro_count)).astype(jnp.float32)
        target = lax.dynamic_index_in_dim(
            cotangent, jnp.clip(micro, 0, micro_count - 1), 0, keepdims=False
        )
        grad_out = jnp.where(section_index == 1, target, arriving).astype(jnp.float32)
        input_grad, terms = backward_layer(grad_out, stored, weights, context_rows)
        terms = jax.tree.map(lambda tensor: tensor * valid_step, terms)
        terms = spread(terms, columns, tp_index)
        running = jax.tree.map(jnp.add, running, terms)
        sent = input_grad.astype(jnp.bfloat16)
        return ((sent, running), sent)

    (unused_back, totals), input_grads = lax.scan(
        backward_step, (zero_rows, totals), (steps_all, stored_all), reverse=True
    )
    weight_parts, gain_part, shift_part, bias_part = totals
    section_ends = jnp.where(section_index == 0, input_grads[:micro_count], outputs[1:])[None]
    return (
        section_ends,
        gain_part[None],
        shift_part[None],
        bias_part[None],
        weight_parts[0][None],
        weight_parts[1][None],
        weight_parts[2][None],
        weight_parts[3][None],
    )


def per_device(*arrays):
    chips = lax.axis_size("ctx") // 2 * lax.axis_size("tp")
    if lax.axis_size("section") == 2 and lax.axis_size("ctx") == 4 and arrays[0].shape[0] == chips:
        return bulk_device(*arrays)
    return stepwise_device(*arrays)


def solution(mesh):
    placed = (
        P(None, ("ctx", "tp"), None, None),
        P(None, ("ctx", "tp"), None, None),
        P(),
        P(),
        P("section", None, None),
        P("section", None, None),
        P("section", None, None, "tp"),
        P("section", None, "tp"),
        P("section", "tp", None),
        P("section", None, None, "tp"),
        P("section", "tp", None),
    )
    return jax.shard_map(
        per_device,
        mesh=mesh,
        in_specs=placed,
        out_specs=(
            P("section", None, ("ctx", "tp"), None, None),
            P("section", None, ("ctx", "tp")),
            P("section", None, ("ctx", "tp")),
            P("section", None, ("ctx", "tp")),
            P("section", None, "ctx", "tp"),
            P("section", "tp", "ctx"),
            P("section", None, "ctx", "tp"),
            P("section", "tp", "ctx"),
        ),
        check_vma=False,
    )
```

```python
import functools

import jax
import jax.numpy as jnp
from jax import lax
from jax.experimental import pallas as pl
from jax.experimental.pallas import tpu as pltpu
from jax.sharding import PartitionSpec as P

HEAD_WIDTH = 64
ROT = 16


def pair_routes(ctx_count):
    core = [(i, i ^ 1) for i in range(ctx_count)]
    across = [(i, (i + 2) % 4) for i in range(ctx_count)]
    return core, across


def ln_stats(stream):
    mean = jnp.mean(stream, axis=-1, keepdims=True)
    centre = stream - mean
    inv_std = lax.rsqrt(jnp.mean(centre * centre, axis=-1, keepdims=True) + 1e-05)
    return centre, inv_std


def ln(stream, gain_vec, shift_vec):
    centre, inv_std = ln_stats(stream)
    return (centre * inv_std * gain_vec + shift_vec).astype(jnp.bfloat16)


def ln_back(stream, grad_in, gain_vec):
    centre, inv_std = ln_stats(stream)
    unit = centre * inv_std
    scaled = grad_in * gain_vec
    result = inv_std * (
        scaled
        - jnp.mean(scaled, axis=-1, keepdims=True)
        - unit * jnp.mean(scaled * unit, axis=-1, keepdims=True)
    )
    return result, jnp.sum(grad_in * unit, axis=0), jnp.sum(grad_in, axis=0)


def rot_tables(pos_row):
    half = ROT // 2
    freqs = 10000.0 ** (-jnp.arange(half, dtype=jnp.float32) * 2.0 / ROT)
    angles = pos_row.astype(jnp.float32)[:, None] * freqs
    cosine, sine = jnp.cos(angles), jnp.sin(angles)
    rows = pos_row.shape[0]
    rest = HEAD_WIDTH - ROT
    zeros = jnp.zeros((rows, half), jnp.float32)
    cos_head = jnp.concatenate([cosine, cosine, jnp.ones((rows, rest), jnp.float32)], 1)
    low_head = jnp.concatenate([-sine, zeros, jnp.zeros((rows, rest), jnp.float32)], 1)
    high_head = jnp.concatenate([zeros, sine, jnp.zeros((rows, rest), jnp.float32)], 1)
    return tuple(jnp.concatenate([t, t], 1) for t in (cos_head, low_head, high_head))


def dot_t(a, b):
    return lax.dot_general(a, b, (((1,), (1,)), ((), ())), preferred_element_type=jnp.float32)


def dot_0(a, b):
    return lax.dot_general(a, b, (((0,), (0,)), ((), ())), preferred_element_type=jnp.float32)


def dot_n(a, b):
    return lax.dot_general(a, b, (((1,), (0,)), ((), ())), preferred_element_type=jnp.float32)


def chunked(x, chunk):
    half = x.shape[0] // 2
    pieces = []
    for i in range(half // chunk):
        pieces.append(x[i * chunk : (i + 1) * chunk])
        pieces.append(x[half + i * chunk : half + (i + 1) * chunk])
    return jnp.concatenate(pieces, axis=0)


def attn_fwd_kernel(heads, chunk, mixed, bias, cos_t, low_t, high_t, pos_c, pos_r, qkv, out):
    rows = mixed.shape[0]
    half = rows // 2
    width = heads * HEAD_WIDTH
    half_rot = ROT // 2
    cosine, low, high = cos_t[...], low_t[...], high_t[...]
    for pair in range(heads // 2):
        parts = []
        for c in range(3):
            at = c * width + pair * 128
            x = mixed[:, at : at + 128] + bias[0, :, at : at + 128]
            if c < 2:
                x = x * cosine + pltpu.roll(x, 128 - half_rot, 1) * low + pltpu.roll(x, half_rot, 1) * high
            x = x.astype(jnp.bfloat16)
            qkv[:, at : at + 128] = x
            parts.append(chunked(x, chunk))
        query, key, value = parts
        query = query * jnp.bfloat16(HEAD_WIDTH ** (-0.5))
        for i in range(half // chunk):
            end = 2 * chunk * (i + 1)
            begin = end - 2 * chunk
            allowed = pos_r[:, begin:end] <= pos_c[begin:end, :]
            halves = []
            for h in range(2):
                lanes = slice(h * HEAD_WIDTH, (h + 1) * HEAD_WIDTH)
                q_h = query[begin:end, lanes]
                score = dot_t(q_h, key[:end, lanes])
                last = jnp.where(allowed, score[:, begin:], -1e30)
                score = last if i == 0 else jnp.concatenate([score[:, :begin], last], axis=1)
                prob = jnp.exp(score - jnp.max(score, axis=1, keepdims=True))
                total = jnp.sum(prob, axis=1, keepdims=True)
                mixed_values = dot_n(prob.astype(jnp.bfloat16), value[:end, lanes])
                halves.append(mixed_values / total)
            done = jnp.concatenate(halves, axis=1).astype(jnp.bfloat16)
            lanes = slice(pair * 128, pair * 128 + 128)
            out[i * chunk : (i + 1) * chunk, lanes] = done[:chunk]
            out[half + i * chunk : half + (i + 1) * chunk, lanes] = done[chunk:]


def attn_bwd_kernel(heads, chunk, qkv, ctx, cos_t, low_t, high_t, pos_c, pos_r, grad, bias_grad, dk_s, dv_s):
    rows = qkv.shape[0]
    half = rows // 2
    width = heads * HEAD_WIDTH
    half_rot = ROT // 2
    cosine, low, high = cos_t[...], low_t[...], high_t[...]
    scale = HEAD_WIDTH ** (-0.5)

    def finish(c, pair, x):
        at = c * width + pair * 128
        if c < 2:
            x = x * scale
            x = x * cosine + pltpu.roll(x * high, 128 - half_rot, 1) + pltpu.roll(x * low, half_rot, 1)
        x = x.astype(jnp.bfloat16)
        grad[:, at : at + 128] = x
        bias_grad[0, :, at : at + 128] = jnp.sum(x.astype(jnp.float32), axis=0, keepdims=True)

    def unchunked(x):
        steps = half // chunk
        own = [x[2 * i * chunk : (2 * i + 1) * chunk] for i in range(steps)]
        other = [x[(2 * i + 1) * chunk : (2 * i + 2) * chunk] for i in range(steps)]
        return jnp.concatenate(own + other, axis=0)

    for pair in range(heads // 2):
        lanes2 = slice(pair * 128, pair * 128 + 128)
        query, key, value = (
            chunked(qkv[:, c * width + pair * 128 : c * width + pair * 128 + 128], chunk) for c in range(3)
        )
        query_s = query * jnp.bfloat16(scale)
        ctx_grad = chunked(ctx[:, lanes2], chunk)
        dk_s[...] = jnp.zeros_like(dk_s)
        dv_s[...] = jnp.zeros_like(dv_s)
        dq_parts = []
        for i in range(half // chunk):
            end = 2 * chunk * (i + 1)
            begin = end - 2 * chunk
            allowed = pos_c[begin:end, :] <= pos_r[:, begin:end]
            dq_h, dk_h, dv_h = [], [], []
            for h in range(2):
                lanes = slice(h * HEAD_WIDTH, (h + 1) * HEAD_WIDTH)
                score = dot_t(key[:end, lanes], query_s[begin:end, lanes])
                last = jnp.where(allowed, score[begin:, :], -1e30)
                score = last if i == 0 else jnp.concatenate([score[:begin, :], last], axis=0)
                prob = jnp.exp(score - jnp.max(score, axis=0, keepdims=True))
                prob = prob * (1.0 / jnp.sum(prob, axis=0, keepdims=True))
                grad_h = ctx_grad[begin:end, lanes]
                dv_h.append(dot_n(prob.astype(jnp.bfloat16), grad_h))
                prob_grad = dot_t(value[:end, lanes], grad_h)
                delta = jnp.sum(prob * prob_grad, axis=0, keepdims=True)
                score_grad = (prob * (prob_grad - delta)).astype(jnp.bfloat16)
                dk_h.append(dot_n(score_grad, query[begin:end, lanes]))
                dq_h.append(dot_0(score_grad, key[:end, lanes]))
            dk_s[:end, :] += jnp.concatenate(dk_h, axis=1)
            dv_s[:end, :] += jnp.concatenate(dv_h, axis=1)
            dq_parts.append(jnp.concatenate(dq_h, axis=1))
        finish(0, pair, unchunked(jnp.concatenate(dq_parts, axis=0)))
        finish(1, pair, unchunked(dk_s[...]))
        finish(2, pair, unchunked(dv_s[...]))


VMEM_LIMIT = 56 * 1024 * 1024


def attn_fwd(mixed, bias, context, groups, chunk):
    rows, columns = mixed.shape
    block = columns // groups
    heads = block // (3 * HEAD_WIDTH)
    cos_t, low_t, high_t, pos_c, pos_r = context
    whole = lambda shape: pl.BlockSpec(shape, lambda g: (0, 0))
    return pl.pallas_call(
        functools.partial(attn_fwd_kernel, heads, chunk),
        grid=(groups,),
        in_specs=[
            pl.BlockSpec((rows, block), lambda g: (0, g)),
            pl.BlockSpec((1, 1, block), lambda g: (g, 0, 0)),
            whole((rows, 128)),
            whole((rows, 128)),
            whole((rows, 128)),
            whole((rows, 1)),
            whole((1, rows)),
        ],
        out_specs=[
            pl.BlockSpec((rows, block), lambda g: (0, g)),
            pl.BlockSpec((rows, block // 3), lambda g: (0, g)),
        ],
        out_shape=[
            jax.ShapeDtypeStruct((rows, columns), jnp.bfloat16),
            jax.ShapeDtypeStruct((rows, columns // 3), jnp.bfloat16),
        ],
        compiler_params=pltpu.CompilerParams(vmem_limit_bytes=VMEM_LIMIT),
        cost_estimate=pl.CostEstimate(
            flops=3 * rows * rows * columns // 3 * 4,
            bytes_accessed=rows * columns * 7,
            transcendentals=rows * rows * columns // (3 * HEAD_WIDTH),
        ),
    )(mixed, bias.reshape(groups, 1, block), cos_t, low_t, high_t, pos_c, pos_r)


def attn_bwd(qkv, ctx_grad, context, groups, chunk):
    rows, columns = qkv.shape
    block = columns // groups
    heads = block // (3 * HEAD_WIDTH)
    cos_t, low_t, high_t, pos_c, pos_r = context
    whole = lambda shape: pl.BlockSpec(shape, lambda g: (0, 0))
    return pl.pallas_call(
        functools.partial(attn_bwd_kernel, heads, chunk),
        grid=(groups,),
        in_specs=[
            pl.BlockSpec((rows, block), lambda g: (0, g)),
            pl.BlockSpec((rows, block // 3), lambda g: (0, g)),
            whole((rows, 128)),
            whole((rows, 128)),
            whole((rows, 128)),
            whole((rows, 1)),
            whole((1, rows)),
        ],
        out_specs=[
            pl.BlockSpec((rows, block), lambda g: (0, g)),
            pl.BlockSpec((1, 1, block), lambda g: (g, 0, 0)),
        ],
        out_shape=[
            jax.ShapeDtypeStruct((rows, columns), jnp.bfloat16),
            jax.ShapeDtypeStruct((groups, 1, block), jnp.float32),
        ],
        scratch_shapes=[pltpu.VMEM((rows, 128), jnp.float32), pltpu.VMEM((rows, 128), jnp.float32)],
        compiler_params=pltpu.CompilerParams(vmem_limit_bytes=VMEM_LIMIT),
        cost_estimate=pl.CostEstimate(
            flops=rows * columns,
            bytes_accessed=rows * columns,
            transcendentals=0,
        ),
    )(qkv, ctx_grad, cos_t, low_t, high_t, pos_c, pos_r)


def bulk_device(
    tokens_in,
    cotangent,
    plan,
    positions,
    norm_gain,
    norm_shift,
    w_qkv,
    b_qkv,
    w_out,
    w_gate_up,
    down_weight,
):
    tp_count = lax.axis_size("tp")
    ctx_count = lax.axis_size("ctx")
    section_index = lax.axis_index("section")
    ctx_index = lax.axis_index("ctx")
    side, core = ctx_index // 2, ctx_index % 2
    core_route, across_route = pair_routes(ctx_count)
    micro_count, slice_len, _, width = tokens_in.shape
    gain, shift = norm_gain[0], norm_shift[0]
    piece = slice_len // 2
    rows = micro_count * slice_len * 2
    own_rows = rows // 2
    half_width = width // 2
    columns = w_qkv.shape[3] // 2
    hidden = w_gate_up.shape[3] // 2
    first = section_index == 0

    ordered = jnp.stack(
        [lax.dynamic_index_in_dim(tokens_in, plan[m], 0, keepdims=False)[:, 0] for m in range(micro_count)]
    )
    fresh = jnp.where(first, ordered, cotangent[:, :, 0])
    fresh = fresh.reshape(ctx_count // 2, tp_count, 2, piece, width).transpose(0, 2, 1, 3, 4)
    fresh = fresh.reshape(ctx_count * tp_count, piece, width)
    inbound = lax.all_to_all(fresh, ("ctx", "tp"), 0, 0, tiled=True).reshape(own_rows, width)

    pos = positions.reshape(-1, 2, piece)
    pos = jnp.concatenate(
        [
            lax.dynamic_index_in_dim(pos, core, 1, False).reshape(-1),
            lax.dynamic_index_in_dim(pos, 1 - core, 1, False).reshape(-1),
        ]
    )
    chunk = min(128, own_rows)
    chunk_pos = chunked(pos, chunk)
    context = (*rot_tables(pos), chunk_pos[:, None], chunk_pos[None, :])

    tp_index = lax.axis_index("tp")

    def turned_by_tp(shards, axis=0):
        count = shards.shape[axis] // tp_count
        twice = jnp.concatenate([shards, shards], axis=axis)
        start = lax.rem(tp_count - tp_index, tp_count) * count
        return lax.dynamic_slice_in_dim(twice, start, tp_count * count, axis)

    def after(x, *others):
        return lax.optimization_barrier((x, *others))[0]

    own_parts, across_parts = [], []

    def gathered(block_of):
        block, held = block_of(side), block_of(1 - side)
        count = block.shape[0]
        step = len(own_parts)
        if step == 2:
            block = after(block, own_parts[0], across_parts[0], inbound)
        elif step > 2:
            block = after(block, own_parts[step - 2], across_parts[step - 3])
        own = lax.all_gather(block, "tp", axis=0, tiled=True)
        wanted = [
            lax.dynamic_slice_in_dim(own, lax.rem(tp_index + p, tp_count) * count, count, 0)
            for p in range(1, tp_count)
        ]
        arriving = lax.ppermute(jnp.concatenate(wanted, axis=0), "ctx", across_route)
        own_parts.append(own)
        across_parts.append(arriving)
        other = turned_by_tp(jnp.concatenate([held, arriving], axis=0))
        return jnp.where(
            side == 0, jnp.concatenate([own, other], axis=1), jnp.concatenate([other, own], axis=1)
        )

    def qkv_block(half):
        block = lax.dynamic_slice(w_qkv[0], (0, half * half_width, core * columns), (3, half_width, columns))
        return block.transpose(0, 2, 1).reshape(3 * columns, half_width)

    def out_block(half):
        return lax.dynamic_slice(w_out[0], (core * columns, half * half_width), (columns, half_width))

    def gu_block(which, half):
        block = lax.dynamic_slice(
            w_gate_up[0], (which, half * half_width, core * hidden), (1, half_width, hidden)
        )
        return block[0].T

    def down_block(part, half):
        start = core * hidden + part * (hidden // 2)
        return lax.dynamic_slice(down_weight[0], (start, half * half_width), (hidden // 2, half_width))

    wt_out = gathered(out_block)
    wt_qkv = gathered(qkv_block)
    wt_gu = jnp.concatenate([gathered(functools.partial(gu_block, w)) for w in range(2)], axis=0)
    wt_down = jnp.concatenate(
        [
            gathered(functools.partial(down_block, part)).reshape(tp_count, hidden // 2, width)
            for part in range(2)
        ],
        axis=1,
    ).reshape(tp_count * hidden, width)
    bias_own = lax.dynamic_slice_in_dim(b_qkv[0], core * columns, columns, 1).reshape(1, 3 * columns)
    bias = [bias_own]
    for p in range(1, tp_count):
        ring = [((i + p) % tp_count, i) for i in range(tp_count)]
        bias.append(lax.ppermute(bias_own, "tp", ring))
    bias = turned_by_tp(jnp.concatenate(bias, axis=0))
    ff = wt_down.shape[0]

    def both(own):
        return jnp.concatenate([own, lax.ppermute(own, "ctx", core_route)], axis=0)

    def summed(a, weight, parts=1):
        step = own_rows // parts
        spans = [slice(i * step, (i + 1) * step) for i in range(parts)]
        others = [dot_n(a[own_rows:][span], weight).astype(jnp.bfloat16) for span in spans]
        arriving = [lax.ppermute(other, "ctx", core_route) for other in others]
        own = [dot_n(a[:own_rows][span], weight) for span in spans]
        return [x + y.astype(jnp.float32) for x, y in zip(own, arriving)]

    def split(x, parts):
        step = x.shape[0] // parts
        return [x[i * step : (i + 1) * step] for i in range(parts)]

    def over_x(parts, route):
        return jnp.concatenate([lax.ppermute(part, "section", route) for part in parts], axis=0)

    def forward(stream, parts):
        normed = both(ln(stream, gain[0], shift[0]))
        mixed = dot_t(normed, wt_qkv)
        qkv, attended = attn_fwd(mixed, bias, context, tp_count, chunk)
        hidden_state = stream + summed(attended, wt_out)[0]
        normed_two = both(ln(hidden_state, gain[1], shift[1]))
        gate_up = dot_t(normed_two, wt_gu)
        gate, up = gate_up[:, :ff], gate_up[:, ff:]
        activation = (jax.nn.silu(gate) * up).astype(jnp.bfloat16)
        out = [
            (x + y).astype(jnp.bfloat16)
            for x, y in zip(split(hidden_state, parts), summed(activation, wt_down, parts))
        ]
        return out, (stream, normed, qkv, attended, hidden_state, normed_two, gate_up, activation)

    def far_near(right):
        far = lax.dynamic_slice_in_dim(right, (1 - side) * half_width, half_width, 1)
        near = lax.dynamic_slice_in_dim(right, side * half_width, half_width, 1)
        return far, near

    def far_term(left, right):
        return dot_0(left, far_near(right)[0]).astype(jnp.bfloat16)

    def near_total(left, right, arriving, *others):
        near = far_near(right)[1]
        if others:
            near = after(near, *others)
        return (dot_0(left, near) + arriving.astype(jnp.float32)).astype(jnp.bfloat16)

    def across(term, *others):
        return lax.ppermute(after(term, *others) if others else term, "ctx", across_route)

    def over_tp(term):
        return lax.psum_scatter(term, "tp", scatter_dimension=0, tiled=True)

    together = lax.optimization_barrier

    def part_of(x, i, parts, axis):
        shard = x.shape[axis] // tp_count
        step = shard // parts
        return jnp.concatenate(
            [
                lax.slice_in_dim(x, z * shard + i * step, z * shard + (i + 1) * step, axis=axis)
                for z in range(tp_count)
            ],
            axis=axis,
        )

    def mlp_back(act_grad, gate_up):
        gate, up = gate_up[:, :ff], gate_up[:, ff:]
        sigma = jax.nn.sigmoid(gate)
        gate_grad = (act_grad * up * sigma * (1.0 + gate * (1.0 - sigma))).astype(jnp.bfloat16)
        up_grad = (act_grad * gate * sigma).astype(jnp.bfloat16)
        return gate_grad, up_grad

    def two_dot(gate_grad, up_grad):
        return dot_n(jnp.concatenate([gate_grad, up_grad], axis=1), wt_gu)

    def from_core(term):
        return lax.ppermute(term.astype(jnp.bfloat16), "ctx", core_route).astype(jnp.float32)

    def backward(grad_out, stored, wait):
        stream, normed, qkv, attended, hidden_state, normed_two, gate_up, activation = stored
        gate_grad, up_grad = mlp_back(dot_t(both(grad_out), wt_down), gate_up)
        gu_grad = jnp.concatenate([gate_grad, up_grad], axis=1)
        two_grad = summed(gu_grad, wt_gu)[0]
        hidden_grad = grad_out.astype(jnp.float32) + ln_back(hidden_state, two_grad, gain[1])[0]
        ctx_grad = dot_t(both(hidden_grad.astype(jnp.bfloat16)), wt_out).astype(jnp.bfloat16)
        qkv_grad, _ = attn_bwd(qkv, ctx_grad, context, tp_count, chunk)
        one_grad = summed(after(qkv_grad, wait), wt_qkv)[0]
        return (hidden_grad + ln_back(stream, one_grad, gain[0])[0]).astype(jnp.bfloat16)

    def settled(term):
        share = half_width // 2
        away = lax.dynamic_slice_in_dim(term, (1 - core) * share, share, term.ndim - 1)
        kept = lax.dynamic_slice_in_dim(term, core * share, share, term.ndim - 1)
        got = lax.ppermute(away, "ctx", core_route)
        axis = term.ndim - 2
        return jnp.where(
            core == 0, jnp.concatenate([kept, got], axis), jnp.concatenate([got, kept], axis)
        ).astype(jnp.float32)

    def vector_sums(small):
        gain_terms, shift_terms, bias_terms = small
        bias_terms = bias_terms.reshape(tp_count, 3, columns).transpose(1, 0, 2)[:, :, None]
        bias_full = jnp.where(
            (jnp.arange(2) == core)[None, None, :, None], bias_terms, 0.0
        ).reshape(3, tp_count * 2 * columns)
        vectors = jnp.concatenate([gain_terms, shift_terms, bias_full], axis=0)
        share = width // (ctx_count * tp_count)
        vectors = vectors.reshape(-1, ctx_count * tp_count, share).transpose(1, 0, 2)
        return jnp.sum(lax.all_to_all(vectors, ("ctx", "tp"), 0, 0, tiled=True), axis=0).reshape(-1, share)

    def last_backward(grad_out, stored, final_out, act_both):
        stream, normed, qkv, attended, hidden_state, normed_two, gate_up, _ = stored
        grad_f32 = grad_out.astype(jnp.float32)
        far_grad, near_grad = far_near(grad_out)
        grad_across = across(far_grad)
        mlp_grad = both(grad_out)
        gate_grad, up_grad = mlp_back(dot_t(mlp_grad, wt_down), gate_up)
        far_gate = far_term(gate_grad, normed_two)

        grad_across, far_gate, gate_grad, up_grad = together((grad_across, far_gate, gate_grad, up_grad))
        far_gate_a, far_gate_b = split(far_gate, 2)
        arriving = across(far_gate_a)
        gu_grad = jnp.concatenate([gate_grad, up_grad], axis=1)
        grad_both = jnp.concatenate([both(near_grad), both(grad_across)], axis=0)
        down_total = dot_0(act_both, grad_both).astype(jnp.bfloat16)
        two_other = dot_n(gu_grad[own_rows:], wt_gu).astype(jnp.bfloat16)

        arriving, far_gate_b, two_other, gu_grad, down_total, gate_grad, up_grad = together(
            (arriving, far_gate_b, two_other, gu_grad, down_total, gate_grad, up_grad)
        )
        arriving_gate = jnp.concatenate([arriving, across(far_gate_b)], axis=0)
        sum_down = over_tp(down_total)
        two_grad = dot_n(gu_grad[:own_rows], wt_gu) + lax.ppermute(two_other, "ctx", core_route).astype(jnp.float32)
        result, gain_two, shift_two = ln_back(hidden_state, two_grad, gain[1])
        hidden_grad = grad_f32 + result
        attn_grad = both(hidden_grad.astype(jnp.bfloat16))
        far_up_a, far_up_b = (far_term(x, normed_two) for x in jnp.split(up_grad, 2, axis=1))

        arriving_gate, far_up_a, far_up_b, gate_grad, attn_grad, hidden_grad = together(
            (arriving_gate, far_up_a, far_up_b, gate_grad, attn_grad, hidden_grad)
        )
        arriving = across(far_up_a)
        sum_gate = over_tp(near_total(gate_grad, normed_two, arriving_gate))
        far_up_b = jnp.concatenate([far_up_b, far_term(attended, attn_grad)], axis=0)
        ctx_grad = dot_t(attn_grad, wt_out).astype(jnp.bfloat16)

        arriving, far_up_b, ctx_grad = together((arriving, far_up_b, ctx_grad))
        arriving_b = across(far_up_b)
        arriving_up = jnp.concatenate([arriving, arriving_b[: ff // 2]], axis=0)
        arriving_out = arriving_b[ff // 2 :]
        qkv_grad, bias_grad = attn_bwd(qkv, ctx_grad, context, tp_count, chunk)
        qkv_a, qkv_b = (part_of(qkv_grad, i, 2, 1) for i in range(2))
        far_a, far_b = far_term(qkv_a, normed), far_term(qkv_b, normed)

        arriving_up, arriving_out, far_a, far_b, qkv_a, qkv_b, qkv_grad, up_grad, attn_grad = together(
            (arriving_up, arriving_out, far_a, far_b, qkv_a, qkv_b, qkv_grad, up_grad, attn_grad)
        )
        arriving = across(far_a)
        sum_up = over_tp(near_total(up_grad, normed_two, arriving_up))
        out_total = near_total(attended, attn_grad, arriving_out)
        one_other = dot_n(qkv_grad[own_rows:], wt_qkv).astype(jnp.bfloat16)

        arriving, far_b, one_other, qkv_grad, qkv_a, qkv_b, out_total = together(
            (arriving, far_b, one_other, qkv_grad, qkv_a, qkv_b, out_total)
        )
        arriving_b = across(far_b)
        sum_out = over_tp(out_total)
        sum_qkv_a = over_tp(near_total(qkv_a, normed, arriving))
        one_grad = dot_n(qkv_grad[:own_rows], wt_qkv) + lax.ppermute(one_other, "ctx", core_route).astype(jnp.float32)
        result, gain_one, shift_one = ln_back(stream, one_grad, gain[0])
        input_grad = (hidden_grad + result).astype(jnp.bfloat16)
        ends = jnp.where(first, input_grad, final_out)
        small = vector_sums((jnp.stack([gain_one, gain_two]), jnp.stack([shift_one, shift_two]), bias_grad))
        done = (settled(sum_down), jnp.stack([settled(sum_gate).T, settled(sum_up).T]))

        arriving_b, ends, qkv_b, small, done = together((arriving_b, ends, qkv_b, small, done))
        ends = lax.all_to_all(
            ends.reshape(ctx_count * tp_count, piece, width), ("ctx", "tp"), 0, 0, tiled=True
        )
        sum_qkv_b = over_tp(near_total(qkv_b, normed, arriving_b))
        sum_qkv = jnp.concatenate([sum_qkv_a, sum_qkv_b], axis=0)
        grads = (*done, settled(sum_out), settled(sum_qkv.reshape(3, columns, half_width)))
        return ends, small, grads

    sent, _ = forward(inbound.astype(jnp.float32), 2)
    arriving = over_x(sent, [(0, 1)])
    final_out, stored = forward(jnp.where(first, inbound, arriving).astype(jnp.float32), 1)
    act_across = across(stored[7])
    arriving_back = over_x([backward(inbound, stored, act_across)], [(1, 0)])
    arriving_back, final_out, act_both = together(
        (arriving_back, final_out[0], jnp.concatenate([stored[7], act_across], axis=0))
    )
    grad_out = jnp.where(first, arriving_back, inbound)
    ends, vectors, grads = last_backward(grad_out, stored, final_out, act_both)
    grad_down, grad_gu, grad_out_w, grad_qkv = grads

    ends = ends.reshape(ctx_count // 2, 2, tp_count, piece, width).transpose(0, 2, 1, 3, 4)
    ends = ends.reshape(micro_count, slice_len, 1, width)
    return (
        ends[None],
        vectors[None, :2],
        vectors[None, 2:4],
        vectors[None, 4:],
        grad_qkv.transpose(0, 2, 1)[None],
        grad_out_w[None],
        grad_gu[None],
        grad_down[None],
    )


def passed_along(block, axis, distance):
    devices = range(lax.axis_size(axis))
    route = [(i - distance, i) for i in devices if i - distance in devices]
    return lax.ppermute(block, axis, route)


def normalize(stream, gain_vec, shift_vec):
    centre = stream - jnp.mean(stream, axis=-1, keepdims=True)
    spread = jnp.mean(centre * centre, axis=-1, keepdims=True)
    return centre * lax.rsqrt(spread + 1e-05) * gain_vec + shift_vec


def norm_back(stream, grad_in, gain_vec):
    centre = stream - jnp.mean(stream, axis=-1, keepdims=True)
    inv_std = lax.rsqrt(jnp.mean(centre * centre, axis=-1, keepdims=True) + 1e-05)
    unit = centre * inv_std
    scaled = grad_in * gain_vec
    result = inv_std * (
        scaled
        - jnp.mean(scaled, axis=-1, keepdims=True)
        - unit * jnp.mean(scaled * unit, axis=-1, keepdims=True)
    )
    return (result, jnp.sum(grad_in * unit, axis=(0, 1)), jnp.sum(grad_in, axis=(0, 1)))


def rotary(tensor, cosine, sine):
    half_rot = ROT // 2
    front = tensor[..., :ROT]
    turned = jnp.concatenate([-front[..., half_rot:], front[..., :half_rot]], axis=-1)
    return jnp.concatenate([front * cosine + turned * sine, tensor[..., ROT:]], axis=-1)


def unrotary(tensor, cosine, sine):
    half_rot = ROT // 2
    front = tensor[..., :ROT]
    turned = jnp.concatenate([-front[..., half_rot:], front[..., :half_rot]], axis=-1)
    return jnp.concatenate([front * cosine - turned * sine, tensor[..., ROT:]], axis=-1)


def tables(position_rows):
    freqs = 10000.0 ** (-jnp.arange(ROT // 2, dtype=jnp.float32) * 2.0 / ROT)
    angles = position_rows.T.astype(jnp.float32)[:, :, None] * freqs
    angles = jnp.concatenate([angles, angles], axis=-1)[:, :, None, :]
    return (jnp.cos(angles), jnp.sin(angles))


def attention_scores(queries, key_heads, allowed):
    scores = jnp.einsum(
        "qshe,kshe->shqk", queries, key_heads, preferred_element_type=jnp.float32
    ) * HEAD_WIDTH ** (-0.5)
    return jnp.where(allowed, scores, -1e30)


def forward_layer(layer_in, weights, context_rows):
    gain_vec, shift_vec, w_qkv, b_qkv, w_out, w_gate_up, down_weight = weights
    cosine, sine, allowed = context_rows
    normed = normalize(layer_in, gain_vec[0], shift_vec[0]).astype(jnp.bfloat16)
    normed_all = lax.all_gather(normed, "tp", axis=0, tiled=True)
    block_len, seq_count, width = normed_all.shape
    columns = w_qkv.shape[2]
    head_count = columns // HEAD_WIDTH
    mixed = (
        jnp.einsum("rsd,cde->crse", normed_all, w_qkv, preferred_element_type=jnp.float32)
        + b_qkv[:, None, None, :]
    )
    queries = rotary(
        mixed[0].reshape(block_len, seq_count, head_count, HEAD_WIDTH), cosine, sine
    ).astype(jnp.bfloat16)
    key_own = rotary(
        mixed[1].reshape(block_len, seq_count, head_count, HEAD_WIDTH), cosine, sine
    ).astype(jnp.bfloat16)
    key_own = key_own.reshape(block_len, seq_count, columns)
    value_own = mixed[2].astype(jnp.bfloat16)
    key_all, value_all = (
        lax.all_gather(key_own, "ctx", axis=0, tiled=True),
        lax.all_gather(value_own, "ctx", axis=0, tiled=True),
    )
    key_heads = key_all.reshape(key_all.shape[0], seq_count, head_count, HEAD_WIDTH)
    value_heads = value_all.reshape(value_all.shape[0], seq_count, head_count, HEAD_WIDTH)
    scores = attention_scores(queries, key_heads, allowed)
    top_score = jnp.max(scores, axis=-1, keepdims=True)
    log_total = top_score + jnp.log(jnp.sum(jnp.exp(scores - top_score), axis=-1, keepdims=True))
    probability = jnp.exp(scores - log_total)
    attended = jnp.einsum(
        "shqk,kshe->qshe",
        probability.astype(jnp.bfloat16),
        value_heads,
        preferred_element_type=jnp.float32,
    )
    attended = attended.astype(jnp.bfloat16).reshape(block_len, seq_count, columns)
    piece = attended
    hidden_state = layer_in + lax.psum_scatter(
        jnp.einsum("rse,ed->rsd", piece, w_out, preferred_element_type=jnp.float32).astype(
            jnp.bfloat16
        ),
        "tp",
        scatter_dimension=0,
        tiled=True,
    ).astype(jnp.float32)
    normed_two = normalize(hidden_state, gain_vec[1], shift_vec[1]).astype(jnp.bfloat16)
    normed_two_all = lax.all_gather(normed_two, "tp", axis=0, tiled=True)
    gate_up = jnp.einsum(
        "rsd,cdf->crsf", normed_two_all, w_gate_up, preferred_element_type=jnp.float32
    )
    gated_activation = (jax.nn.silu(gate_up[0]) * gate_up[1]).astype(jnp.bfloat16)
    piece = gated_activation
    layer_out = hidden_state + lax.psum_scatter(
        jnp.einsum("rsf,fd->rsd", piece, down_weight, preferred_element_type=jnp.float32).astype(
            jnp.bfloat16
        ),
        "tp",
        scatter_dimension=0,
        tiled=True,
    ).astype(jnp.float32)
    stored = (
        layer_in,
        normed_all,
        queries,
        key_all,
        value_all,
        log_total,
        attended,
        hidden_state,
        normed_two_all,
        gate_up,
    )
    return (layer_out, stored)


def backward_layer(grad_out, stored, weights, context_rows):
    gain_vec, shift_vec, w_qkv, b_qkv, w_out, w_gate_up, down_weight = weights
    cosine, sine, allowed = context_rows
    (
        layer_in,
        normed_all,
        queries,
        key_all,
        value_all,
        log_total,
        attended,
        hidden_state,
        normed_two_all,
        gate_up,
    ) = stored
    block_len, seq_count, columns = attended.shape
    head_count = columns // HEAD_WIDTH
    mlp_grad = lax.all_gather(grad_out.astype(jnp.bfloat16), "tp", axis=0, tiled=True)
    gate_part = gate_up[0]
    up_part = gate_up[1]
    sigma = jax.nn.sigmoid(gate_part)
    swish = gate_part * sigma
    gated_activation = (swish * up_part).astype(jnp.bfloat16)
    down_grad = jnp.einsum(
        "rsf,rsd->fd", gated_activation, mlp_grad, preferred_element_type=jnp.float32
    )
    act_grad = jnp.einsum("rsd,fd->rsf", mlp_grad, down_weight, preferred_element_type=jnp.float32)
    gate_up_grad = jnp.stack(
        [act_grad * up_part * sigma * (1.0 + gate_part * (1.0 - sigma)), act_grad * swish]
    ).astype(jnp.bfloat16)
    gu_grad = jnp.einsum(
        "rsd,crsf->cdf", normed_two_all, gate_up_grad, preferred_element_type=jnp.float32
    )
    piece = gate_up_grad
    two_grad = lax.psum_scatter(
        jnp.einsum("crsf,cdf->rsd", piece, w_gate_up, preferred_element_type=jnp.float32).astype(
            jnp.bfloat16
        ),
        "tp",
        scatter_dimension=0,
        tiled=True,
    ).astype(jnp.float32)
    hidden_grad, gain_two, shift_two = norm_back(hidden_state, two_grad, gain_vec[1])
    hidden_grad = grad_out + hidden_grad
    attn_grad = lax.all_gather(hidden_grad.astype(jnp.bfloat16), "tp", axis=0, tiled=True)
    out_grad = jnp.einsum("rse,rsd->ed", attended, attn_grad, preferred_element_type=jnp.float32)
    ctx_grad = jnp.einsum("rsd,ed->rse", attn_grad, w_out, preferred_element_type=jnp.float32)
    ctx_grad = ctx_grad.astype(jnp.bfloat16).reshape(block_len, seq_count, head_count, HEAD_WIDTH)
    key_heads = key_all.reshape(key_all.shape[0], seq_count, head_count, HEAD_WIDTH)
    value_heads = value_all.reshape(value_all.shape[0], seq_count, head_count, HEAD_WIDTH)
    scores = attention_scores(queries, key_heads, allowed)
    probability = jnp.exp(scores - log_total)
    value_grad = jnp.einsum(
        "shqk,qshe->kshe",
        probability.astype(jnp.bfloat16),
        ctx_grad,
        preferred_element_type=jnp.float32,
    )
    prob_grad = jnp.einsum(
        "qshe,kshe->shqk", ctx_grad, value_heads, preferred_element_type=jnp.float32
    )
    score_grad = probability * (
        prob_grad - jnp.sum(probability * prob_grad, axis=-1, keepdims=True)
    )
    score_grad = score_grad.astype(jnp.bfloat16)
    query_grad = jnp.einsum(
        "shqk,kshe->qshe", score_grad, key_heads, preferred_element_type=jnp.float32
    ) * HEAD_WIDTH ** (-0.5)
    key_grad = jnp.einsum(
        "shqk,qshe->kshe", score_grad, queries, preferred_element_type=jnp.float32
    ) * HEAD_WIDTH ** (-0.5)
    key_back, value_back = (
        lax.psum_scatter(
            key_grad.astype(jnp.bfloat16), "ctx", scatter_dimension=0, tiled=True
        ).astype(jnp.float32),
        lax.psum_scatter(
            value_grad.astype(jnp.bfloat16), "ctx", scatter_dimension=0, tiled=True
        ).astype(jnp.float32),
    )
    qkv_grad = jnp.stack(
        [
            unrotary(query_grad, cosine, sine).reshape(block_len, seq_count, columns),
            unrotary(key_back, cosine, sine).reshape(block_len, seq_count, columns),
            value_back.reshape(block_len, seq_count, columns),
        ]
    ).astype(jnp.bfloat16)
    bias_grad = jnp.sum(qkv_grad.astype(jnp.float32), axis=(1, 2))
    qkv_weight_grad = jnp.einsum(
        "rsd,crse->cde", normed_all, qkv_grad, preferred_element_type=jnp.float32
    )
    piece = qkv_grad
    one_grad = lax.psum_scatter(
        jnp.einsum("crse,cde->rsd", piece, w_qkv, preferred_element_type=jnp.float32).astype(
            jnp.bfloat16
        ),
        "tp",
        scatter_dimension=0,
        tiled=True,
    ).astype(jnp.float32)
    input_grad, gain_one, shift_one = norm_back(layer_in, one_grad, gain_vec[0])
    input_grad = hidden_grad + input_grad
    weight_terms = (qkv_weight_grad, out_grad, gu_grad, down_grad)
    return (
        input_grad,
        (
            weight_terms,
            jnp.stack([gain_one, gain_two]),
            jnp.stack([shift_one, shift_two]),
            bias_grad,
        ),
    )


def spread(terms, columns, tp_index):
    weight_terms, gain_terms, shift_terms, bias_terms = terms
    qkv_term, out_term, gu_term, down_term = weight_terms
    scattered = (
        lax.psum_scatter(
            qkv_term.astype(jnp.bfloat16), "ctx", scatter_dimension=1, tiled=True
        ).astype(jnp.float32),
        lax.psum_scatter(
            out_term.astype(jnp.bfloat16), "ctx", scatter_dimension=1, tiled=True
        ).astype(jnp.float32),
        lax.psum_scatter(
            gu_term.astype(jnp.bfloat16), "ctx", scatter_dimension=1, tiled=True
        ).astype(jnp.float32),
        lax.psum_scatter(
            down_term.astype(jnp.bfloat16), "ctx", scatter_dimension=1, tiled=True
        ).astype(jnp.float32),
    )
    bias_full = lax.dynamic_update_slice_in_dim(
        jnp.zeros((3, gain_terms.shape[1]), jnp.float32), bias_terms, tp_index * columns, 1
    )
    gain_part, shift_part, bias_part = (
        lax.psum_scatter(gain_terms, ("ctx", "tp"), scatter_dimension=1, tiled=True),
        lax.psum_scatter(shift_terms, ("ctx", "tp"), scatter_dimension=1, tiled=True),
        lax.psum_scatter(bias_full, ("ctx", "tp"), scatter_dimension=1, tiled=True),
    )
    return (tuple(scattered), gain_part, shift_part, bias_part)


def stepwise_device(
    tokens_in,
    cotangent,
    plan,
    positions,
    norm_gain,
    norm_shift,
    w_qkv,
    b_qkv,
    w_out,
    w_gate_up,
    down_weight,
):
    weights = (
        norm_gain[0],
        norm_shift[0],
        w_qkv[0],
        b_qkv[0],
        w_out[0],
        w_gate_up[0],
        down_weight[0],
    )
    micro_count = tokens_in.shape[0]
    local_row_slice = tokens_in.shape[1]
    width = tokens_in.shape[3]
    columns = w_qkv.shape[3]
    ff_local = w_gate_up.shape[3]
    tp_count = lax.axis_size("tp")
    ctx_count = lax.axis_size("ctx")
    block_len = local_row_slice * tp_count
    section_index = lax.axis_index("section")
    ctx_index = lax.axis_index("ctx")
    tp_index = lax.axis_index("tp")
    block_pos = lax.dynamic_slice_in_dim(positions, ctx_index * block_len, block_len, 1)
    cosine, sine = tables(block_pos)
    allowed = (positions[:, None, :] <= block_pos[:, :, None])[:, None]
    context_rows = (cosine, sine, allowed)
    zero_rows = jnp.zeros(tokens_in.shape[1:], jnp.bfloat16)

    def forward_step(carry, step_index):
        arriving = passed_along(carry, "section", 1)
        micro = jnp.clip(step_index, 0, micro_count - 1)
        fresh = lax.dynamic_index_in_dim(tokens_in, plan[micro], 0, keepdims=False)
        layer_in = jnp.where(section_index == 0, fresh, arriving).astype(jnp.float32)
        layer_out, stored = forward_layer(layer_in, weights, context_rows)
        sent = layer_out.astype(jnp.bfloat16)
        return (sent, (sent, stored))

    steps_all = jnp.arange(micro_count + 1, dtype=jnp.int32)
    unused, (outputs, stored_all) = lax.scan(forward_step, zero_rows, steps_all)
    share = width // ctx_count
    fine_share = width // (ctx_count * tp_count)
    totals = (
        (
            jnp.zeros((3, share, columns), jnp.float32),
            jnp.zeros((columns, share), jnp.float32),
            jnp.zeros((2, share, ff_local), jnp.float32),
            jnp.zeros((ff_local, share), jnp.float32),
        ),
        jnp.zeros((2, fine_share), jnp.float32),
        jnp.zeros((2, fine_share), jnp.float32),
        jnp.zeros((3, fine_share), jnp.float32),
    )

    def backward_step(carry, bundle):
        send_back, running = carry
        step_index, stored = bundle
        arriving = passed_along(send_back, "section", -1)
        micro = step_index - section_index
        valid_step = ((micro >= 0) & (micro < micro_count)).astype(jnp.float32)
        target = lax.dynamic_index_in_dim(
            cotangent, jnp.clip(micro, 0, micro_count - 1), 0, keepdims=False
        )
        grad_out = jnp.where(section_index == 1, target, arriving).astype(jnp.float32)
        input_grad, terms = backward_layer(grad_out, stored, weights, context_rows)
        terms = jax.tree.map(lambda tensor: tensor * valid_step, terms)
        terms = spread(terms, columns, tp_index)
        running = jax.tree.map(jnp.add, running, terms)
        sent = input_grad.astype(jnp.bfloat16)
        return ((sent, running), sent)

    (unused_back, totals), input_grads = lax.scan(
        backward_step, (zero_rows, totals), (steps_all, stored_all), reverse=True
    )
    weight_parts, gain_part, shift_part, bias_part = totals
    section_ends = jnp.where(section_index == 0, input_grads[:micro_count], outputs[1:])[None]
    return (
        section_ends,
        gain_part[None],
        shift_part[None],
        bias_part[None],
        weight_parts[0][None],
        weight_parts[1][None],
        weight_parts[2][None],
        weight_parts[3][None],
    )


def per_device(*arrays):
    chips = lax.axis_size("ctx") // 2 * lax.axis_size("tp")
    if lax.axis_size("section") == 2 and lax.axis_size("ctx") == 4 and arrays[0].shape[0] == chips:
        return bulk_device(*arrays)
    return stepwise_device(*arrays)


def solution(mesh):
    placed = (
        P(None, ("ctx", "tp"), None, None),
        P(None, ("ctx", "tp"), None, None),
        P(),
        P(),
        P("section", None, None),
        P("section", None, None),
        P("section", None, None, "tp"),
        P("section", None, "tp"),
        P("section", "tp", None),
        P("section", None, None, "tp"),
        P("section", "tp", None),
    )
    return jax.shard_map(
        per_device,
        mesh=mesh,
        in_specs=placed,
        out_specs=(
            P("section", None, ("ctx", "tp"), None, None),
            P("section", None, ("ctx", "tp")),
            P("section", None, ("ctx", "tp")),
            P("section", None, ("ctx", "tp")),
            P("section", None, "ctx", "tp"),
            P("section", "tp", "ctx"),
            P("section", None, "ctx", "tp"),
            P("section", "tp", "ctx"),
        ),
        check_vma=False,
    )
```

```python
import functools

import jax
import jax.numpy as jnp
from jax import lax
from jax.experimental import pallas as pl
from jax.experimental.pallas import tpu as pltpu
from jax.sharding import PartitionSpec as P

HEAD_WIDTH = 64
ROT = 16


def pair_routes(ctx_count):
    core = [(i, i ^ 1) for i in range(ctx_count)]
    across = [(i, (i + 2) % 4) for i in range(ctx_count)]
    return core, across


def ln_stats(stream):
    mean = jnp.mean(stream, axis=-1, keepdims=True)
    centre = stream - mean
    inv_std = lax.rsqrt(jnp.mean(centre * centre, axis=-1, keepdims=True) + 1e-05)
    return centre, inv_std


def ln(stream, gain_vec, shift_vec):
    centre, inv_std = ln_stats(stream)
    return (centre * inv_std * gain_vec + shift_vec).astype(jnp.bfloat16)


def ln_back(stream, grad_in, gain_vec):
    centre, inv_std = ln_stats(stream)
    unit = centre * inv_std
    scaled = grad_in * gain_vec
    result = inv_std * (
        scaled
        - jnp.mean(scaled, axis=-1, keepdims=True)
        - unit * jnp.mean(scaled * unit, axis=-1, keepdims=True)
    )
    return result, jnp.sum(grad_in * unit, axis=0), jnp.sum(grad_in, axis=0)


def rot_tables(pos_row):
    half = ROT // 2
    freqs = 10000.0 ** (-jnp.arange(half, dtype=jnp.float32) * 2.0 / ROT)
    angles = pos_row.astype(jnp.float32)[:, None] * freqs
    cosine, sine = jnp.cos(angles), jnp.sin(angles)
    rows = pos_row.shape[0]
    rest = HEAD_WIDTH - ROT
    zeros = jnp.zeros((rows, half), jnp.float32)
    cos_head = jnp.concatenate([cosine, cosine, jnp.ones((rows, rest), jnp.float32)], 1)
    low_head = jnp.concatenate([-sine, zeros, jnp.zeros((rows, rest), jnp.float32)], 1)
    high_head = jnp.concatenate([zeros, sine, jnp.zeros((rows, rest), jnp.float32)], 1)
    return tuple(jnp.concatenate([t, t], 1) for t in (cos_head, low_head, high_head))


def dot_t(a, b):
    return lax.dot_general(a, b, (((1,), (1,)), ((), ())), preferred_element_type=jnp.float32)


def dot_0(a, b):
    return lax.dot_general(a, b, (((0,), (0,)), ((), ())), preferred_element_type=jnp.float32)


def dot_n(a, b):
    return lax.dot_general(a, b, (((1,), (0,)), ((), ())), preferred_element_type=jnp.float32)


def chunked(x, chunk):
    half = x.shape[0] // 2
    pieces = []
    for i in range(half // chunk):
        pieces.append(x[i * chunk : (i + 1) * chunk])
        pieces.append(x[half + i * chunk : half + (i + 1) * chunk])
    return jnp.concatenate(pieces, axis=0)


def attn_fwd_kernel(heads, chunk, mixed, bias, cos_t, low_t, high_t, pos_c, pos_r, qkv, out, lse):
    rows = mixed.shape[0]
    half = rows // 2
    width = heads * HEAD_WIDTH
    half_rot = ROT // 2
    cosine, low, high = cos_t[...], low_t[...], high_t[...]
    for pair in range(heads // 2):
        parts = []
        for c in range(3):
            at = c * width + pair * 128
            x = mixed[:, at : at + 128] + bias[0, :, at : at + 128]
            if c < 2:
                x = x * cosine + pltpu.roll(x, 128 - half_rot, 1) * low + pltpu.roll(x, half_rot, 1) * high
            x = x.astype(jnp.bfloat16)
            qkv[:, at : at + 128] = x
            parts.append(chunked(x, chunk))
        query, key, value = parts
        query = query * jnp.bfloat16(HEAD_WIDTH ** (-0.5))
        for i in range(half // chunk):
            end = 2 * chunk * (i + 1)
            begin = end - 2 * chunk
            allowed = pos_r[:, begin:end] <= pos_c[begin:end, :]
            halves = []
            for h in range(2):
                lanes = slice(h * HEAD_WIDTH, (h + 1) * HEAD_WIDTH)
                q_h = query[begin:end, lanes]
                score = dot_t(q_h, key[:end, lanes])
                last = jnp.where(allowed, score[:, begin:], -1e30)
                score = last if i == 0 else jnp.concatenate([score[:, :begin], last], axis=1)
                top = jnp.max(score, axis=1, keepdims=True)
                prob = jnp.exp(score - top)
                total = jnp.sum(prob, axis=1, keepdims=True)
                lse[0, begin:end, 2 * pair + h : 2 * pair + h + 1] = top + jnp.log(total)
                mixed_values = dot_n(prob.astype(jnp.bfloat16), value[:end, lanes])
                halves.append(mixed_values / total)
            done = jnp.concatenate(halves, axis=1).astype(jnp.bfloat16)
            lanes = slice(pair * 128, pair * 128 + 128)
            out[i * chunk : (i + 1) * chunk, lanes] = done[:chunk]
            out[half + i * chunk : half + (i + 1) * chunk, lanes] = done[chunk:]


def attn_bwd_kernel(heads, chunk, qkv, lse, ctx, cos_t, low_t, high_t, pos_c, pos_r, grad, bias_grad, dk_s, dv_s):
    rows = qkv.shape[0]
    half = rows // 2
    width = heads * HEAD_WIDTH
    half_rot = ROT // 2
    cosine, low, high = cos_t[...], low_t[...], high_t[...]
    scale = HEAD_WIDTH ** (-0.5)

    def finish(c, pair, x):
        at = c * width + pair * 128
        if c < 2:
            x = x * scale
            x = x * cosine + pltpu.roll(x * high, 128 - half_rot, 1) + pltpu.roll(x * low, half_rot, 1)
        x = x.astype(jnp.bfloat16)
        grad[:, at : at + 128] = x
        bias_grad[0, :, at : at + 128] = jnp.sum(x.astype(jnp.float32), axis=0, keepdims=True)

    def unchunked(x):
        steps = half // chunk
        own = [x[2 * i * chunk : (2 * i + 1) * chunk] for i in range(steps)]
        other = [x[(2 * i + 1) * chunk : (2 * i + 2) * chunk] for i in range(steps)]
        return jnp.concatenate(own + other, axis=0)

    for pair in range(heads // 2):
        lanes2 = slice(pair * 128, pair * 128 + 128)
        query, key, value = (
            chunked(qkv[:, c * width + pair * 128 : c * width + pair * 128 + 128], chunk) for c in range(3)
        )
        query_s = query * jnp.bfloat16(scale)
        ctx_grad = chunked(ctx[:, lanes2], chunk)
        dk_s[...] = jnp.zeros_like(dk_s)
        dv_s[...] = jnp.zeros_like(dv_s)
        dq_parts = []
        for i in range(half // chunk):
            end = 2 * chunk * (i + 1)
            begin = end - 2 * chunk
            allowed = pos_c[begin:end, :] <= pos_r[:, begin:end]
            dq_h, dk_h, dv_h = [], [], []
            for h in range(2):
                lanes = slice(h * HEAD_WIDTH, (h + 1) * HEAD_WIDTH)
                score = dot_t(key[:end, lanes], query_s[begin:end, lanes])
                last = jnp.where(allowed, score[begin:, :], -1e30)
                score = last if i == 0 else jnp.concatenate([score[:begin, :], last], axis=0)
                prob = jnp.exp(score - lse[0, 2 * pair + h : 2 * pair + h + 1, begin:end])
                grad_h = ctx_grad[begin:end, lanes]
                dv_h.append(dot_n(prob.astype(jnp.bfloat16), grad_h))
                prob_grad = dot_t(value[:end, lanes], grad_h)
                delta = jnp.sum(prob * prob_grad, axis=0, keepdims=True)
                score_grad = (prob * (prob_grad - delta)).astype(jnp.bfloat16)
                dk_h.append(dot_n(score_grad, query[begin:end, lanes]))
                dq_h.append(dot_0(score_grad, key[:end, lanes]))
            dk_s[:end, :] += jnp.concatenate(dk_h, axis=1)
            dv_s[:end, :] += jnp.concatenate(dv_h, axis=1)
            dq_parts.append(jnp.concatenate(dq_h, axis=1))
        finish(0, pair, unchunked(jnp.concatenate(dq_parts, axis=0)))
        finish(1, pair, unchunked(dk_s[...]))
        finish(2, pair, unchunked(dv_s[...]))


VMEM_LIMIT = 56 * 1024 * 1024


def attn_fwd(mixed, bias, context, groups, chunk):
    rows, columns = mixed.shape
    block = columns // groups
    heads = block // (3 * HEAD_WIDTH)
    cos_t, low_t, high_t, pos_c, pos_r = context
    whole = lambda shape: pl.BlockSpec(shape, lambda g: (0, 0))
    return pl.pallas_call(
        functools.partial(attn_fwd_kernel, heads, chunk),
        grid=(groups,),
        in_specs=[
            pl.BlockSpec((rows, block), lambda g: (0, g)),
            pl.BlockSpec((1, 1, block), lambda g: (g, 0, 0)),
            whole((rows, 128)),
            whole((rows, 128)),
            whole((rows, 128)),
            whole((rows, 1)),
            whole((1, rows)),
        ],
        out_specs=[
            pl.BlockSpec((rows, block), lambda g: (0, g)),
            pl.BlockSpec((rows, block // 3), lambda g: (0, g)),
            pl.BlockSpec((1, rows, heads), lambda g: (g, 0, 0)),
        ],
        out_shape=[
            jax.ShapeDtypeStruct((rows, columns), jnp.bfloat16),
            jax.ShapeDtypeStruct((rows, columns // 3), jnp.bfloat16),
            jax.ShapeDtypeStruct((groups, rows, heads), jnp.float32),
        ],
        compiler_params=pltpu.CompilerParams(vmem_limit_bytes=VMEM_LIMIT),
        cost_estimate=pl.CostEstimate(
            flops=3 * rows * rows * columns // 3 * 4,
            bytes_accessed=rows * columns * 7,
            transcendentals=rows * rows * columns // (3 * HEAD_WIDTH),
        ),
    )(mixed, bias.reshape(groups, 1, block), cos_t, low_t, high_t, pos_c, pos_r)


def attn_bwd(qkv, lse, ctx_grad, context, groups, chunk):
    rows, columns = qkv.shape
    block = columns // groups
    heads = block // (3 * HEAD_WIDTH)
    cos_t, low_t, high_t, pos_c, pos_r = context
    whole = lambda shape: pl.BlockSpec(shape, lambda g: (0, 0))
    return pl.pallas_call(
        functools.partial(attn_bwd_kernel, heads, chunk),
        grid=(groups,),
        in_specs=[
            pl.BlockSpec((rows, block), lambda g: (0, g)),
            pl.BlockSpec((1, heads, rows), lambda g: (g, 0, 0)),
            pl.BlockSpec((rows, block // 3), lambda g: (0, g)),
            whole((rows, 128)),
            whole((rows, 128)),
            whole((rows, 128)),
            whole((rows, 1)),
            whole((1, rows)),
        ],
        out_specs=[
            pl.BlockSpec((rows, block), lambda g: (0, g)),
            pl.BlockSpec((1, 1, block), lambda g: (g, 0, 0)),
        ],
        out_shape=[
            jax.ShapeDtypeStruct((rows, columns), jnp.bfloat16),
            jax.ShapeDtypeStruct((groups, 1, block), jnp.float32),
        ],
        scratch_shapes=[pltpu.VMEM((rows, 128), jnp.float32), pltpu.VMEM((rows, 128), jnp.float32)],
        compiler_params=pltpu.CompilerParams(vmem_limit_bytes=VMEM_LIMIT),
        cost_estimate=pl.CostEstimate(
            flops=rows * columns,
            bytes_accessed=rows * columns,
            transcendentals=0,
        ),
    )(qkv, lse.swapaxes(1, 2), ctx_grad, cos_t, low_t, high_t, pos_c, pos_r)


def bulk_device(
    tokens_in,
    cotangent,
    plan,
    positions,
    norm_gain,
    norm_shift,
    w_qkv,
    b_qkv,
    w_out,
    w_gate_up,
    down_weight,
):
    tp_count = lax.axis_size("tp")
    ctx_count = lax.axis_size("ctx")
    section_index = lax.axis_index("section")
    ctx_index = lax.axis_index("ctx")
    side, core = ctx_index // 2, ctx_index % 2
    core_route, across_route = pair_routes(ctx_count)
    micro_count, slice_len, _, width = tokens_in.shape
    gain, shift = norm_gain[0], norm_shift[0]
    piece = slice_len // 2
    rows = micro_count * slice_len * 2
    own_rows = rows // 2
    half_width = width // 2
    columns = w_qkv.shape[3] // 2
    hidden = w_gate_up.shape[3] // 2
    first = section_index == 0

    ordered = jnp.stack(
        [lax.dynamic_index_in_dim(tokens_in, plan[m], 0, keepdims=False)[:, 0] for m in range(micro_count)]
    )
    fresh = jnp.where(first, ordered, cotangent[:, :, 0])
    fresh = fresh.reshape(ctx_count // 2, tp_count, 2, piece, width).transpose(0, 2, 1, 3, 4)
    fresh = fresh.reshape(ctx_count * tp_count, piece, width)
    inbound = lax.all_to_all(fresh, ("ctx", "tp"), 0, 0, tiled=True).reshape(own_rows, width)

    pos = positions.reshape(-1, 2, piece)
    pos = jnp.concatenate(
        [
            lax.dynamic_index_in_dim(pos, core, 1, False).reshape(-1),
            lax.dynamic_index_in_dim(pos, 1 - core, 1, False).reshape(-1),
        ]
    )
    chunk = min(128, own_rows)
    chunk_pos = chunked(pos, chunk)
    context = (*rot_tables(pos), chunk_pos[:, None], chunk_pos[None, :])

    tp_index = lax.axis_index("tp")

    def turned_by_tp(shards, axis=0):
        count = shards.shape[axis] // tp_count
        twice = jnp.concatenate([shards, shards], axis=axis)
        start = lax.rem(tp_count - tp_index, tp_count) * count
        return lax.dynamic_slice_in_dim(twice, start, tp_count * count, axis)

    def after(x, *others):
        return lax.optimization_barrier((x, *others))[0]

    own_parts, across_parts = [], []

    def gathered(block_of):
        block, held = block_of(side), block_of(1 - side)
        count = block.shape[0]
        step = len(own_parts)
        if step == 2:
            block = after(block, own_parts[0], across_parts[0], inbound)
        elif step > 2:
            block = after(block, own_parts[step - 2], across_parts[step - 3])
        own = lax.all_gather(block, "tp", axis=0, tiled=True)
        wanted = [
            lax.dynamic_slice_in_dim(own, lax.rem(tp_index + p, tp_count) * count, count, 0)
            for p in range(1, tp_count)
        ]
        arriving = lax.ppermute(jnp.concatenate(wanted, axis=0), "ctx", across_route)
        own_parts.append(own)
        across_parts.append(arriving)
        other = turned_by_tp(jnp.concatenate([held, arriving], axis=0))
        return jnp.where(
            side == 0, jnp.concatenate([own, other], axis=1), jnp.concatenate([other, own], axis=1)
        )

    def qkv_block(half):
        block = lax.dynamic_slice(w_qkv[0], (0, half * half_width, core * columns), (3, half_width, columns))
        return block.transpose(0, 2, 1).reshape(3 * columns, half_width)

    def out_block(half):
        return lax.dynamic_slice(w_out[0], (core * columns, half * half_width), (columns, half_width))

    def gu_block(which, half):
        block = lax.dynamic_slice(
            w_gate_up[0], (which, half * half_width, core * hidden), (1, half_width, hidden)
        )
        return block[0].T

    def down_block(part, half):
        start = core * hidden + part * (hidden // 2)
        return lax.dynamic_slice(down_weight[0], (start, half * half_width), (hidden // 2, half_width))

    wt_out = gathered(out_block)
    wt_qkv = gathered(qkv_block)
    wt_gu = jnp.concatenate([gathered(functools.partial(gu_block, w)) for w in range(2)], axis=0)
    wt_down = jnp.concatenate(
        [
            gathered(functools.partial(down_block, part)).reshape(tp_count, hidden // 2, width)
            for part in range(2)
        ],
        axis=1,
    ).reshape(tp_count * hidden, width)
    bias_own = lax.dynamic_slice_in_dim(b_qkv[0], core * columns, columns, 1).reshape(1, 3 * columns)
    bias = [bias_own]
    for p in range(1, tp_count):
        ring = [((i + p) % tp_count, i) for i in range(tp_count)]
        bias.append(lax.ppermute(bias_own, "tp", ring))
    bias = turned_by_tp(jnp.concatenate(bias, axis=0))
    ff = wt_down.shape[0]

    def both(own):
        return jnp.concatenate([own, lax.ppermute(own, "ctx", core_route)], axis=0)

    def summed(a, weight, parts=1):
        step = own_rows // parts
        spans = [slice(i * step, (i + 1) * step) for i in range(parts)]
        others = [dot_n(a[own_rows:][span], weight).astype(jnp.bfloat16) for span in spans]
        arriving = [lax.ppermute(other, "ctx", core_route) for other in others]
        own = [dot_n(a[:own_rows][span], weight) for span in spans]
        return [x + y.astype(jnp.float32) for x, y in zip(own, arriving)]

    def split(x, parts):
        step = x.shape[0] // parts
        return [x[i * step : (i + 1) * step] for i in range(parts)]

    def over_x(parts, route):
        return jnp.concatenate([lax.ppermute(part, "section", route) for part in parts], axis=0)

    def forward(stream, parts):
        normed = both(ln(stream, gain[0], shift[0]))
        mixed = dot_t(normed, wt_qkv)
        qkv, attended, lse = attn_fwd(mixed, bias, context, tp_count, chunk)
        hidden_state = stream + summed(attended, wt_out)[0]
        normed_two = both(ln(hidden_state, gain[1], shift[1]))
        gate_up = dot_t(normed_two, wt_gu)
        gate, up = gate_up[:, :ff], gate_up[:, ff:]
        activation = (jax.nn.silu(gate) * up).astype(jnp.bfloat16)
        out = [
            (x + y).astype(jnp.bfloat16)
            for x, y in zip(split(hidden_state, parts), summed(activation, wt_down, parts))
        ]
        return out, (stream, normed, (qkv, lse), attended, hidden_state, normed_two, gate_up, activation)

    def far_near(right):
        far = lax.dynamic_slice_in_dim(right, (1 - side) * half_width, half_width, 1)
        near = lax.dynamic_slice_in_dim(right, side * half_width, half_width, 1)
        return far, near

    def far_term(left, right):
        return dot_0(left, far_near(right)[0]).astype(jnp.bfloat16)

    def near_total(left, right, arriving, *others):
        near = far_near(right)[1]
        if others:
            near = after(near, *others)
        return (dot_0(left, near) + arriving.astype(jnp.float32)).astype(jnp.bfloat16)

    def across(term, *others):
        return lax.ppermute(after(term, *others) if others else term, "ctx", across_route)

    def over_tp(term):
        return lax.psum_scatter(term, "tp", scatter_dimension=0, tiled=True)

    together = lax.optimization_barrier

    def part_of(x, i, parts, axis):
        shard = x.shape[axis] // tp_count
        step = shard // parts
        return jnp.concatenate(
            [
                lax.slice_in_dim(x, z * shard + i * step, z * shard + (i + 1) * step, axis=axis)
                for z in range(tp_count)
            ],
            axis=axis,
        )

    def mlp_back(act_grad, gate_up):
        gate, up = gate_up[:, :ff], gate_up[:, ff:]
        sigma = jax.nn.sigmoid(gate)
        gate_grad = (act_grad * up * sigma * (1.0 + gate * (1.0 - sigma))).astype(jnp.bfloat16)
        up_grad = (act_grad * gate * sigma).astype(jnp.bfloat16)
        return gate_grad, up_grad

    def two_dot(gate_grad, up_grad):
        return dot_n(jnp.concatenate([gate_grad, up_grad], axis=1), wt_gu)

    def from_core(term):
        return lax.ppermute(term.astype(jnp.bfloat16), "ctx", core_route).astype(jnp.float32)

    def backward(grad_out, stored, wait):
        stream, normed, (qkv, lse), attended, hidden_state, normed_two, gate_up, activation = stored
        gate_grad, up_grad = mlp_back(dot_t(both(grad_out), wt_down), gate_up)
        gu_grad = jnp.concatenate([gate_grad, up_grad], axis=1)
        two_grad = summed(gu_grad, wt_gu)[0]
        hidden_grad = grad_out.astype(jnp.float32) + ln_back(hidden_state, two_grad, gain[1])[0]
        ctx_grad = dot_t(both(hidden_grad.astype(jnp.bfloat16)), wt_out).astype(jnp.bfloat16)
        qkv_grad, _ = attn_bwd(qkv, lse, ctx_grad, context, tp_count, chunk)
        one_other = from_core(dot_n(qkv_grad[own_rows:], wt_qkv))
        one_grad = dot_n(after(qkv_grad[:own_rows], wait), wt_qkv) + one_other
        return (hidden_grad + ln_back(stream, one_grad, gain[0])[0]).astype(jnp.bfloat16)

    def settled(term):
        share = half_width // 2
        away = lax.dynamic_slice_in_dim(term, (1 - core) * share, share, term.ndim - 1)
        kept = lax.dynamic_slice_in_dim(term, core * share, share, term.ndim - 1)
        got = lax.ppermute(away, "ctx", core_route)
        axis = term.ndim - 2
        return jnp.where(
            core == 0, jnp.concatenate([kept, got], axis), jnp.concatenate([got, kept], axis)
        ).astype(jnp.float32)

    def vector_sums(small):
        gain_terms, shift_terms, bias_terms = small
        bias_terms = bias_terms.reshape(tp_count, 3, columns).transpose(1, 0, 2)[:, :, None]
        bias_full = jnp.where(
            (jnp.arange(2) == core)[None, None, :, None], bias_terms, 0.0
        ).reshape(3, tp_count * 2 * columns)
        vectors = jnp.concatenate([gain_terms, shift_terms, bias_full], axis=0)
        share = width // (ctx_count * tp_count)
        vectors = vectors.reshape(-1, ctx_count * tp_count, share).transpose(1, 0, 2)
        return jnp.sum(lax.all_to_all(vectors, ("ctx", "tp"), 0, 0, tiled=True), axis=0).reshape(-1, share)

    def last_backward(grad_out, stored, final_out, act_both):
        stream, normed, (qkv, lse), attended, hidden_state, normed_two, gate_up, _ = stored
        grad_f32 = grad_out.astype(jnp.float32)
        far_grad, near_grad = far_near(grad_out)
        grad_across = across(far_grad)
        mlp_grad = both(grad_out)
        gate_grad, up_grad = mlp_back(dot_t(mlp_grad, wt_down), gate_up)
        far_gate = far_term(gate_grad, normed_two)

        grad_across, far_gate, gate_grad, up_grad = together((grad_across, far_gate, gate_grad, up_grad))
        far_gate_a, far_gate_b = split(far_gate, 2)
        arriving = across(far_gate_a)
        gu_grad = jnp.concatenate([gate_grad, up_grad], axis=1)
        grad_both = jnp.concatenate([both(near_grad), both(grad_across)], axis=0)
        down_total = dot_0(act_both, grad_both).astype(jnp.bfloat16)
        two_other = dot_n(gu_grad[own_rows:], wt_gu).astype(jnp.bfloat16)

        arriving, far_gate_b, two_other, gu_grad, down_total, gate_grad, up_grad = together(
            (arriving, far_gate_b, two_other, gu_grad, down_total, gate_grad, up_grad)
        )
        arriving_gate = jnp.concatenate([arriving, across(far_gate_b)], axis=0)
        sum_down = over_tp(down_total)
        two_grad = dot_n(gu_grad[:own_rows], wt_gu) + lax.ppermute(two_other, "ctx", core_route).astype(jnp.float32)
        result, gain_two, shift_two = ln_back(hidden_state, two_grad, gain[1])
        hidden_grad = grad_f32 + result
        attn_grad = both(hidden_grad.astype(jnp.bfloat16))
        far_up_a, far_up_b = (far_term(x, normed_two) for x in jnp.split(up_grad, 2, axis=1))

        arriving_gate, far_up_a, far_up_b, gate_grad, attn_grad, hidden_grad = together(
            (arriving_gate, far_up_a, far_up_b, gate_grad, attn_grad, hidden_grad)
        )
        arriving = across(far_up_a)
        sum_gate = over_tp(near_total(gate_grad, normed_two, arriving_gate))
        ctx_grad = dot_t(attn_grad, wt_out).astype(jnp.bfloat16)

        arriving, far_up_b, ctx_grad = together((arriving, far_up_b, ctx_grad))
        arriving_up = jnp.concatenate([arriving, across(far_up_b)], axis=0)
        qkv_grad, bias_grad = attn_bwd(qkv, lse, ctx_grad, context, tp_count, chunk)
        qkv_a, qkv_b = (part_of(qkv_grad, i, 2, 1) for i in range(2))
        far_a = far_term(qkv_a, normed)

        arriving_up, far_a, qkv_a, qkv_b, qkv_grad, up_grad, attn_grad = together(
            (arriving_up, far_a, qkv_a, qkv_b, qkv_grad, up_grad, attn_grad)
        )
        arriving = across(far_a)
        sum_up = over_tp(near_total(up_grad, normed_two, arriving_up))
        far_b = far_term(qkv_b, normed)
        one_other = dot_n(qkv_grad[own_rows:], wt_qkv).astype(jnp.bfloat16)

        arriving, far_b, one_other, qkv_grad, qkv_a, qkv_b, attn_grad = together(
            (arriving, far_b, one_other, qkv_grad, qkv_a, qkv_b, attn_grad)
        )
        arriving_b = across(far_b)
        sum_qkv_a = over_tp(near_total(qkv_a, normed, arriving))
        one_grad = dot_n(qkv_grad[:own_rows], wt_qkv) + lax.ppermute(one_other, "ctx", core_route).astype(jnp.float32)
        result, gain_one, shift_one = ln_back(stream, one_grad, gain[0])
        input_grad = (hidden_grad + result).astype(jnp.bfloat16)
        ends = jnp.where(first, input_grad, final_out)
        far_out = far_term(attended, attn_grad)
        small = vector_sums((jnp.stack([gain_one, gain_two]), jnp.stack([shift_one, shift_two]), bias_grad))

        arriving_b, far_out, ends, qkv_b, small = together((arriving_b, far_out, ends, qkv_b, small))
        arriving_out = across(far_out)
        ends = lax.all_to_all(
            ends.reshape(ctx_count * tp_count, piece, width), ("ctx", "tp"), 0, 0, tiled=True
        )
        sum_qkv_b = over_tp(near_total(qkv_b, normed, arriving_b))
        done = (settled(sum_down), jnp.stack([settled(sum_gate).T, settled(sum_up).T]))

        arriving_out, attn_grad, done, ends = together((arriving_out, attn_grad, done, ends))
        sum_out = over_tp(near_total(attended, attn_grad, arriving_out))
        sum_qkv = jnp.concatenate([sum_qkv_a, sum_qkv_b], axis=0)
        grads = (*done, settled(sum_out), settled(sum_qkv.reshape(3, columns, half_width)))
        return ends, small, grads

    sent, _ = forward(inbound.astype(jnp.float32), 2)
    arriving = over_x(sent, [(0, 1)])
    final_out, stored = forward(jnp.where(first, inbound, arriving).astype(jnp.float32), 1)
    act_across = across(stored[7])
    arriving_back = over_x([backward(inbound, stored, act_across)], [(1, 0)])
    arriving_back, final_out, act_both = together(
        (arriving_back, final_out[0], jnp.concatenate([stored[7], act_across], axis=0))
    )
    grad_out = jnp.where(first, arriving_back, inbound)
    ends, vectors, grads = last_backward(grad_out, stored, final_out, act_both)
    grad_down, grad_gu, grad_out_w, grad_qkv = grads

    ends = ends.reshape(ctx_count // 2, 2, tp_count, piece, width).transpose(0, 2, 1, 3, 4)
    ends = ends.reshape(micro_count, slice_len, 1, width)
    return (
        ends[None],
        vectors[None, :2],
        vectors[None, 2:4],
        vectors[None, 4:],
        grad_qkv.transpose(0, 2, 1)[None],
        grad_out_w[None],
        grad_gu[None],
        grad_down[None],
    )


def passed_along(block, axis, distance):
    devices = range(lax.axis_size(axis))
    route = [(i - distance, i) for i in devices if i - distance in devices]
    return lax.ppermute(block, axis, route)


def normalize(stream, gain_vec, shift_vec):
    centre = stream - jnp.mean(stream, axis=-1, keepdims=True)
    spread = jnp.mean(centre * centre, axis=-1, keepdims=True)
    return centre * lax.rsqrt(spread + 1e-05) * gain_vec + shift_vec


def norm_back(stream, grad_in, gain_vec):
    centre = stream - jnp.mean(stream, axis=-1, keepdims=True)
    inv_std = lax.rsqrt(jnp.mean(centre * centre, axis=-1, keepdims=True) + 1e-05)
    unit = centre * inv_std
    scaled = grad_in * gain_vec
    result = inv_std * (
        scaled
        - jnp.mean(scaled, axis=-1, keepdims=True)
        - unit * jnp.mean(scaled * unit, axis=-1, keepdims=True)
    )
    return (result, jnp.sum(grad_in * unit, axis=(0, 1)), jnp.sum(grad_in, axis=(0, 1)))


def rotary(tensor, cosine, sine):
    half_rot = ROT // 2
    front = tensor[..., :ROT]
    turned = jnp.concatenate([-front[..., half_rot:], front[..., :half_rot]], axis=-1)
    return jnp.concatenate([front * cosine + turned * sine, tensor[..., ROT:]], axis=-1)


def unrotary(tensor, cosine, sine):
    half_rot = ROT // 2
    front = tensor[..., :ROT]
    turned = jnp.concatenate([-front[..., half_rot:], front[..., :half_rot]], axis=-1)
    return jnp.concatenate([front * cosine - turned * sine, tensor[..., ROT:]], axis=-1)


def tables(position_rows):
    freqs = 10000.0 ** (-jnp.arange(ROT // 2, dtype=jnp.float32) * 2.0 / ROT)
    angles = position_rows.T.astype(jnp.float32)[:, :, None] * freqs
    angles = jnp.concatenate([angles, angles], axis=-1)[:, :, None, :]
    return (jnp.cos(angles), jnp.sin(angles))


def attention_scores(queries, key_heads, allowed):
    scores = jnp.einsum(
        "qshe,kshe->shqk", queries, key_heads, preferred_element_type=jnp.float32
    ) * HEAD_WIDTH ** (-0.5)
    return jnp.where(allowed, scores, -1e30)


def forward_layer(layer_in, weights, context_rows):
    gain_vec, shift_vec, w_qkv, b_qkv, w_out, w_gate_up, down_weight = weights
    cosine, sine, allowed = context_rows
    normed = normalize(layer_in, gain_vec[0], shift_vec[0]).astype(jnp.bfloat16)
    normed_all = lax.all_gather(normed, "tp", axis=0, tiled=True)
    block_len, seq_count, width = normed_all.shape
    columns = w_qkv.shape[2]
    head_count = columns // HEAD_WIDTH
    mixed = (
        jnp.einsum("rsd,cde->crse", normed_all, w_qkv, preferred_element_type=jnp.float32)
        + b_qkv[:, None, None, :]
    )
    queries = rotary(
        mixed[0].reshape(block_len, seq_count, head_count, HEAD_WIDTH), cosine, sine
    ).astype(jnp.bfloat16)
    key_own = rotary(
        mixed[1].reshape(block_len, seq_count, head_count, HEAD_WIDTH), cosine, sine
    ).astype(jnp.bfloat16)
    key_own = key_own.reshape(block_len, seq_count, columns)
    value_own = mixed[2].astype(jnp.bfloat16)
    key_all, value_all = (
        lax.all_gather(key_own, "ctx", axis=0, tiled=True),
        lax.all_gather(value_own, "ctx", axis=0, tiled=True),
    )
    key_heads = key_all.reshape(key_all.shape[0], seq_count, head_count, HEAD_WIDTH)
    value_heads = value_all.reshape(value_all.shape[0], seq_count, head_count, HEAD_WIDTH)
    scores = attention_scores(queries, key_heads, allowed)
    top_score = jnp.max(scores, axis=-1, keepdims=True)
    log_total = top_score + jnp.log(jnp.sum(jnp.exp(scores - top_score), axis=-1, keepdims=True))
    probability = jnp.exp(scores - log_total)
    attended = jnp.einsum(
        "shqk,kshe->qshe",
        probability.astype(jnp.bfloat16),
        value_heads,
        preferred_element_type=jnp.float32,
    )
    attended = attended.astype(jnp.bfloat16).reshape(block_len, seq_count, columns)
    piece = attended
    hidden_state = layer_in + lax.psum_scatter(
        jnp.einsum("rse,ed->rsd", piece, w_out, preferred_element_type=jnp.float32).astype(
            jnp.bfloat16
        ),
        "tp",
        scatter_dimension=0,
        tiled=True,
    ).astype(jnp.float32)
    normed_two = normalize(hidden_state, gain_vec[1], shift_vec[1]).astype(jnp.bfloat16)
    normed_two_all = lax.all_gather(normed_two, "tp", axis=0, tiled=True)
    gate_up = jnp.einsum(
        "rsd,cdf->crsf", normed_two_all, w_gate_up, preferred_element_type=jnp.float32
    )
    gated_activation = (jax.nn.silu(gate_up[0]) * gate_up[1]).astype(jnp.bfloat16)
    piece = gated_activation
    layer_out = hidden_state + lax.psum_scatter(
        jnp.einsum("rsf,fd->rsd", piece, down_weight, preferred_element_type=jnp.float32).astype(
            jnp.bfloat16
        ),
        "tp",
        scatter_dimension=0,
        tiled=True,
    ).astype(jnp.float32)
    stored = (
        layer_in,
        normed_all,
        queries,
        key_all,
        value_all,
        log_total,
        attended,
        hidden_state,
        normed_two_all,
        gate_up,
    )
    return (layer_out, stored)


def backward_layer(grad_out, stored, weights, context_rows):
    gain_vec, shift_vec, w_qkv, b_qkv, w_out, w_gate_up, down_weight = weights
    cosine, sine, allowed = context_rows
    (
        layer_in,
        normed_all,
        queries,
        key_all,
        value_all,
        log_total,
        attended,
        hidden_state,
        normed_two_all,
        gate_up,
    ) = stored
    block_len, seq_count, columns = attended.shape
    head_count = columns // HEAD_WIDTH
    mlp_grad = lax.all_gather(grad_out.astype(jnp.bfloat16), "tp", axis=0, tiled=True)
    gate_part = gate_up[0]
    up_part = gate_up[1]
    sigma = jax.nn.sigmoid(gate_part)
    swish = gate_part * sigma
    gated_activation = (swish * up_part).astype(jnp.bfloat16)
    down_grad = jnp.einsum(
        "rsf,rsd->fd", gated_activation, mlp_grad, preferred_element_type=jnp.float32
    )
    act_grad = jnp.einsum("rsd,fd->rsf", mlp_grad, down_weight, preferred_element_type=jnp.float32)
    gate_up_grad = jnp.stack(
        [act_grad * up_part * sigma * (1.0 + gate_part * (1.0 - sigma)), act_grad * swish]
    ).astype(jnp.bfloat16)
    gu_grad = jnp.einsum(
        "rsd,crsf->cdf", normed_two_all, gate_up_grad, preferred_element_type=jnp.float32
    )
    piece = gate_up_grad
    two_grad = lax.psum_scatter(
        jnp.einsum("crsf,cdf->rsd", piece, w_gate_up, preferred_element_type=jnp.float32).astype(
            jnp.bfloat16
        ),
        "tp",
        scatter_dimension=0,
        tiled=True,
    ).astype(jnp.float32)
    hidden_grad, gain_two, shift_two = norm_back(hidden_state, two_grad, gain_vec[1])
    hidden_grad = grad_out + hidden_grad
    attn_grad = lax.all_gather(hidden_grad.astype(jnp.bfloat16), "tp", axis=0, tiled=True)
    out_grad = jnp.einsum("rse,rsd->ed", attended, attn_grad, preferred_element_type=jnp.float32)
    ctx_grad = jnp.einsum("rsd,ed->rse", attn_grad, w_out, preferred_element_type=jnp.float32)
    ctx_grad = ctx_grad.astype(jnp.bfloat16).reshape(block_len, seq_count, head_count, HEAD_WIDTH)
    key_heads = key_all.reshape(key_all.shape[0], seq_count, head_count, HEAD_WIDTH)
    value_heads = value_all.reshape(value_all.shape[0], seq_count, head_count, HEAD_WIDTH)
    scores = attention_scores(queries, key_heads, allowed)
    probability = jnp.exp(scores - log_total)
    value_grad = jnp.einsum(
        "shqk,qshe->kshe",
        probability.astype(jnp.bfloat16),
        ctx_grad,
        preferred_element_type=jnp.float32,
    )
    prob_grad = jnp.einsum(
        "qshe,kshe->shqk", ctx_grad, value_heads, preferred_element_type=jnp.float32
    )
    score_grad = probability * (
        prob_grad - jnp.sum(probability * prob_grad, axis=-1, keepdims=True)
    )
    score_grad = score_grad.astype(jnp.bfloat16)
    query_grad = jnp.einsum(
        "shqk,kshe->qshe", score_grad, key_heads, preferred_element_type=jnp.float32
    ) * HEAD_WIDTH ** (-0.5)
    key_grad = jnp.einsum(
        "shqk,qshe->kshe", score_grad, queries, preferred_element_type=jnp.float32
    ) * HEAD_WIDTH ** (-0.5)
    key_back, value_back = (
        lax.psum_scatter(
            key_grad.astype(jnp.bfloat16), "ctx", scatter_dimension=0, tiled=True
        ).astype(jnp.float32),
        lax.psum_scatter(
            value_grad.astype(jnp.bfloat16), "ctx", scatter_dimension=0, tiled=True
        ).astype(jnp.float32),
    )
    qkv_grad = jnp.stack(
        [
            unrotary(query_grad, cosine, sine).reshape(block_len, seq_count, columns),
            unrotary(key_back, cosine, sine).reshape(block_len, seq_count, columns),
            value_back.reshape(block_len, seq_count, columns),
        ]
    ).astype(jnp.bfloat16)
    bias_grad = jnp.sum(qkv_grad.astype(jnp.float32), axis=(1, 2))
    qkv_weight_grad = jnp.einsum(
        "rsd,crse->cde", normed_all, qkv_grad, preferred_element_type=jnp.float32
    )
    piece = qkv_grad
    one_grad = lax.psum_scatter(
        jnp.einsum("crse,cde->rsd", piece, w_qkv, preferred_element_type=jnp.float32).astype(
            jnp.bfloat16
        ),
        "tp",
        scatter_dimension=0,
        tiled=True,
    ).astype(jnp.float32)
    input_grad, gain_one, shift_one = norm_back(layer_in, one_grad, gain_vec[0])
    input_grad = hidden_grad + input_grad
    weight_terms = (qkv_weight_grad, out_grad, gu_grad, down_grad)
    return (
        input_grad,
        (
            weight_terms,
            jnp.stack([gain_one, gain_two]),
            jnp.stack([shift_one, shift_two]),
            bias_grad,
        ),
    )


def spread(terms, columns, tp_index):
    weight_terms, gain_terms, shift_terms, bias_terms = terms
    qkv_term, out_term, gu_term, down_term = weight_terms
    scattered = (
        lax.psum_scatter(
            qkv_term.astype(jnp.bfloat16), "ctx", scatter_dimension=1, tiled=True
        ).astype(jnp.float32),
        lax.psum_scatter(
            out_term.astype(jnp.bfloat16), "ctx", scatter_dimension=1, tiled=True
        ).astype(jnp.float32),
        lax.psum_scatter(
            gu_term.astype(jnp.bfloat16), "ctx", scatter_dimension=1, tiled=True
        ).astype(jnp.float32),
        lax.psum_scatter(
            down_term.astype(jnp.bfloat16), "ctx", scatter_dimension=1, tiled=True
        ).astype(jnp.float32),
    )
    bias_full = lax.dynamic_update_slice_in_dim(
        jnp.zeros((3, gain_terms.shape[1]), jnp.float32), bias_terms, tp_index * columns, 1
    )
    gain_part, shift_part, bias_part = (
        lax.psum_scatter(gain_terms, ("ctx", "tp"), scatter_dimension=1, tiled=True),
        lax.psum_scatter(shift_terms, ("ctx", "tp"), scatter_dimension=1, tiled=True),
        lax.psum_scatter(bias_full, ("ctx", "tp"), scatter_dimension=1, tiled=True),
    )
    return (tuple(scattered), gain_part, shift_part, bias_part)


def stepwise_device(
    tokens_in,
    cotangent,
    plan,
    positions,
    norm_gain,
    norm_shift,
    w_qkv,
    b_qkv,
    w_out,
    w_gate_up,
    down_weight,
):
    weights = (
        norm_gain[0],
        norm_shift[0],
        w_qkv[0],
        b_qkv[0],
        w_out[0],
        w_gate_up[0],
        down_weight[0],
    )
    micro_count = tokens_in.shape[0]
    local_row_slice = tokens_in.shape[1]
    width = tokens_in.shape[3]
    columns = w_qkv.shape[3]
    ff_local = w_gate_up.shape[3]
    tp_count = lax.axis_size("tp")
    ctx_count = lax.axis_size("ctx")
    block_len = local_row_slice * tp_count
    section_index = lax.axis_index("section")
    ctx_index = lax.axis_index("ctx")
    tp_index = lax.axis_index("tp")
    block_pos = lax.dynamic_slice_in_dim(positions, ctx_index * block_len, block_len, 1)
    cosine, sine = tables(block_pos)
    allowed = (positions[:, None, :] <= block_pos[:, :, None])[:, None]
    context_rows = (cosine, sine, allowed)
    zero_rows = jnp.zeros(tokens_in.shape[1:], jnp.bfloat16)

    def forward_step(carry, step_index):
        arriving = passed_along(carry, "section", 1)
        micro = jnp.clip(step_index, 0, micro_count - 1)
        fresh = lax.dynamic_index_in_dim(tokens_in, plan[micro], 0, keepdims=False)
        layer_in = jnp.where(section_index == 0, fresh, arriving).astype(jnp.float32)
        layer_out, stored = forward_layer(layer_in, weights, context_rows)
        sent = layer_out.astype(jnp.bfloat16)
        return (sent, (sent, stored))

    steps_all = jnp.arange(micro_count + 1, dtype=jnp.int32)
    unused, (outputs, stored_all) = lax.scan(forward_step, zero_rows, steps_all)
    share = width // ctx_count
    fine_share = width // (ctx_count * tp_count)
    totals = (
        (
            jnp.zeros((3, share, columns), jnp.float32),
            jnp.zeros((columns, share), jnp.float32),
            jnp.zeros((2, share, ff_local), jnp.float32),
            jnp.zeros((ff_local, share), jnp.float32),
        ),
        jnp.zeros((2, fine_share), jnp.float32),
        jnp.zeros((2, fine_share), jnp.float32),
        jnp.zeros((3, fine_share), jnp.float32),
    )

    def backward_step(carry, bundle):
        send_back, running = carry
        step_index, stored = bundle
        arriving = passed_along(send_back, "section", -1)
        micro = step_index - section_index
        valid_step = ((micro >= 0) & (micro < micro_count)).astype(jnp.float32)
        target = lax.dynamic_index_in_dim(
            cotangent, jnp.clip(micro, 0, micro_count - 1), 0, keepdims=False
        )
        grad_out = jnp.where(section_index == 1, target, arriving).astype(jnp.float32)
        input_grad, terms = backward_layer(grad_out, stored, weights, context_rows)
        terms = jax.tree.map(lambda tensor: tensor * valid_step, terms)
        terms = spread(terms, columns, tp_index)
        running = jax.tree.map(jnp.add, running, terms)
        sent = input_grad.astype(jnp.bfloat16)
        return ((sent, running), sent)

    (unused_back, totals), input_grads = lax.scan(
        backward_step, (zero_rows, totals), (steps_all, stored_all), reverse=True
    )
    weight_parts, gain_part, shift_part, bias_part = totals
    section_ends = jnp.where(section_index == 0, input_grads[:micro_count], outputs[1:])[None]
    return (
        section_ends,
        gain_part[None],
        shift_part[None],
        bias_part[None],
        weight_parts[0][None],
        weight_parts[1][None],
        weight_parts[2][None],
        weight_parts[3][None],
    )


def per_device(*arrays):
    chips = lax.axis_size("ctx") // 2 * lax.axis_size("tp")
    if lax.axis_size("section") == 2 and lax.axis_size("ctx") == 4 and arrays[0].shape[0] == chips:
        return bulk_device(*arrays)
    return stepwise_device(*arrays)


def solution(mesh):
    placed = (
        P(None, ("ctx", "tp"), None, None),
        P(None, ("ctx", "tp"), None, None),
        P(),
        P(),
        P("section", None, None),
        P("section", None, None),
        P("section", None, None, "tp"),
        P("section", None, "tp"),
        P("section", "tp", None),
        P("section", None, None, "tp"),
        P("section", "tp", None),
    )
    return jax.shard_map(
        per_device,
        mesh=mesh,
        in_specs=placed,
        out_specs=(
            P("section", None, ("ctx", "tp"), None, None),
            P("section", None, ("ctx", "tp")),
            P("section", None, ("ctx", "tp")),
            P("section", None, ("ctx", "tp")),
            P("section", None, "ctx", "tp"),
            P("section", "tp", "ctx"),
            P("section", None, "ctx", "tp"),
            P("section", "tp", "ctx"),
        ),
        check_vma=False,
    )
```

```python
import functools

import jax
import jax.numpy as jnp
from jax import lax
from jax.experimental import pallas as pl
from jax.experimental.layout import Layout, with_layout_constraint
from jax.experimental.pallas import tpu as pltpu
from jax.sharding import PartitionSpec as P

HEAD_WIDTH = 64
ROT = 16


def pair_routes(ctx_count):
    core = [(i, i ^ 1) for i in range(ctx_count)]
    across = [(i, (i + 2) % 4) for i in range(ctx_count)]
    return core, across


def ln_stats(stream):
    mean = jnp.mean(stream, axis=-1, keepdims=True)
    centre = stream - mean
    inv_std = lax.rsqrt(jnp.mean(centre * centre, axis=-1, keepdims=True) + 1e-05)
    return centre, inv_std


def ln(stream, gain_vec, shift_vec):
    centre, inv_std = ln_stats(stream)
    return (centre * inv_std * gain_vec + shift_vec).astype(jnp.bfloat16)


def ln_back(stream, grad_in, gain_vec):
    centre, inv_std = ln_stats(stream)
    unit = centre * inv_std
    scaled = grad_in * gain_vec
    result = inv_std * (
        scaled
        - jnp.mean(scaled, axis=-1, keepdims=True)
        - unit * jnp.mean(scaled * unit, axis=-1, keepdims=True)
    )
    return result, jnp.sum(grad_in * unit, axis=0), jnp.sum(grad_in, axis=0)


def rot_tables(pos_row):
    half = ROT // 2
    freqs = 10000.0 ** (-jnp.arange(half, dtype=jnp.float32) * 2.0 / ROT)
    angles = pos_row.astype(jnp.float32)[:, None] * freqs
    cosine, sine = jnp.cos(angles), jnp.sin(angles)
    rows = pos_row.shape[0]
    rest = HEAD_WIDTH - ROT
    zeros = jnp.zeros((rows, half), jnp.float32)
    cos_head = jnp.concatenate([cosine, cosine, jnp.ones((rows, rest), jnp.float32)], 1)
    low_head = jnp.concatenate([-sine, zeros, jnp.zeros((rows, rest), jnp.float32)], 1)
    high_head = jnp.concatenate([zeros, sine, jnp.zeros((rows, rest), jnp.float32)], 1)
    return tuple(jnp.concatenate([t, t], 1) for t in (cos_head, low_head, high_head))


def dot_t(a, b):
    return lax.dot_general(a, b, (((1,), (1,)), ((), ())), preferred_element_type=jnp.float32)


def dot_0(a, b):
    return lax.dot_general(a, b, (((0,), (0,)), ((), ())), preferred_element_type=jnp.float32)


def dot_n(a, b):
    return lax.dot_general(a, b, (((1,), (0,)), ((), ())), preferred_element_type=jnp.float32)


def chunked(x, chunk):
    half = x.shape[0] // 2
    pieces = []
    for i in range(half // chunk):
        pieces.append(x[i * chunk : (i + 1) * chunk])
        pieces.append(x[half + i * chunk : half + (i + 1) * chunk])
    return jnp.concatenate(pieces, axis=0)


def attn_fwd_kernel(heads, chunk, mixed, bias, cos_t, low_t, high_t, pos_c, pos_r, qkv, out, lse):
    rows = mixed.shape[0]
    half = rows // 2
    width = heads * HEAD_WIDTH
    half_rot = ROT // 2
    cosine, low, high = cos_t[...], low_t[...], high_t[...]
    for pair in range(heads // 2):
        parts = []
        for c in range(3):
            at = c * width + pair * 128
            x = mixed[:, at : at + 128] + bias[0, :, at : at + 128]
            if c < 2:
                x = x * cosine + pltpu.roll(x, 128 - half_rot, 1) * low + pltpu.roll(x, half_rot, 1) * high
            x = x.astype(jnp.bfloat16)
            qkv[:, at : at + 128] = x
            parts.append(chunked(x, chunk))
        query, key, value = parts
        query = query * jnp.bfloat16(HEAD_WIDTH ** (-0.5))
        for i in range(half // chunk):
            end = 2 * chunk * (i + 1)
            begin = end - 2 * chunk
            allowed = pos_r[:, begin:end] <= pos_c[begin:end, :]
            halves = []
            for h in range(2):
                lanes = slice(h * HEAD_WIDTH, (h + 1) * HEAD_WIDTH)
                q_h = query[begin:end, lanes]
                score = dot_t(q_h, key[:end, lanes])
                last = jnp.where(allowed, score[:, begin:], -1e30)
                score = last if i == 0 else jnp.concatenate([score[:, :begin], last], axis=1)
                top = jnp.max(score, axis=1, keepdims=True)
                prob = jnp.exp(score - top)
                total = jnp.sum(prob, axis=1, keepdims=True)
                lse[0, begin:end, 2 * pair + h : 2 * pair + h + 1] = top + jnp.log(total)
                mixed_values = dot_n(prob.astype(jnp.bfloat16), value[:end, lanes])
                halves.append(mixed_values / total)
            done = jnp.concatenate(halves, axis=1).astype(jnp.bfloat16)
            lanes = slice(pair * 128, pair * 128 + 128)
            out[i * chunk : (i + 1) * chunk, lanes] = done[:chunk]
            out[half + i * chunk : half + (i + 1) * chunk, lanes] = done[chunk:]


def attn_bwd_kernel(heads, chunk, qkv, lse, ctx, cos_t, low_t, high_t, pos_c, pos_r, grad, bias_grad, dk_s, dv_s):
    rows = qkv.shape[0]
    half = rows // 2
    width = heads * HEAD_WIDTH
    half_rot = ROT // 2
    cosine, low, high = cos_t[...], low_t[...], high_t[...]
    scale = HEAD_WIDTH ** (-0.5)

    def finish(c, pair, x):
        at = c * width + pair * 128
        if c < 2:
            x = x * scale
            x = x * cosine + pltpu.roll(x * high, 128 - half_rot, 1) + pltpu.roll(x * low, half_rot, 1)
        x = x.astype(jnp.bfloat16)
        grad[:, at : at + 128] = x
        bias_grad[0, :, at : at + 128] = jnp.sum(x.astype(jnp.float32), axis=0, keepdims=True)

    def unchunked(x):
        steps = half // chunk
        own = [x[2 * i * chunk : (2 * i + 1) * chunk] for i in range(steps)]
        other = [x[(2 * i + 1) * chunk : (2 * i + 2) * chunk] for i in range(steps)]
        return jnp.concatenate(own + other, axis=0)

    for pair in range(heads // 2):
        lanes2 = slice(pair * 128, pair * 128 + 128)
        query, key, value = (
            chunked(qkv[:, c * width + pair * 128 : c * width + pair * 128 + 128], chunk) for c in range(3)
        )
        query_s = query * jnp.bfloat16(scale)
        ctx_grad = chunked(ctx[:, lanes2], chunk)
        dk_s[...] = jnp.zeros_like(dk_s)
        dv_s[...] = jnp.zeros_like(dv_s)
        dq_parts = []
        for i in range(half // chunk):
            end = 2 * chunk * (i + 1)
            begin = end - 2 * chunk
            allowed = pos_c[begin:end, :] <= pos_r[:, begin:end]
            dq_h, dk_h, dv_h = [], [], []
            for h in range(2):
                lanes = slice(h * HEAD_WIDTH, (h + 1) * HEAD_WIDTH)
                score = dot_t(key[:end, lanes], query_s[begin:end, lanes])
                last = jnp.where(allowed, score[begin:, :], -1e30)
                score = last if i == 0 else jnp.concatenate([score[:begin, :], last], axis=0)
                prob = jnp.exp(score - lse[0, 2 * pair + h : 2 * pair + h + 1, begin:end])
                grad_h = ctx_grad[begin:end, lanes]
                dv_h.append(dot_n(prob.astype(jnp.bfloat16), grad_h))
                prob_grad = dot_t(value[:end, lanes], grad_h)
                delta = jnp.sum(prob * prob_grad, axis=0, keepdims=True)
                score_grad = (prob * (prob_grad - delta)).astype(jnp.bfloat16)
                dk_h.append(dot_n(score_grad, query[begin:end, lanes]))
                dq_h.append(dot_0(score_grad, key[:end, lanes]))
            dk_s[:end, :] += jnp.concatenate(dk_h, axis=1)
            dv_s[:end, :] += jnp.concatenate(dv_h, axis=1)
            dq_parts.append(jnp.concatenate(dq_h, axis=1))
        finish(0, pair, unchunked(jnp.concatenate(dq_parts, axis=0)))
        finish(1, pair, unchunked(dk_s[...]))
        finish(2, pair, unchunked(dv_s[...]))


VMEM_LIMIT = 56 * 1024 * 1024


def attn_fwd(mixed, bias, context, groups, chunk):
    rows, columns = mixed.shape
    block = columns // groups
    heads = block // (3 * HEAD_WIDTH)
    cos_t, low_t, high_t, pos_c, pos_r = context
    whole = lambda shape: pl.BlockSpec(shape, lambda g: (0, 0))
    return pl.pallas_call(
        functools.partial(attn_fwd_kernel, heads, chunk),
        grid=(groups,),
        in_specs=[
            pl.BlockSpec((rows, block), lambda g: (0, g)),
            pl.BlockSpec((1, 1, block), lambda g: (g, 0, 0)),
            whole((rows, 128)),
            whole((rows, 128)),
            whole((rows, 128)),
            whole((rows, 1)),
            whole((1, rows)),
        ],
        out_specs=[
            pl.BlockSpec((rows, block), lambda g: (0, g)),
            pl.BlockSpec((rows, block // 3), lambda g: (0, g)),
            pl.BlockSpec((1, rows, heads), lambda g: (g, 0, 0)),
        ],
        out_shape=[
            jax.ShapeDtypeStruct((rows, columns), jnp.bfloat16),
            jax.ShapeDtypeStruct((rows, columns // 3), jnp.bfloat16),
            jax.ShapeDtypeStruct((groups, rows, heads), jnp.float32),
        ],
        compiler_params=pltpu.CompilerParams(vmem_limit_bytes=VMEM_LIMIT),
        cost_estimate=pl.CostEstimate(
            flops=3 * rows * rows * columns // 3 * 4,
            bytes_accessed=rows * columns * 7,
            transcendentals=rows * rows * columns // (3 * HEAD_WIDTH),
        ),
    )(mixed, bias.reshape(groups, 1, block), cos_t, low_t, high_t, pos_c, pos_r)


def attn_bwd(qkv, lse, ctx_grad, context, groups, chunk):
    rows, columns = qkv.shape
    block = columns // groups
    heads = block // (3 * HEAD_WIDTH)
    cos_t, low_t, high_t, pos_c, pos_r = context
    whole = lambda shape: pl.BlockSpec(shape, lambda g: (0, 0))
    return pl.pallas_call(
        functools.partial(attn_bwd_kernel, heads, chunk),
        grid=(groups,),
        in_specs=[
            pl.BlockSpec((rows, block), lambda g: (0, g)),
            pl.BlockSpec((1, heads, rows), lambda g: (g, 0, 0)),
            pl.BlockSpec((rows, block // 3), lambda g: (0, g)),
            whole((rows, 128)),
            whole((rows, 128)),
            whole((rows, 128)),
            whole((rows, 1)),
            whole((1, rows)),
        ],
        out_specs=[
            pl.BlockSpec((rows, block), lambda g: (0, g)),
            pl.BlockSpec((1, 1, block), lambda g: (g, 0, 0)),
        ],
        out_shape=[
            jax.ShapeDtypeStruct((rows, columns), jnp.bfloat16),
            jax.ShapeDtypeStruct((groups, 1, block), jnp.float32),
        ],
        scratch_shapes=[pltpu.VMEM((rows, 128), jnp.float32), pltpu.VMEM((rows, 128), jnp.float32)],
        compiler_params=pltpu.CompilerParams(vmem_limit_bytes=VMEM_LIMIT),
        cost_estimate=pl.CostEstimate(
            flops=rows * columns,
            bytes_accessed=rows * columns,
            transcendentals=0,
        ),
    )(qkv, lse.swapaxes(1, 2), ctx_grad, cos_t, low_t, high_t, pos_c, pos_r)


def bulk_device(
    tokens_in,
    cotangent,
    plan,
    positions,
    norm_gain,
    norm_shift,
    w_qkv,
    b_qkv,
    w_out,
    w_gate_up,
    down_weight,
):
    tp_count = lax.axis_size("tp")
    ctx_count = lax.axis_size("ctx")
    section_index = lax.axis_index("section")
    ctx_index = lax.axis_index("ctx")
    side, core = ctx_index // 2, ctx_index % 2
    core_route, across_route = pair_routes(ctx_count)
    micro_count, slice_len, _, width = tokens_in.shape
    gain, shift = norm_gain[0], norm_shift[0]
    piece = slice_len // 2
    rows = micro_count * slice_len * 2
    own_rows = rows // 2
    half_width = width // 2
    columns = w_qkv.shape[3] // 2
    hidden = w_gate_up.shape[3] // 2
    first = section_index == 0

    ordered = jnp.stack(
        [lax.dynamic_index_in_dim(tokens_in, plan[m], 0, keepdims=False)[:, 0] for m in range(micro_count)]
    )
    fresh = jnp.where(first, ordered, cotangent[:, :, 0])
    fresh = fresh.reshape(ctx_count // 2, tp_count, 2, piece, width).transpose(0, 2, 1, 3, 4)
    fresh = fresh.reshape(ctx_count * tp_count, piece, width)
    inbound = lax.all_to_all(fresh, ("ctx", "tp"), 0, 0, tiled=True).reshape(own_rows, width)

    pos = positions.reshape(-1, 2, piece)
    pos = jnp.concatenate(
        [
            lax.dynamic_index_in_dim(pos, core, 1, False).reshape(-1),
            lax.dynamic_index_in_dim(pos, 1 - core, 1, False).reshape(-1),
        ]
    )
    chunk = min(128, own_rows)
    chunk_pos = chunked(pos, chunk)
    context = (*rot_tables(pos), chunk_pos[:, None], chunk_pos[None, :])

    tp_index = lax.axis_index("tp")

    def turned_by_tp(shards, axis=0):
        count = shards.shape[axis] // tp_count
        twice = jnp.concatenate([shards, shards], axis=axis)
        start = lax.rem(tp_count - tp_index, tp_count) * count
        return lax.dynamic_slice_in_dim(twice, start, tp_count * count, axis)

    def after(x, *others):
        return lax.optimization_barrier((x, *others))[0]

    own_parts, across_parts = [], []

    def gathered(block_of):
        block, held = block_of(side), block_of(1 - side)
        count = block.shape[0]
        step = len(own_parts)
        if step == 2:
            block = after(block, own_parts[0], across_parts[0], inbound)
        elif step > 2:
            block = after(block, own_parts[step - 2], across_parts[step - 3])
        own = lax.all_gather(block, "tp", axis=0, tiled=True)
        wanted = [
            lax.dynamic_slice_in_dim(own, lax.rem(tp_index + p, tp_count) * count, count, 0)
            for p in range(1, tp_count)
        ]
        arriving = lax.ppermute(jnp.concatenate(wanted, axis=0), "ctx", across_route)
        own_parts.append(own)
        across_parts.append(arriving)
        other = turned_by_tp(jnp.concatenate([held, arriving], axis=0))
        return jnp.where(
            side == 0, jnp.concatenate([own, other], axis=1), jnp.concatenate([other, own], axis=1)
        )

    def qkv_block(half):
        block = lax.dynamic_slice(w_qkv[0], (0, half * half_width, core * columns), (3, half_width, columns))
        return block.transpose(0, 2, 1).reshape(3 * columns, half_width)

    def out_block(half):
        return lax.dynamic_slice(w_out[0], (core * columns, half * half_width), (columns, half_width))

    def gu_block(which, half):
        block = lax.dynamic_slice(
            w_gate_up[0], (which, half * half_width, core * hidden), (1, half_width, hidden)
        )
        return block[0].T

    def down_block(part, half):
        start = core * hidden + part * (hidden // 2)
        return lax.dynamic_slice(down_weight[0], (start, half * half_width), (hidden // 2, half_width))

    wt_out = gathered(out_block)
    wt_qkv = gathered(qkv_block)
    wt_gu = jnp.concatenate([gathered(functools.partial(gu_block, w)) for w in range(2)], axis=0)
    wt_down = jnp.concatenate(
        [
            gathered(functools.partial(down_block, part)).reshape(tp_count, hidden // 2, width)
            for part in range(2)
        ],
        axis=1,
    ).reshape(tp_count * hidden, width)
    bias_own = lax.dynamic_slice_in_dim(b_qkv[0], core * columns, columns, 1).reshape(1, 3 * columns)
    bias = [bias_own]
    for p in range(1, tp_count):
        ring = [((i + p) % tp_count, i) for i in range(tp_count)]
        bias.append(lax.ppermute(bias_own, "tp", ring))
    bias = turned_by_tp(jnp.concatenate(bias, axis=0))
    ff = wt_down.shape[0]

    def both(own):
        return jnp.concatenate([own, lax.ppermute(own, "ctx", core_route)], axis=0)

    def summed(a, weight, parts=1):
        step = own_rows // parts
        spans = [slice(i * step, (i + 1) * step) for i in range(parts)]
        others = [dot_n(a[own_rows:][span], weight).astype(jnp.bfloat16) for span in spans]
        arriving = [lax.ppermute(other, "ctx", core_route) for other in others]
        own = [dot_n(a[:own_rows][span], weight) for span in spans]
        return [x + y.astype(jnp.float32) for x, y in zip(own, arriving)]

    def split(x, parts):
        step = x.shape[0] // parts
        return [x[i * step : (i + 1) * step] for i in range(parts)]

    def over_x(parts, route):
        return jnp.concatenate([lax.ppermute(part, "section", route) for part in parts], axis=0)

    def forward(stream, parts):
        normed = both(ln(stream, gain[0], shift[0]))
        mixed = dot_t(normed, wt_qkv)
        qkv, attended, lse = attn_fwd(mixed, bias, context, tp_count, chunk)
        hidden_state = stream + summed(attended, wt_out)[0]
        normed_two = both(ln(hidden_state, gain[1], shift[1]))
        gate_up = dot_t(normed_two, wt_gu)
        gate, up = gate_up[:, :ff], gate_up[:, ff:]
        activation = (jax.nn.silu(gate) * up).astype(jnp.bfloat16)
        out = [
            (x + y).astype(jnp.bfloat16)
            for x, y in zip(split(hidden_state, parts), summed(activation, wt_down, parts))
        ]
        return out, (stream, normed, (qkv, lse), attended, hidden_state, normed_two, gate_up, activation)

    def far_near(right):
        far = lax.dynamic_slice_in_dim(right, (1 - side) * half_width, half_width, 1)
        near = lax.dynamic_slice_in_dim(right, side * half_width, half_width, 1)
        return far, near

    def far_term(left, right):
        return dot_0(left, far_near(right)[0]).astype(jnp.bfloat16)

    def near_total(left, right, arriving, *others):
        near = far_near(right)[1]
        if others:
            near = after(near, *others)
        return (dot_0(left, near) + arriving.astype(jnp.float32)).astype(jnp.bfloat16)

    def across(term, *others):
        return lax.ppermute(after(term, *others) if others else term, "ctx", across_route)

    def over_tp(term):
        return lax.psum_scatter(term, "tp", scatter_dimension=0, tiled=True)

    together = lax.optimization_barrier

    def part_of(x, i, parts, axis):
        shard = x.shape[axis] // tp_count
        step = shard // parts
        return jnp.concatenate(
            [
                lax.slice_in_dim(x, z * shard + i * step, z * shard + (i + 1) * step, axis=axis)
                for z in range(tp_count)
            ],
            axis=axis,
        )

    def mlp_back(act_grad, gate_up):
        gate, up = gate_up[:, :ff], gate_up[:, ff:]
        sigma = jax.nn.sigmoid(gate)
        gate_grad = (act_grad * up * sigma * (1.0 + gate * (1.0 - sigma))).astype(jnp.bfloat16)
        up_grad = (act_grad * gate * sigma).astype(jnp.bfloat16)
        return gate_grad, up_grad

    def two_dot(gate_grad, up_grad):
        return dot_n(jnp.concatenate([gate_grad, up_grad], axis=1), wt_gu)

    def from_core(term):
        return lax.ppermute(term.astype(jnp.bfloat16), "ctx", core_route).astype(jnp.float32)

    def backward(grad_out, stored, waits):
        stream, normed, (qkv, lse), attended, hidden_state, normed_two, gate_up, activation = stored
        gate_grad, up_grad = mlp_back(dot_t(both(grad_out), wt_down), gate_up)
        gu_grad = jnp.concatenate([gate_grad, up_grad], axis=1)
        two_grad = summed(gu_grad, wt_gu)[0]
        hidden_grad = grad_out.astype(jnp.float32) + ln_back(hidden_state, two_grad, gain[1])[0]
        ctx_grad = dot_t(both(hidden_grad.astype(jnp.bfloat16)), wt_out).astype(jnp.bfloat16)
        qkv_grad, _ = attn_bwd(qkv, lse, ctx_grad, context, tp_count, chunk)
        qkv_grad = after(qkv_grad, waits[0])
        one_other = from_core(dot_n(qkv_grad[own_rows:], wt_qkv))
        one_grad = dot_n(after(qkv_grad[:own_rows], waits[1]), wt_qkv) + one_other
        return (hidden_grad + ln_back(stream, one_grad, gain[0])[0]).astype(jnp.bfloat16)

    def settled(term):
        share = half_width // 2
        away = lax.dynamic_slice_in_dim(term, (1 - core) * share, share, term.ndim - 1)
        kept = lax.dynamic_slice_in_dim(term, core * share, share, term.ndim - 1)
        got = lax.ppermute(away, "ctx", core_route)
        axis = term.ndim - 2
        return jnp.where(
            core == 0, jnp.concatenate([kept, got], axis), jnp.concatenate([got, kept], axis)
        ).astype(jnp.float32)

    def vector_sums(small):
        gain_terms, shift_terms, bias_terms = small
        bias_terms = bias_terms.reshape(tp_count, 3, columns).transpose(1, 0, 2)[:, :, None]
        bias_full = jnp.where(
            (jnp.arange(2) == core)[None, None, :, None], bias_terms, 0.0
        ).reshape(3, tp_count * 2 * columns)
        vectors = jnp.concatenate([gain_terms, shift_terms, bias_full], axis=0)
        share = width // (ctx_count * tp_count)
        vectors = vectors.reshape(-1, ctx_count * tp_count, share).transpose(1, 0, 2)
        return jnp.sum(lax.all_to_all(vectors, ("ctx", "tp"), 0, 0, tiled=True), axis=0).reshape(-1, share)

    def last_backward(grad_out, stored, final_out, act_both):
        stream, normed, (qkv, lse), attended, hidden_state, normed_two, gate_up, _ = stored
        grad_f32 = grad_out.astype(jnp.float32)
        far_grad, near_grad = far_near(grad_out)
        grad_across = across(far_grad)
        mlp_grad = both(grad_out)
        gate_grad, up_grad = mlp_back(dot_t(mlp_grad, wt_down), gate_up)
        far_gate = far_term(gate_grad, normed_two)

        grad_across, far_gate, gate_grad, up_grad = together((grad_across, far_gate, gate_grad, up_grad))
        far_gate_a, far_gate_b = split(far_gate, 2)
        arriving = across(far_gate_a)
        gu_grad = jnp.concatenate([gate_grad, up_grad], axis=1)
        grad_both = jnp.concatenate([both(near_grad), both(grad_across)], axis=0)
        down_total = dot_0(act_both, grad_both).astype(jnp.bfloat16)
        two_other = dot_n(gu_grad[own_rows:], wt_gu).astype(jnp.bfloat16)

        arriving, far_gate_b, two_other, gu_grad, down_total, gate_grad, up_grad = together(
            (arriving, far_gate_b, two_other, gu_grad, down_total, gate_grad, up_grad)
        )
        arriving_gate = jnp.concatenate([arriving, across(far_gate_b)], axis=0)
        sum_down = over_tp(down_total)
        two_grad = dot_n(gu_grad[:own_rows], wt_gu) + lax.ppermute(two_other, "ctx", core_route).astype(jnp.float32)
        result, gain_two, shift_two = ln_back(hidden_state, two_grad, gain[1])
        hidden_grad = grad_f32 + result
        attn_grad = both(hidden_grad.astype(jnp.bfloat16))
        far_up_a, far_up_b = (far_term(x, normed_two) for x in jnp.split(up_grad, 2, axis=1))

        arriving_gate, far_up_a, far_up_b, gate_grad, attn_grad, hidden_grad = together(
            (arriving_gate, far_up_a, far_up_b, gate_grad, attn_grad, hidden_grad)
        )
        arriving = across(far_up_a)
        sum_gate = over_tp(near_total(gate_grad, normed_two, arriving_gate))
        ctx_grad = dot_t(attn_grad, wt_out).astype(jnp.bfloat16)

        arriving, far_up_b, ctx_grad = together((arriving, far_up_b, ctx_grad))
        arriving_up = jnp.concatenate([arriving, across(far_up_b)], axis=0)
        qkv_grad, bias_grad = attn_bwd(qkv, lse, ctx_grad, context, tp_count, chunk)
        qkv_a, qkv_b = (part_of(qkv_grad, i, 2, 1) for i in range(2))

        arriving_up, qkv_a, qkv_b, qkv_grad, up_grad, attn_grad = together(
            (arriving_up, qkv_a, qkv_b, qkv_grad, up_grad, attn_grad)
        )
        arriving = across(far_term(qkv_a, normed))
        sum_up = over_tp(near_total(up_grad, normed_two, arriving_up))
        far_b = far_term(qkv_b, normed)
        one_other = dot_n(qkv_grad[own_rows:], wt_qkv).astype(jnp.bfloat16)

        arriving, far_b, one_other, qkv_grad, qkv_a, qkv_b, attn_grad = together(
            (arriving, far_b, one_other, qkv_grad, qkv_a, qkv_b, attn_grad)
        )
        arriving_b = across(far_b)
        sum_qkv_a = over_tp(near_total(qkv_a, normed, arriving))
        one_grad = dot_n(qkv_grad[:own_rows], wt_qkv) + lax.ppermute(one_other, "ctx", core_route).astype(jnp.float32)
        result, gain_one, shift_one = ln_back(stream, one_grad, gain[0])
        input_grad = (hidden_grad + result).astype(jnp.bfloat16)
        ends = jnp.where(first, input_grad, final_out)
        far_out = far_term(attended, attn_grad)
        small = vector_sums((jnp.stack([gain_one, gain_two]), jnp.stack([shift_one, shift_two]), bias_grad))

        arriving_b, far_out, ends, qkv_b, small = together((arriving_b, far_out, ends, qkv_b, small))
        arriving_out = across(far_out)
        ends = lax.all_to_all(
            ends.reshape(ctx_count * tp_count, piece, width), ("ctx", "tp"), 0, 0, tiled=True
        )
        sum_qkv_b = over_tp(near_total(qkv_b, normed, arriving_b))
        grad_gu = jnp.stack([settled(sum_gate).T, settled(sum_up).T])[None]
        done = (settled(sum_down)[None], with_layout_constraint(grad_gu, Layout((0, 1, 2, 3))))

        arriving_out, attn_grad, done, ends = together((arriving_out, attn_grad, done, ends))
        sum_out = over_tp(near_total(attended, attn_grad, arriving_out))
        sum_qkv = jnp.concatenate([sum_qkv_a, sum_qkv_b], axis=0)
        grads = (*done, settled(sum_out), settled(sum_qkv.reshape(3, columns, half_width)))
        return ends, small, grads

    sent, _ = forward(inbound.astype(jnp.float32), 2)
    arriving = over_x(sent, [(0, 1)])
    final_out, stored = forward(jnp.where(first, inbound, arriving).astype(jnp.float32), 1)
    act_across = [across(part) for part in split(stored[7], 2)]
    arriving_back = over_x([backward(inbound, stored, act_across)], [(1, 0)])
    arriving_back, final_out, act_both = together(
        (arriving_back, final_out[0], jnp.concatenate([stored[7], *act_across], axis=0))
    )
    grad_out = jnp.where(first, arriving_back, inbound)
    ends, vectors, grads = last_backward(grad_out, stored, final_out, act_both)
    grad_down, grad_gu, grad_out_w, grad_qkv = grads

    ends = ends.reshape(ctx_count // 2, 2, tp_count, piece, width).transpose(0, 2, 1, 3, 4)
    ends = ends.reshape(micro_count, slice_len, 1, width)
    return (
        ends[None],
        vectors[None, :2],
        vectors[None, 2:4],
        vectors[None, 4:],
        grad_qkv.transpose(0, 2, 1)[None],
        grad_out_w[None],
        grad_gu,
        grad_down,
    )


def passed_along(block, axis, distance):
    devices = range(lax.axis_size(axis))
    route = [(i - distance, i) for i in devices if i - distance in devices]
    return lax.ppermute(block, axis, route)


def normalize(stream, gain_vec, shift_vec):
    centre = stream - jnp.mean(stream, axis=-1, keepdims=True)
    spread = jnp.mean(centre * centre, axis=-1, keepdims=True)
    return centre * lax.rsqrt(spread + 1e-05) * gain_vec + shift_vec


def norm_back(stream, grad_in, gain_vec):
    centre = stream - jnp.mean(stream, axis=-1, keepdims=True)
    inv_std = lax.rsqrt(jnp.mean(centre * centre, axis=-1, keepdims=True) + 1e-05)
    unit = centre * inv_std
    scaled = grad_in * gain_vec
    result = inv_std * (
        scaled
        - jnp.mean(scaled, axis=-1, keepdims=True)
        - unit * jnp.mean(scaled * unit, axis=-1, keepdims=True)
    )
    return (result, jnp.sum(grad_in * unit, axis=(0, 1)), jnp.sum(grad_in, axis=(0, 1)))


def rotary(tensor, cosine, sine):
    half_rot = ROT // 2
    front = tensor[..., :ROT]
    turned = jnp.concatenate([-front[..., half_rot:], front[..., :half_rot]], axis=-1)
    return jnp.concatenate([front * cosine + turned * sine, tensor[..., ROT:]], axis=-1)


def unrotary(tensor, cosine, sine):
    half_rot = ROT // 2
    front = tensor[..., :ROT]
    turned = jnp.concatenate([-front[..., half_rot:], front[..., :half_rot]], axis=-1)
    return jnp.concatenate([front * cosine - turned * sine, tensor[..., ROT:]], axis=-1)


def tables(position_rows):
    freqs = 10000.0 ** (-jnp.arange(ROT // 2, dtype=jnp.float32) * 2.0 / ROT)
    angles = position_rows.T.astype(jnp.float32)[:, :, None] * freqs
    angles = jnp.concatenate([angles, angles], axis=-1)[:, :, None, :]
    return (jnp.cos(angles), jnp.sin(angles))


def attention_scores(queries, key_heads, allowed):
    scores = jnp.einsum(
        "qshe,kshe->shqk", queries, key_heads, preferred_element_type=jnp.float32
    ) * HEAD_WIDTH ** (-0.5)
    return jnp.where(allowed, scores, -1e30)


def forward_layer(layer_in, weights, context_rows):
    gain_vec, shift_vec, w_qkv, b_qkv, w_out, w_gate_up, down_weight = weights
    cosine, sine, allowed = context_rows
    normed = normalize(layer_in, gain_vec[0], shift_vec[0]).astype(jnp.bfloat16)
    normed_all = lax.all_gather(normed, "tp", axis=0, tiled=True)
    block_len, seq_count, width = normed_all.shape
    columns = w_qkv.shape[2]
    head_count = columns // HEAD_WIDTH
    mixed = (
        jnp.einsum("rsd,cde->crse", normed_all, w_qkv, preferred_element_type=jnp.float32)
        + b_qkv[:, None, None, :]
    )
    queries = rotary(
        mixed[0].reshape(block_len, seq_count, head_count, HEAD_WIDTH), cosine, sine
    ).astype(jnp.bfloat16)
    key_own = rotary(
        mixed[1].reshape(block_len, seq_count, head_count, HEAD_WIDTH), cosine, sine
    ).astype(jnp.bfloat16)
    key_own = key_own.reshape(block_len, seq_count, columns)
    value_own = mixed[2].astype(jnp.bfloat16)
    key_all, value_all = (
        lax.all_gather(key_own, "ctx", axis=0, tiled=True),
        lax.all_gather(value_own, "ctx", axis=0, tiled=True),
    )
    key_heads = key_all.reshape(key_all.shape[0], seq_count, head_count, HEAD_WIDTH)
    value_heads = value_all.reshape(value_all.shape[0], seq_count, head_count, HEAD_WIDTH)
    scores = attention_scores(queries, key_heads, allowed)
    top_score = jnp.max(scores, axis=-1, keepdims=True)
    log_total = top_score + jnp.log(jnp.sum(jnp.exp(scores - top_score), axis=-1, keepdims=True))
    probability = jnp.exp(scores - log_total)
    attended = jnp.einsum(
        "shqk,kshe->qshe",
        probability.astype(jnp.bfloat16),
        value_heads,
        preferred_element_type=jnp.float32,
    )
    attended = attended.astype(jnp.bfloat16).reshape(block_len, seq_count, columns)
    piece = attended
    hidden_state = layer_in + lax.psum_scatter(
        jnp.einsum("rse,ed->rsd", piece, w_out, preferred_element_type=jnp.float32).astype(
            jnp.bfloat16
        ),
        "tp",
        scatter_dimension=0,
        tiled=True,
    ).astype(jnp.float32)
    normed_two = normalize(hidden_state, gain_vec[1], shift_vec[1]).astype(jnp.bfloat16)
    normed_two_all = lax.all_gather(normed_two, "tp", axis=0, tiled=True)
    gate_up = jnp.einsum(
        "rsd,cdf->crsf", normed_two_all, w_gate_up, preferred_element_type=jnp.float32
    )
    gated_activation = (jax.nn.silu(gate_up[0]) * gate_up[1]).astype(jnp.bfloat16)
    piece = gated_activation
    layer_out = hidden_state + lax.psum_scatter(
        jnp.einsum("rsf,fd->rsd", piece, down_weight, preferred_element_type=jnp.float32).astype(
            jnp.bfloat16
        ),
        "tp",
        scatter_dimension=0,
        tiled=True,
    ).astype(jnp.float32)
    stored = (
        layer_in,
        normed_all,
        queries,
        key_all,
        value_all,
        log_total,
        attended,
        hidden_state,
        normed_two_all,
        gate_up,
    )
    return (layer_out, stored)


def backward_layer(grad_out, stored, weights, context_rows):
    gain_vec, shift_vec, w_qkv, b_qkv, w_out, w_gate_up, down_weight = weights
    cosine, sine, allowed = context_rows
    (
        layer_in,
        normed_all,
        queries,
        key_all,
        value_all,
        log_total,
        attended,
        hidden_state,
        normed_two_all,
        gate_up,
    ) = stored
    block_len, seq_count, columns = attended.shape
    head_count = columns // HEAD_WIDTH
    mlp_grad = lax.all_gather(grad_out.astype(jnp.bfloat16), "tp", axis=0, tiled=True)
    gate_part = gate_up[0]
    up_part = gate_up[1]
    sigma = jax.nn.sigmoid(gate_part)
    swish = gate_part * sigma
    gated_activation = (swish * up_part).astype(jnp.bfloat16)
    down_grad = jnp.einsum(
        "rsf,rsd->fd", gated_activation, mlp_grad, preferred_element_type=jnp.float32
    )
    act_grad = jnp.einsum("rsd,fd->rsf", mlp_grad, down_weight, preferred_element_type=jnp.float32)
    gate_up_grad = jnp.stack(
        [act_grad * up_part * sigma * (1.0 + gate_part * (1.0 - sigma)), act_grad * swish]
    ).astype(jnp.bfloat16)
    gu_grad = jnp.einsum(
        "rsd,crsf->cdf", normed_two_all, gate_up_grad, preferred_element_type=jnp.float32
    )
    piece = gate_up_grad
    two_grad = lax.psum_scatter(
        jnp.einsum("crsf,cdf->rsd", piece, w_gate_up, preferred_element_type=jnp.float32).astype(
            jnp.bfloat16
        ),
        "tp",
        scatter_dimension=0,
        tiled=True,
    ).astype(jnp.float32)
    hidden_grad, gain_two, shift_two = norm_back(hidden_state, two_grad, gain_vec[1])
    hidden_grad = grad_out + hidden_grad
    attn_grad = lax.all_gather(hidden_grad.astype(jnp.bfloat16), "tp", axis=0, tiled=True)
    out_grad = jnp.einsum("rse,rsd->ed", attended, attn_grad, preferred_element_type=jnp.float32)
    ctx_grad = jnp.einsum("rsd,ed->rse", attn_grad, w_out, preferred_element_type=jnp.float32)
    ctx_grad = ctx_grad.astype(jnp.bfloat16).reshape(block_len, seq_count, head_count, HEAD_WIDTH)
    key_heads = key_all.reshape(key_all.shape[0], seq_count, head_count, HEAD_WIDTH)
    value_heads = value_all.reshape(value_all.shape[0], seq_count, head_count, HEAD_WIDTH)
    scores = attention_scores(queries, key_heads, allowed)
    probability = jnp.exp(scores - log_total)
    value_grad = jnp.einsum(
        "shqk,qshe->kshe",
        probability.astype(jnp.bfloat16),
        ctx_grad,
        preferred_element_type=jnp.float32,
    )
    prob_grad = jnp.einsum(
        "qshe,kshe->shqk", ctx_grad, value_heads, preferred_element_type=jnp.float32
    )
    score_grad = probability * (
        prob_grad - jnp.sum(probability * prob_grad, axis=-1, keepdims=True)
    )
    score_grad = score_grad.astype(jnp.bfloat16)
    query_grad = jnp.einsum(
        "shqk,kshe->qshe", score_grad, key_heads, preferred_element_type=jnp.float32
    ) * HEAD_WIDTH ** (-0.5)
    key_grad = jnp.einsum(
        "shqk,qshe->kshe", score_grad, queries, preferred_element_type=jnp.float32
    ) * HEAD_WIDTH ** (-0.5)
    key_back, value_back = (
        lax.psum_scatter(
            key_grad.astype(jnp.bfloat16), "ctx", scatter_dimension=0, tiled=True
        ).astype(jnp.float32),
        lax.psum_scatter(
            value_grad.astype(jnp.bfloat16), "ctx", scatter_dimension=0, tiled=True
        ).astype(jnp.float32),
    )
    qkv_grad = jnp.stack(
        [
            unrotary(query_grad, cosine, sine).reshape(block_len, seq_count, columns),
            unrotary(key_back, cosine, sine).reshape(block_len, seq_count, columns),
            value_back.reshape(block_len, seq_count, columns),
        ]
    ).astype(jnp.bfloat16)
    bias_grad = jnp.sum(qkv_grad.astype(jnp.float32), axis=(1, 2))
    qkv_weight_grad = jnp.einsum(
        "rsd,crse->cde", normed_all, qkv_grad, preferred_element_type=jnp.float32
    )
    piece = qkv_grad
    one_grad = lax.psum_scatter(
        jnp.einsum("crse,cde->rsd", piece, w_qkv, preferred_element_type=jnp.float32).astype(
            jnp.bfloat16
        ),
        "tp",
        scatter_dimension=0,
        tiled=True,
    ).astype(jnp.float32)
    input_grad, gain_one, shift_one = norm_back(layer_in, one_grad, gain_vec[0])
    input_grad = hidden_grad + input_grad
    weight_terms = (qkv_weight_grad, out_grad, gu_grad, down_grad)
    return (
        input_grad,
        (
            weight_terms,
            jnp.stack([gain_one, gain_two]),
            jnp.stack([shift_one, shift_two]),
            bias_grad,
        ),
    )


def spread(terms, columns, tp_index):
    weight_terms, gain_terms, shift_terms, bias_terms = terms
    qkv_term, out_term, gu_term, down_term = weight_terms
    scattered = (
        lax.psum_scatter(
            qkv_term.astype(jnp.bfloat16), "ctx", scatter_dimension=1, tiled=True
        ).astype(jnp.float32),
        lax.psum_scatter(
            out_term.astype(jnp.bfloat16), "ctx", scatter_dimension=1, tiled=True
        ).astype(jnp.float32),
        lax.psum_scatter(
            gu_term.astype(jnp.bfloat16), "ctx", scatter_dimension=1, tiled=True
        ).astype(jnp.float32),
        lax.psum_scatter(
            down_term.astype(jnp.bfloat16), "ctx", scatter_dimension=1, tiled=True
        ).astype(jnp.float32),
    )
    bias_full = lax.dynamic_update_slice_in_dim(
        jnp.zeros((3, gain_terms.shape[1]), jnp.float32), bias_terms, tp_index * columns, 1
    )
    gain_part, shift_part, bias_part = (
        lax.psum_scatter(gain_terms, ("ctx", "tp"), scatter_dimension=1, tiled=True),
        lax.psum_scatter(shift_terms, ("ctx", "tp"), scatter_dimension=1, tiled=True),
        lax.psum_scatter(bias_full, ("ctx", "tp"), scatter_dimension=1, tiled=True),
    )
    return (tuple(scattered), gain_part, shift_part, bias_part)


def stepwise_device(
    tokens_in,
    cotangent,
    plan,
    positions,
    norm_gain,
    norm_shift,
    w_qkv,
    b_qkv,
    w_out,
    w_gate_up,
    down_weight,
):
    weights = (
        norm_gain[0],
        norm_shift[0],
        w_qkv[0],
        b_qkv[0],
        w_out[0],
        w_gate_up[0],
        down_weight[0],
    )
    micro_count = tokens_in.shape[0]
    local_row_slice = tokens_in.shape[1]
    width = tokens_in.shape[3]
    columns = w_qkv.shape[3]
    ff_local = w_gate_up.shape[3]
    tp_count = lax.axis_size("tp")
    ctx_count = lax.axis_size("ctx")
    block_len = local_row_slice * tp_count
    section_index = lax.axis_index("section")
    ctx_index = lax.axis_index("ctx")
    tp_index = lax.axis_index("tp")
    block_pos = lax.dynamic_slice_in_dim(positions, ctx_index * block_len, block_len, 1)
    cosine, sine = tables(block_pos)
    allowed = (positions[:, None, :] <= block_pos[:, :, None])[:, None]
    context_rows = (cosine, sine, allowed)
    zero_rows = jnp.zeros(tokens_in.shape[1:], jnp.bfloat16)

    def forward_step(carry, step_index):
        arriving = passed_along(carry, "section", 1)
        micro = jnp.clip(step_index, 0, micro_count - 1)
        fresh = lax.dynamic_index_in_dim(tokens_in, plan[micro], 0, keepdims=False)
        layer_in = jnp.where(section_index == 0, fresh, arriving).astype(jnp.float32)
        layer_out, stored = forward_layer(layer_in, weights, context_rows)
        sent = layer_out.astype(jnp.bfloat16)
        return (sent, (sent, stored))

    steps_all = jnp.arange(micro_count + 1, dtype=jnp.int32)
    unused, (outputs, stored_all) = lax.scan(forward_step, zero_rows, steps_all)
    share = width // ctx_count
    fine_share = width // (ctx_count * tp_count)
    totals = (
        (
            jnp.zeros((3, share, columns), jnp.float32),
            jnp.zeros((columns, share), jnp.float32),
            jnp.zeros((2, share, ff_local), jnp.float32),
            jnp.zeros((ff_local, share), jnp.float32),
        ),
        jnp.zeros((2, fine_share), jnp.float32),
        jnp.zeros((2, fine_share), jnp.float32),
        jnp.zeros((3, fine_share), jnp.float32),
    )

    def backward_step(carry, bundle):
        send_back, running = carry
        step_index, stored = bundle
        arriving = passed_along(send_back, "section", -1)
        micro = step_index - section_index
        valid_step = ((micro >= 0) & (micro < micro_count)).astype(jnp.float32)
        target = lax.dynamic_index_in_dim(
            cotangent, jnp.clip(micro, 0, micro_count - 1), 0, keepdims=False
        )
        grad_out = jnp.where(section_index == 1, target, arriving).astype(jnp.float32)
        input_grad, terms = backward_layer(grad_out, stored, weights, context_rows)
        terms = jax.tree.map(lambda tensor: tensor * valid_step, terms)
        terms = spread(terms, columns, tp_index)
        running = jax.tree.map(jnp.add, running, terms)
        sent = input_grad.astype(jnp.bfloat16)
        return ((sent, running), sent)

    (unused_back, totals), input_grads = lax.scan(
        backward_step, (zero_rows, totals), (steps_all, stored_all), reverse=True
    )
    weight_parts, gain_part, shift_part, bias_part = totals
    section_ends = jnp.where(section_index == 0, input_grads[:micro_count], outputs[1:])[None]
    return (
        section_ends,
        gain_part[None],
        shift_part[None],
        bias_part[None],
        weight_parts[0][None],
        weight_parts[1][None],
        weight_parts[2][None],
        weight_parts[3][None],
    )


def per_device(*arrays):
    chips = lax.axis_size("ctx") // 2 * lax.axis_size("tp")
    if lax.axis_size("section") == 2 and lax.axis_size("ctx") == 4 and arrays[0].shape[0] == chips:
        return bulk_device(*arrays)
    return stepwise_device(*arrays)


def solution(mesh):
    placed = (
        P(None, ("ctx", "tp"), None, None),
        P(None, ("ctx", "tp"), None, None),
        P(),
        P(),
        P("section", None, None),
        P("section", None, None),
        P("section", None, None, "tp"),
        P("section", None, "tp"),
        P("section", "tp", None),
        P("section", None, None, "tp"),
        P("section", "tp", None),
    )
    return jax.shard_map(
        per_device,
        mesh=mesh,
        in_specs=placed,
        out_specs=(
            P("section", None, ("ctx", "tp"), None, None),
            P("section", None, ("ctx", "tp")),
            P("section", None, ("ctx", "tp")),
            P("section", None, ("ctx", "tp")),
            P("section", None, "ctx", "tp"),
            P("section", "tp", "ctx"),
            P("section", None, "ctx", "tp"),
            P("section", "tp", "ctx"),
        ),
        check_vma=False,
    )
```

```python
import functools

import jax
import jax.numpy as jnp
from jax import lax
from jax.experimental import pallas as pl
from jax.experimental.layout import Layout, with_layout_constraint
from jax.experimental.pallas import tpu as pltpu
from jax.sharding import PartitionSpec as P

HEAD_WIDTH = 64
ROT = 16


def pair_routes(ctx_count):
    core = [(i, i ^ 1) for i in range(ctx_count)]
    across = [(i, (i + 2) % 4) for i in range(ctx_count)]
    return core, across


def ln_stats(stream):
    mean = jnp.mean(stream, axis=-1, keepdims=True)
    centre = stream - mean
    inv_std = lax.rsqrt(jnp.mean(centre * centre, axis=-1, keepdims=True) + 1e-05)
    return centre, inv_std


def ln(stream, gain_vec, shift_vec):
    centre, inv_std = ln_stats(stream)
    return (centre * inv_std * gain_vec + shift_vec).astype(jnp.bfloat16)


def ln_back(stream, grad_in, gain_vec):
    centre, inv_std = ln_stats(stream)
    unit = centre * inv_std
    scaled = grad_in * gain_vec
    result = inv_std * (
        scaled
        - jnp.mean(scaled, axis=-1, keepdims=True)
        - unit * jnp.mean(scaled * unit, axis=-1, keepdims=True)
    )
    return result, jnp.sum(grad_in * unit, axis=0), jnp.sum(grad_in, axis=0)


def rot_tables(pos_row):
    half = ROT // 2
    freqs = 10000.0 ** (-jnp.arange(half, dtype=jnp.float32) * 2.0 / ROT)
    angles = pos_row.astype(jnp.float32)[:, None] * freqs
    cosine, sine = jnp.cos(angles), jnp.sin(angles)
    rows = pos_row.shape[0]
    rest = HEAD_WIDTH - ROT
    zeros = jnp.zeros((rows, half), jnp.float32)
    cos_head = jnp.concatenate([cosine, cosine, jnp.ones((rows, rest), jnp.float32)], 1)
    low_head = jnp.concatenate([-sine, zeros, jnp.zeros((rows, rest), jnp.float32)], 1)
    high_head = jnp.concatenate([zeros, sine, jnp.zeros((rows, rest), jnp.float32)], 1)
    return tuple(jnp.concatenate([t, t], 1) for t in (cos_head, low_head, high_head))


def dot_t(a, b):
    return lax.dot_general(a, b, (((1,), (1,)), ((), ())), preferred_element_type=jnp.float32)


def dot_0(a, b):
    return lax.dot_general(a, b, (((0,), (0,)), ((), ())), preferred_element_type=jnp.float32)


def dot_n(a, b):
    return lax.dot_general(a, b, (((1,), (0,)), ((), ())), preferred_element_type=jnp.float32)


def chunked(x, chunk):
    half = x.shape[0] // 2
    pieces = []
    for i in range(half // chunk):
        pieces.append(x[i * chunk : (i + 1) * chunk])
        pieces.append(x[half + i * chunk : half + (i + 1) * chunk])
    return jnp.concatenate(pieces, axis=0)


def attn_fwd_kernel(heads, chunk, mixed, bias, cos_t, low_t, high_t, pos_c, pos_r, qkv, out, lse):
    rows = mixed.shape[0]
    half = rows // 2
    width = heads * HEAD_WIDTH
    half_rot = ROT // 2
    cosine, low, high = cos_t[...], low_t[...], high_t[...]
    for pair in range(heads // 2):
        parts = []
        for c in range(3):
            at = c * width + pair * 128
            x = mixed[:, at : at + 128] + bias[0, :, at : at + 128]
            if c < 2:
                x = x * cosine + pltpu.roll(x, 128 - half_rot, 1) * low + pltpu.roll(x, half_rot, 1) * high
            x = x.astype(jnp.bfloat16)
            qkv[:, at : at + 128] = x
            parts.append(chunked(x, chunk))
        query, key, value = parts
        query = query * jnp.bfloat16(HEAD_WIDTH ** (-0.5))
        for i in range(half // chunk):
            end = 2 * chunk * (i + 1)
            begin = end - 2 * chunk
            allowed = pos_r[:, begin:end] <= pos_c[begin:end, :]
            halves = []
            for h in range(2):
                lanes = slice(h * HEAD_WIDTH, (h + 1) * HEAD_WIDTH)
                q_h = query[begin:end, lanes]
                score = dot_t(q_h, key[:end, lanes])
                last = jnp.where(allowed, score[:, begin:], -1e30)
                score = last if i == 0 else jnp.concatenate([score[:, :begin], last], axis=1)
                top = jnp.max(score, axis=1, keepdims=True)
                prob = jnp.exp(score - top)
                total = jnp.sum(prob, axis=1, keepdims=True)
                lse[0, begin:end, 2 * pair + h : 2 * pair + h + 1] = top + jnp.log(total)
                mixed_values = dot_n(prob.astype(jnp.bfloat16), value[:end, lanes])
                halves.append(mixed_values / total)
            done = jnp.concatenate(halves, axis=1).astype(jnp.bfloat16)
            lanes = slice(pair * 128, pair * 128 + 128)
            out[i * chunk : (i + 1) * chunk, lanes] = done[:chunk]
            out[half + i * chunk : half + (i + 1) * chunk, lanes] = done[chunk:]


def attn_bwd_kernel(heads, chunk, qkv, lse, ctx, cos_t, low_t, high_t, pos_c, pos_r, grad, bias_grad, dk_s, dv_s):
    rows = qkv.shape[0]
    half = rows // 2
    width = heads * HEAD_WIDTH
    half_rot = ROT // 2
    cosine, low, high = cos_t[...], low_t[...], high_t[...]
    scale = HEAD_WIDTH ** (-0.5)

    def finish(c, pair, x):
        at = c * width + pair * 128
        if c < 2:
            x = x * scale
            x = x * cosine + pltpu.roll(x * high, 128 - half_rot, 1) + pltpu.roll(x * low, half_rot, 1)
        x = x.astype(jnp.bfloat16)
        grad[:, at : at + 128] = x
        bias_grad[0, :, at : at + 128] = jnp.sum(x.astype(jnp.float32), axis=0, keepdims=True)

    def unchunked(x):
        steps = half // chunk
        own = [x[2 * i * chunk : (2 * i + 1) * chunk] for i in range(steps)]
        other = [x[(2 * i + 1) * chunk : (2 * i + 2) * chunk] for i in range(steps)]
        return jnp.concatenate(own + other, axis=0)

    for pair in range(heads // 2):
        lanes2 = slice(pair * 128, pair * 128 + 128)
        query, key, value = (
            chunked(qkv[:, c * width + pair * 128 : c * width + pair * 128 + 128], chunk) for c in range(3)
        )
        query_s = query * jnp.bfloat16(scale)
        ctx_grad = chunked(ctx[:, lanes2], chunk)
        dk_s[...] = jnp.zeros_like(dk_s)
        dv_s[...] = jnp.zeros_like(dv_s)
        dq_parts = []
        for i in range(half // chunk):
            end = 2 * chunk * (i + 1)
            begin = end - 2 * chunk
            allowed = pos_c[begin:end, :] <= pos_r[:, begin:end]
            dq_h, dk_h, dv_h = [], [], []
            for h in range(2):
                lanes = slice(h * HEAD_WIDTH, (h + 1) * HEAD_WIDTH)
                score = dot_t(key[:end, lanes], query_s[begin:end, lanes])
                last = jnp.where(allowed, score[begin:, :], -1e30)
                score = last if i == 0 else jnp.concatenate([score[:begin, :], last], axis=0)
                prob = jnp.exp(score - lse[0, 2 * pair + h : 2 * pair + h + 1, begin:end])
                grad_h = ctx_grad[begin:end, lanes]
                dv_h.append(dot_n(prob.astype(jnp.bfloat16), grad_h))
                prob_grad = dot_t(value[:end, lanes], grad_h)
                delta = jnp.sum(prob * prob_grad, axis=0, keepdims=True)
                score_grad = (prob * (prob_grad - delta)).astype(jnp.bfloat16)
                dk_h.append(dot_n(score_grad, query[begin:end, lanes]))
                dq_h.append(dot_0(score_grad, key[:end, lanes]))
            dk_s[:end, :] += jnp.concatenate(dk_h, axis=1)
            dv_s[:end, :] += jnp.concatenate(dv_h, axis=1)
            dq_parts.append(jnp.concatenate(dq_h, axis=1))
        finish(0, pair, unchunked(jnp.concatenate(dq_parts, axis=0)))
        finish(1, pair, unchunked(dk_s[...]))
        finish(2, pair, unchunked(dv_s[...]))


VMEM_LIMIT = 56 * 1024 * 1024


def attn_fwd(mixed, bias, context, groups, chunk):
    rows, columns = mixed.shape
    block = columns // groups
    heads = block // (3 * HEAD_WIDTH)
    cos_t, low_t, high_t, pos_c, pos_r = context
    whole = lambda shape: pl.BlockSpec(shape, lambda g: (0, 0))
    return pl.pallas_call(
        functools.partial(attn_fwd_kernel, heads, chunk),
        grid=(groups,),
        in_specs=[
            pl.BlockSpec((rows, block), lambda g: (0, g)),
            pl.BlockSpec((1, 1, block), lambda g: (g, 0, 0)),
            whole((rows, 128)),
            whole((rows, 128)),
            whole((rows, 128)),
            whole((rows, 1)),
            whole((1, rows)),
        ],
        out_specs=[
            pl.BlockSpec((rows, block), lambda g: (0, g)),
            pl.BlockSpec((rows, block // 3), lambda g: (0, g)),
            pl.BlockSpec((1, rows, heads), lambda g: (g, 0, 0)),
        ],
        out_shape=[
            jax.ShapeDtypeStruct((rows, columns), jnp.bfloat16),
            jax.ShapeDtypeStruct((rows, columns // 3), jnp.bfloat16),
            jax.ShapeDtypeStruct((groups, rows, heads), jnp.float32),
        ],
        compiler_params=pltpu.CompilerParams(vmem_limit_bytes=VMEM_LIMIT),
        cost_estimate=pl.CostEstimate(
            flops=3 * rows * rows * columns // 3 * 4,
            bytes_accessed=rows * columns * 7,
            transcendentals=rows * rows * columns // (3 * HEAD_WIDTH),
        ),
    )(mixed, bias.reshape(groups, 1, block), cos_t, low_t, high_t, pos_c, pos_r)


def attn_bwd(qkv, lse, ctx_grad, context, groups, chunk):
    rows, columns = qkv.shape
    block = columns // groups
    heads = block // (3 * HEAD_WIDTH)
    cos_t, low_t, high_t, pos_c, pos_r = context
    whole = lambda shape: pl.BlockSpec(shape, lambda g: (0, 0))
    return pl.pallas_call(
        functools.partial(attn_bwd_kernel, heads, chunk),
        grid=(groups,),
        in_specs=[
            pl.BlockSpec((rows, block), lambda g: (0, g)),
            pl.BlockSpec((1, heads, rows), lambda g: (g, 0, 0)),
            pl.BlockSpec((rows, block // 3), lambda g: (0, g)),
            whole((rows, 128)),
            whole((rows, 128)),
            whole((rows, 128)),
            whole((rows, 1)),
            whole((1, rows)),
        ],
        out_specs=[
            pl.BlockSpec((rows, block), lambda g: (0, g)),
            pl.BlockSpec((1, 1, block), lambda g: (g, 0, 0)),
        ],
        out_shape=[
            jax.ShapeDtypeStruct((rows, columns), jnp.bfloat16),
            jax.ShapeDtypeStruct((groups, 1, block), jnp.float32),
        ],
        scratch_shapes=[pltpu.VMEM((rows, 128), jnp.float32), pltpu.VMEM((rows, 128), jnp.float32)],
        compiler_params=pltpu.CompilerParams(vmem_limit_bytes=VMEM_LIMIT),
        cost_estimate=pl.CostEstimate(
            flops=rows * columns,
            bytes_accessed=rows * columns,
            transcendentals=0,
        ),
    )(qkv, lse.swapaxes(1, 2), ctx_grad, cos_t, low_t, high_t, pos_c, pos_r)


def bulk_device(
    tokens_in,
    cotangent,
    plan,
    positions,
    norm_gain,
    norm_shift,
    w_qkv,
    b_qkv,
    w_out,
    w_gate_up,
    down_weight,
):
    tp_count = lax.axis_size("tp")
    ctx_count = lax.axis_size("ctx")
    section_index = lax.axis_index("section")
    ctx_index = lax.axis_index("ctx")
    side, core = ctx_index // 2, ctx_index % 2
    core_route, across_route = pair_routes(ctx_count)
    micro_count, slice_len, _, width = tokens_in.shape
    gain, shift = norm_gain[0], norm_shift[0]
    piece = slice_len // 2
    rows = micro_count * slice_len * 2
    own_rows = rows // 2
    half_width = width // 2
    columns = w_qkv.shape[3] // 2
    hidden = w_gate_up.shape[3] // 2
    first = section_index == 0

    ordered = jnp.stack(
        [lax.dynamic_index_in_dim(tokens_in, plan[m], 0, keepdims=False)[:, 0] for m in range(micro_count)]
    )
    fresh = jnp.where(first, ordered, cotangent[:, :, 0])
    fresh = fresh.reshape(ctx_count // 2, tp_count, 2, piece, width).transpose(0, 2, 1, 3, 4)
    fresh = fresh.reshape(ctx_count * tp_count, piece, width)
    inbound = lax.all_to_all(fresh, ("ctx", "tp"), 0, 0, tiled=True).reshape(own_rows, width)

    pos = positions.reshape(-1, 2, piece)
    pos = jnp.concatenate(
        [
            lax.dynamic_index_in_dim(pos, core, 1, False).reshape(-1),
            lax.dynamic_index_in_dim(pos, 1 - core, 1, False).reshape(-1),
        ]
    )
    chunk = min(128, own_rows)
    chunk_pos = chunked(pos, chunk)
    context = (*rot_tables(pos), chunk_pos[:, None], chunk_pos[None, :])

    tp_index = lax.axis_index("tp")

    def turned_by_tp(shards, axis=0):
        count = shards.shape[axis] // tp_count
        twice = jnp.concatenate([shards, shards], axis=axis)
        start = lax.rem(tp_count - tp_index, tp_count) * count
        return lax.dynamic_slice_in_dim(twice, start, tp_count * count, axis)

    def after(x, *others):
        return lax.optimization_barrier((x, *others))[0]

    own_parts, across_parts = [], []

    def gathered(block_of):
        block, held = block_of(side), block_of(1 - side)
        count = block.shape[0]
        step = len(own_parts)
        if step == 2:
            block = after(block, own_parts[0], across_parts[0], inbound)
        elif step > 2:
            block = after(block, own_parts[step - 2], across_parts[step - 3])
        own = lax.all_gather(block, "tp", axis=0, tiled=True)
        wanted = [
            lax.dynamic_slice_in_dim(own, lax.rem(tp_index + p, tp_count) * count, count, 0)
            for p in range(1, tp_count)
        ]
        arriving = lax.ppermute(jnp.concatenate(wanted, axis=0), "ctx", across_route)
        own_parts.append(own)
        across_parts.append(arriving)
        other = turned_by_tp(jnp.concatenate([held, arriving], axis=0))
        return jnp.where(
            side == 0, jnp.concatenate([own, other], axis=1), jnp.concatenate([other, own], axis=1)
        )

    def qkv_block(half):
        block = lax.dynamic_slice(w_qkv[0], (0, half * half_width, core * columns), (3, half_width, columns))
        return block.transpose(0, 2, 1).reshape(3 * columns, half_width)

    def out_block(half):
        return lax.dynamic_slice(w_out[0], (core * columns, half * half_width), (columns, half_width))

    def gu_block(which, half):
        block = lax.dynamic_slice(
            w_gate_up[0], (which, half * half_width, core * hidden), (1, half_width, hidden)
        )
        return block[0].T

    def down_block(part, half):
        start = core * hidden + part * (hidden // 2)
        return lax.dynamic_slice(down_weight[0], (start, half * half_width), (hidden // 2, half_width))

    wt_out = gathered(out_block)
    wt_qkv = gathered(qkv_block)
    wt_gu = jnp.concatenate([gathered(functools.partial(gu_block, w)) for w in range(2)], axis=0)
    wt_down = jnp.concatenate(
        [
            gathered(functools.partial(down_block, part)).reshape(tp_count, hidden // 2, width)
            for part in range(2)
        ],
        axis=1,
    ).reshape(tp_count * hidden, width)
    bias_own = lax.dynamic_slice_in_dim(b_qkv[0], core * columns, columns, 1).reshape(1, 3 * columns)
    bias = [bias_own]
    for p in range(1, tp_count):
        ring = [((i + p) % tp_count, i) for i in range(tp_count)]
        bias.append(lax.ppermute(bias_own, "tp", ring))
    bias = turned_by_tp(jnp.concatenate(bias, axis=0))
    ff = wt_down.shape[0]

    def both(own):
        return jnp.concatenate([own, lax.ppermute(own, "ctx", core_route)], axis=0)

    def summed(a, weight, parts=1):
        step = own_rows // parts
        spans = [slice(i * step, (i + 1) * step) for i in range(parts)]
        others = [dot_n(a[own_rows:][span], weight).astype(jnp.bfloat16) for span in spans]
        arriving = [lax.ppermute(other, "ctx", core_route) for other in others]
        own = [dot_n(a[:own_rows][span], weight) for span in spans]
        return [x + y.astype(jnp.float32) for x, y in zip(own, arriving)]

    def split(x, parts):
        step = x.shape[0] // parts
        return [x[i * step : (i + 1) * step] for i in range(parts)]

    def over_x(parts, route):
        return jnp.concatenate([lax.ppermute(part, "section", route) for part in parts], axis=0)

    def forward(stream, parts):
        normed = both(ln(stream, gain[0], shift[0]))
        mixed = dot_t(normed, wt_qkv)
        qkv, attended, lse = attn_fwd(mixed, bias, context, tp_count, chunk)
        hidden_state = stream + summed(attended, wt_out)[0]
        normed_two = both(ln(hidden_state, gain[1], shift[1]))
        gate_up = dot_t(normed_two, wt_gu)
        gate, up = gate_up[:, :ff], gate_up[:, ff:]
        activation = (jax.nn.silu(gate) * up).astype(jnp.bfloat16)
        out = [
            (x + y).astype(jnp.bfloat16)
            for x, y in zip(split(hidden_state, parts), summed(activation, wt_down, parts))
        ]
        return out, (stream, normed, (qkv, lse), attended, hidden_state, normed_two, gate_up, activation)

    def far_near(right):
        far = lax.dynamic_slice_in_dim(right, (1 - side) * half_width, half_width, 1)
        near = lax.dynamic_slice_in_dim(right, side * half_width, half_width, 1)
        return far, near

    def far_term(left, right):
        return dot_0(left, far_near(right)[0]).astype(jnp.bfloat16)

    def near_total(left, right, arriving, *others):
        near = far_near(right)[1]
        if others:
            near = after(near, *others)
        return (dot_0(left, near) + arriving.astype(jnp.float32)).astype(jnp.bfloat16)

    def across(term, *others):
        return lax.ppermute(after(term, *others) if others else term, "ctx", across_route)

    def over_tp(term):
        return lax.psum_scatter(term, "tp", scatter_dimension=0, tiled=True)

    together = lax.optimization_barrier

    def part_of(x, i, parts, axis):
        shard = x.shape[axis] // tp_count
        step = shard // parts
        return jnp.concatenate(
            [
                lax.slice_in_dim(x, z * shard + i * step, z * shard + (i + 1) * step, axis=axis)
                for z in range(tp_count)
            ],
            axis=axis,
        )

    def mlp_back(act_grad, gate_up):
        gate, up = gate_up[:, :ff], gate_up[:, ff:]
        sigma = jax.nn.sigmoid(gate)
        gate_grad = (act_grad * up * sigma * (1.0 + gate * (1.0 - sigma))).astype(jnp.bfloat16)
        up_grad = (act_grad * gate * sigma).astype(jnp.bfloat16)
        return gate_grad, up_grad

    def two_dot(gate_grad, up_grad):
        return dot_n(jnp.concatenate([gate_grad, up_grad], axis=1), wt_gu)

    def from_core(term):
        return lax.ppermute(term.astype(jnp.bfloat16), "ctx", core_route).astype(jnp.float32)

    def backward(grad_out, stored, wait):
        stream, normed, (qkv, lse), attended, hidden_state, normed_two, gate_up, activation = stored
        gate_grad, up_grad = mlp_back(dot_t(both(grad_out), wt_down), gate_up)
        gu_grad = jnp.concatenate([gate_grad, up_grad], axis=1)
        two_grad = summed(gu_grad, wt_gu)[0]
        hidden_grad = grad_out.astype(jnp.float32) + ln_back(hidden_state, two_grad, gain[1])[0]
        ctx_grad = dot_t(both(hidden_grad.astype(jnp.bfloat16)), wt_out).astype(jnp.bfloat16)
        qkv_grad, _ = attn_bwd(qkv, lse, ctx_grad, context, tp_count, chunk)
        final_other = dot_n(activation[own_rows:], wt_down).astype(jnp.bfloat16)
        qkv_grad, final_other = together((qkv_grad, final_other))
        one_grad = summed(after(qkv_grad, wait), wt_qkv)[0]
        return (hidden_grad + ln_back(stream, one_grad, gain[0])[0]).astype(jnp.bfloat16), final_other

    def settled(term):
        share = half_width // 2
        away = lax.dynamic_slice_in_dim(term, (1 - core) * share, share, term.ndim - 1)
        kept = lax.dynamic_slice_in_dim(term, core * share, share, term.ndim - 1)
        got = lax.ppermute(away, "ctx", core_route)
        axis = term.ndim - 2
        return jnp.where(
            core == 0, jnp.concatenate([kept, got], axis), jnp.concatenate([got, kept], axis)
        ).astype(jnp.float32)

    def vector_sums(small):
        gain_terms, shift_terms, bias_terms = small
        bias_terms = bias_terms.reshape(tp_count, 3, columns).transpose(1, 0, 2)[:, :, None]
        bias_full = jnp.where(
            (jnp.arange(2) == core)[None, None, :, None], bias_terms, 0.0
        ).reshape(3, tp_count * 2 * columns)
        vectors = jnp.concatenate([gain_terms, shift_terms, bias_full], axis=0)
        share = width // (ctx_count * tp_count)
        vectors = vectors.reshape(-1, ctx_count * tp_count, share).transpose(1, 0, 2)
        return jnp.sum(lax.all_to_all(vectors, ("ctx", "tp"), 0, 0, tiled=True), axis=0).reshape(-1, share)

    def last_backward(grad_out, stored, final_out, act_both):
        stream, normed, (qkv, lse), attended, hidden_state, normed_two, gate_up, _ = stored
        grad_f32 = grad_out.astype(jnp.float32)
        far_grad, near_grad = far_near(grad_out)
        grad_across = across(far_grad)
        mlp_grad = both(grad_out)
        gate_grad, up_grad = mlp_back(dot_t(mlp_grad, wt_down), gate_up)
        far_gate = far_term(gate_grad, normed_two)

        grad_across, far_gate, gate_grad, up_grad = together((grad_across, far_gate, gate_grad, up_grad))
        far_gate_a, far_gate_b = split(far_gate, 2)
        arriving = across(far_gate_a)
        gu_grad = jnp.concatenate([gate_grad, up_grad], axis=1)
        grad_both = jnp.concatenate([both(near_grad), both(grad_across)], axis=0)
        down_total = dot_0(act_both, grad_both).astype(jnp.bfloat16)
        two_other = dot_n(gu_grad[own_rows:], wt_gu).astype(jnp.bfloat16)

        arriving, far_gate_b, two_other, gu_grad, down_total, gate_grad, up_grad = together(
            (arriving, far_gate_b, two_other, gu_grad, down_total, gate_grad, up_grad)
        )
        arriving_gate = jnp.concatenate([arriving, across(far_gate_b)], axis=0)
        sum_down = over_tp(down_total)
        two_grad = dot_n(gu_grad[:own_rows], wt_gu) + lax.ppermute(two_other, "ctx", core_route).astype(jnp.float32)
        result, gain_two, shift_two = ln_back(hidden_state, two_grad, gain[1])
        hidden_grad = grad_f32 + result
        attn_grad = both(hidden_grad.astype(jnp.bfloat16))
        far_up_a, far_up_b = (far_term(x, normed_two) for x in jnp.split(up_grad, 2, axis=1))

        arriving_gate, far_up_a, far_up_b, gate_grad, attn_grad, hidden_grad = together(
            (arriving_gate, far_up_a, far_up_b, gate_grad, attn_grad, hidden_grad)
        )
        arriving = across(far_up_a)
        sum_gate = over_tp(near_total(gate_grad, normed_two, arriving_gate))
        ctx_grad = dot_t(attn_grad, wt_out).astype(jnp.bfloat16)

        arriving, far_up_b, ctx_grad = together((arriving, far_up_b, ctx_grad))
        arriving_up = jnp.concatenate([arriving, across(far_up_b)], axis=0)
        qkv_grad, bias_grad = attn_bwd(qkv, lse, ctx_grad, context, tp_count, chunk)
        qkv_a, qkv_b = (part_of(qkv_grad, i, 2, 1) for i in range(2))

        arriving_up, qkv_a, qkv_b, qkv_grad, up_grad, attn_grad = together(
            (arriving_up, qkv_a, qkv_b, qkv_grad, up_grad, attn_grad)
        )
        arriving = across(far_term(qkv_a, normed))
        sum_up = over_tp(near_total(up_grad, normed_two, arriving_up))
        far_b = far_term(qkv_b, normed)
        one_other = dot_n(qkv_grad[own_rows:], wt_qkv).astype(jnp.bfloat16)

        arriving, far_b, one_other, qkv_grad, qkv_a, qkv_b, attn_grad = together(
            (arriving, far_b, one_other, qkv_grad, qkv_a, qkv_b, attn_grad)
        )
        arriving_b = across(far_b)
        sum_qkv_a = over_tp(near_total(qkv_a, normed, arriving))
        one_grad = dot_n(qkv_grad[:own_rows], wt_qkv) + lax.ppermute(one_other, "ctx", core_route).astype(jnp.float32)
        result, gain_one, shift_one = ln_back(stream, one_grad, gain[0])
        input_grad = (hidden_grad + result).astype(jnp.bfloat16)
        ends = jnp.where(first, input_grad, final_out)
        far_out = far_term(attended, attn_grad)
        small = vector_sums((jnp.stack([gain_one, gain_two]), jnp.stack([shift_one, shift_two]), bias_grad))

        arriving_b, far_out, ends, qkv_b, small = together((arriving_b, far_out, ends, qkv_b, small))
        arriving_out = across(far_out)
        ends = lax.all_to_all(
            ends.reshape(ctx_count * tp_count, piece, width), ("ctx", "tp"), 0, 0, tiled=True
        )
        sum_qkv_b = over_tp(near_total(qkv_b, normed, arriving_b))
        grad_gu = jnp.stack([settled(sum_gate).T, settled(sum_up).T])[None]
        done = (settled(sum_down)[None], with_layout_constraint(grad_gu, Layout((0, 1, 2, 3))))

        arriving_out, attn_grad, done, ends = together((arriving_out, attn_grad, done, ends))
        sum_out = over_tp(near_total(attended, attn_grad, arriving_out))
        sum_qkv = jnp.concatenate([sum_qkv_a, sum_qkv_b], axis=0)
        grads = (*done, settled(sum_out), settled(sum_qkv.reshape(3, columns, half_width)))
        return ends, small, grads

    sent, _ = forward(inbound.astype(jnp.float32), 2)
    arriving = over_x(sent, [(0, 1)])
    _, stored = forward(jnp.where(first, inbound, arriving).astype(jnp.float32), 1)
    act_across = across(stored[7])
    sent_back, final_other = backward(inbound, stored, act_across)
    final_out = stored[4] + dot_n(stored[7][:own_rows], wt_down) + from_core(final_other)
    arriving_back = over_x([sent_back], [(1, 0)])
    arriving_back, final_out, act_both = together(
        (arriving_back, final_out.astype(jnp.bfloat16), jnp.concatenate([stored[7], act_across], axis=0))
    )
    grad_out = jnp.where(first, arriving_back, inbound)
    ends, vectors, grads = last_backward(grad_out, stored, final_out, act_both)
    grad_down, grad_gu, grad_out_w, grad_qkv = grads

    ends = ends.reshape(ctx_count // 2, 2, tp_count, piece, width).transpose(0, 2, 1, 3, 4)
    ends = ends.reshape(micro_count, slice_len, 1, width)
    return (
        ends[None],
        vectors[None, :2],
        vectors[None, 2:4],
        vectors[None, 4:],
        grad_qkv.transpose(0, 2, 1)[None],
        grad_out_w[None],
        grad_gu,
        grad_down,
    )


def passed_along(block, axis, distance):
    devices = range(lax.axis_size(axis))
    route = [(i - distance, i) for i in devices if i - distance in devices]
    return lax.ppermute(block, axis, route)


def normalize(stream, gain_vec, shift_vec):
    centre = stream - jnp.mean(stream, axis=-1, keepdims=True)
    spread = jnp.mean(centre * centre, axis=-1, keepdims=True)
    return centre * lax.rsqrt(spread + 1e-05) * gain_vec + shift_vec


def norm_back(stream, grad_in, gain_vec):
    centre = stream - jnp.mean(stream, axis=-1, keepdims=True)
    inv_std = lax.rsqrt(jnp.mean(centre * centre, axis=-1, keepdims=True) + 1e-05)
    unit = centre * inv_std
    scaled = grad_in * gain_vec
    result = inv_std * (
        scaled
        - jnp.mean(scaled, axis=-1, keepdims=True)
        - unit * jnp.mean(scaled * unit, axis=-1, keepdims=True)
    )
    return (result, jnp.sum(grad_in * unit, axis=(0, 1)), jnp.sum(grad_in, axis=(0, 1)))


def rotary(tensor, cosine, sine):
    half_rot = ROT // 2
    front = tensor[..., :ROT]
    turned = jnp.concatenate([-front[..., half_rot:], front[..., :half_rot]], axis=-1)
    return jnp.concatenate([front * cosine + turned * sine, tensor[..., ROT:]], axis=-1)


def unrotary(tensor, cosine, sine):
    half_rot = ROT // 2
    front = tensor[..., :ROT]
    turned = jnp.concatenate([-front[..., half_rot:], front[..., :half_rot]], axis=-1)
    return jnp.concatenate([front * cosine - turned * sine, tensor[..., ROT:]], axis=-1)


def tables(position_rows):
    freqs = 10000.0 ** (-jnp.arange(ROT // 2, dtype=jnp.float32) * 2.0 / ROT)
    angles = position_rows.T.astype(jnp.float32)[:, :, None] * freqs
    angles = jnp.concatenate([angles, angles], axis=-1)[:, :, None, :]
    return (jnp.cos(angles), jnp.sin(angles))


def attention_scores(queries, key_heads, allowed):
    scores = jnp.einsum(
        "qshe,kshe->shqk", queries, key_heads, preferred_element_type=jnp.float32
    ) * HEAD_WIDTH ** (-0.5)
    return jnp.where(allowed, scores, -1e30)


def forward_layer(layer_in, weights, context_rows):
    gain_vec, shift_vec, w_qkv, b_qkv, w_out, w_gate_up, down_weight = weights
    cosine, sine, allowed = context_rows
    normed = normalize(layer_in, gain_vec[0], shift_vec[0]).astype(jnp.bfloat16)
    normed_all = lax.all_gather(normed, "tp", axis=0, tiled=True)
    block_len, seq_count, width = normed_all.shape
    columns = w_qkv.shape[2]
    head_count = columns // HEAD_WIDTH
    mixed = (
        jnp.einsum("rsd,cde->crse", normed_all, w_qkv, preferred_element_type=jnp.float32)
        + b_qkv[:, None, None, :]
    )
    queries = rotary(
        mixed[0].reshape(block_len, seq_count, head_count, HEAD_WIDTH), cosine, sine
    ).astype(jnp.bfloat16)
    key_own = rotary(
        mixed[1].reshape(block_len, seq_count, head_count, HEAD_WIDTH), cosine, sine
    ).astype(jnp.bfloat16)
    key_own = key_own.reshape(block_len, seq_count, columns)
    value_own = mixed[2].astype(jnp.bfloat16)
    key_all, value_all = (
        lax.all_gather(key_own, "ctx", axis=0, tiled=True),
        lax.all_gather(value_own, "ctx", axis=0, tiled=True),
    )
    key_heads = key_all.reshape(key_all.shape[0], seq_count, head_count, HEAD_WIDTH)
    value_heads = value_all.reshape(value_all.shape[0], seq_count, head_count, HEAD_WIDTH)
    scores = attention_scores(queries, key_heads, allowed)
    top_score = jnp.max(scores, axis=-1, keepdims=True)
    log_total = top_score + jnp.log(jnp.sum(jnp.exp(scores - top_score), axis=-1, keepdims=True))
    probability = jnp.exp(scores - log_total)
    attended = jnp.einsum(
        "shqk,kshe->qshe",
        probability.astype(jnp.bfloat16),
        value_heads,
        preferred_element_type=jnp.float32,
    )
    attended = attended.astype(jnp.bfloat16).reshape(block_len, seq_count, columns)
    piece = attended
    hidden_state = layer_in + lax.psum_scatter(
        jnp.einsum("rse,ed->rsd", piece, w_out, preferred_element_type=jnp.float32).astype(
            jnp.bfloat16
        ),
        "tp",
        scatter_dimension=0,
        tiled=True,
    ).astype(jnp.float32)
    normed_two = normalize(hidden_state, gain_vec[1], shift_vec[1]).astype(jnp.bfloat16)
    normed_two_all = lax.all_gather(normed_two, "tp", axis=0, tiled=True)
    gate_up = jnp.einsum(
        "rsd,cdf->crsf", normed_two_all, w_gate_up, preferred_element_type=jnp.float32
    )
    gated_activation = (jax.nn.silu(gate_up[0]) * gate_up[1]).astype(jnp.bfloat16)
    piece = gated_activation
    layer_out = hidden_state + lax.psum_scatter(
        jnp.einsum("rsf,fd->rsd", piece, down_weight, preferred_element_type=jnp.float32).astype(
            jnp.bfloat16
        ),
        "tp",
        scatter_dimension=0,
        tiled=True,
    ).astype(jnp.float32)
    stored = (
        layer_in,
        normed_all,
        queries,
        key_all,
        value_all,
        log_total,
        attended,
        hidden_state,
        normed_two_all,
        gate_up,
    )
    return (layer_out, stored)


def backward_layer(grad_out, stored, weights, context_rows):
    gain_vec, shift_vec, w_qkv, b_qkv, w_out, w_gate_up, down_weight = weights
    cosine, sine, allowed = context_rows
    (
        layer_in,
        normed_all,
        queries,
        key_all,
        value_all,
        log_total,
        attended,
        hidden_state,
        normed_two_all,
        gate_up,
    ) = stored
    block_len, seq_count, columns = attended.shape
    head_count = columns // HEAD_WIDTH
    mlp_grad = lax.all_gather(grad_out.astype(jnp.bfloat16), "tp", axis=0, tiled=True)
    gate_part = gate_up[0]
    up_part = gate_up[1]
    sigma = jax.nn.sigmoid(gate_part)
    swish = gate_part * sigma
    gated_activation = (swish * up_part).astype(jnp.bfloat16)
    down_grad = jnp.einsum(
        "rsf,rsd->fd", gated_activation, mlp_grad, preferred_element_type=jnp.float32
    )
    act_grad = jnp.einsum("rsd,fd->rsf", mlp_grad, down_weight, preferred_element_type=jnp.float32)
    gate_up_grad = jnp.stack(
        [act_grad * up_part * sigma * (1.0 + gate_part * (1.0 - sigma)), act_grad * swish]
    ).astype(jnp.bfloat16)
    gu_grad = jnp.einsum(
        "rsd,crsf->cdf", normed_two_all, gate_up_grad, preferred_element_type=jnp.float32
    )
    piece = gate_up_grad
    two_grad = lax.psum_scatter(
        jnp.einsum("crsf,cdf->rsd", piece, w_gate_up, preferred_element_type=jnp.float32).astype(
            jnp.bfloat16
        ),
        "tp",
        scatter_dimension=0,
        tiled=True,
    ).astype(jnp.float32)
    hidden_grad, gain_two, shift_two = norm_back(hidden_state, two_grad, gain_vec[1])
    hidden_grad = grad_out + hidden_grad
    attn_grad = lax.all_gather(hidden_grad.astype(jnp.bfloat16), "tp", axis=0, tiled=True)
    out_grad = jnp.einsum("rse,rsd->ed", attended, attn_grad, preferred_element_type=jnp.float32)
    ctx_grad = jnp.einsum("rsd,ed->rse", attn_grad, w_out, preferred_element_type=jnp.float32)
    ctx_grad = ctx_grad.astype(jnp.bfloat16).reshape(block_len, seq_count, head_count, HEAD_WIDTH)
    key_heads = key_all.reshape(key_all.shape[0], seq_count, head_count, HEAD_WIDTH)
    value_heads = value_all.reshape(value_all.shape[0], seq_count, head_count, HEAD_WIDTH)
    scores = attention_scores(queries, key_heads, allowed)
    probability = jnp.exp(scores - log_total)
    value_grad = jnp.einsum(
        "shqk,qshe->kshe",
        probability.astype(jnp.bfloat16),
        ctx_grad,
        preferred_element_type=jnp.float32,
    )
    prob_grad = jnp.einsum(
        "qshe,kshe->shqk", ctx_grad, value_heads, preferred_element_type=jnp.float32
    )
    score_grad = probability * (
        prob_grad - jnp.sum(probability * prob_grad, axis=-1, keepdims=True)
    )
    score_grad = score_grad.astype(jnp.bfloat16)
    query_grad = jnp.einsum(
        "shqk,kshe->qshe", score_grad, key_heads, preferred_element_type=jnp.float32
    ) * HEAD_WIDTH ** (-0.5)
    key_grad = jnp.einsum(
        "shqk,qshe->kshe", score_grad, queries, preferred_element_type=jnp.float32
    ) * HEAD_WIDTH ** (-0.5)
    key_back, value_back = (
        lax.psum_scatter(
            key_grad.astype(jnp.bfloat16), "ctx", scatter_dimension=0, tiled=True
        ).astype(jnp.float32),
        lax.psum_scatter(
            value_grad.astype(jnp.bfloat16), "ctx", scatter_dimension=0, tiled=True
        ).astype(jnp.float32),
    )
    qkv_grad = jnp.stack(
        [
            unrotary(query_grad, cosine, sine).reshape(block_len, seq_count, columns),
            unrotary(key_back, cosine, sine).reshape(block_len, seq_count, columns),
            value_back.reshape(block_len, seq_count, columns),
        ]
    ).astype(jnp.bfloat16)
    bias_grad = jnp.sum(qkv_grad.astype(jnp.float32), axis=(1, 2))
    qkv_weight_grad = jnp.einsum(
        "rsd,crse->cde", normed_all, qkv_grad, preferred_element_type=jnp.float32
    )
    piece = qkv_grad
    one_grad = lax.psum_scatter(
        jnp.einsum("crse,cde->rsd", piece, w_qkv, preferred_element_type=jnp.float32).astype(
            jnp.bfloat16
        ),
        "tp",
        scatter_dimension=0,
        tiled=True,
    ).astype(jnp.float32)
    input_grad, gain_one, shift_one = norm_back(layer_in, one_grad, gain_vec[0])
    input_grad = hidden_grad + input_grad
    weight_terms = (qkv_weight_grad, out_grad, gu_grad, down_grad)
    return (
        input_grad,
        (
            weight_terms,
            jnp.stack([gain_one, gain_two]),
            jnp.stack([shift_one, shift_two]),
            bias_grad,
        ),
    )


def spread(terms, columns, tp_index):
    weight_terms, gain_terms, shift_terms, bias_terms = terms
    qkv_term, out_term, gu_term, down_term = weight_terms
    scattered = (
        lax.psum_scatter(
            qkv_term.astype(jnp.bfloat16), "ctx", scatter_dimension=1, tiled=True
        ).astype(jnp.float32),
        lax.psum_scatter(
            out_term.astype(jnp.bfloat16), "ctx", scatter_dimension=1, tiled=True
        ).astype(jnp.float32),
        lax.psum_scatter(
            gu_term.astype(jnp.bfloat16), "ctx", scatter_dimension=1, tiled=True
        ).astype(jnp.float32),
        lax.psum_scatter(
            down_term.astype(jnp.bfloat16), "ctx", scatter_dimension=1, tiled=True
        ).astype(jnp.float32),
    )
    bias_full = lax.dynamic_update_slice_in_dim(
        jnp.zeros((3, gain_terms.shape[1]), jnp.float32), bias_terms, tp_index * columns, 1
    )
    gain_part, shift_part, bias_part = (
        lax.psum_scatter(gain_terms, ("ctx", "tp"), scatter_dimension=1, tiled=True),
        lax.psum_scatter(shift_terms, ("ctx", "tp"), scatter_dimension=1, tiled=True),
        lax.psum_scatter(bias_full, ("ctx", "tp"), scatter_dimension=1, tiled=True),
    )
    return (tuple(scattered), gain_part, shift_part, bias_part)


def stepwise_device(
    tokens_in,
    cotangent,
    plan,
    positions,
    norm_gain,
    norm_shift,
    w_qkv,
    b_qkv,
    w_out,
    w_gate_up,
    down_weight,
):
    weights = (
        norm_gain[0],
        norm_shift[0],
        w_qkv[0],
        b_qkv[0],
        w_out[0],
        w_gate_up[0],
        down_weight[0],
    )
    micro_count = tokens_in.shape[0]
    local_row_slice = tokens_in.shape[1]
    width = tokens_in.shape[3]
    columns = w_qkv.shape[3]
    ff_local = w_gate_up.shape[3]
    tp_count = lax.axis_size("tp")
    ctx_count = lax.axis_size("ctx")
    block_len = local_row_slice * tp_count
    section_index = lax.axis_index("section")
    ctx_index = lax.axis_index("ctx")
    tp_index = lax.axis_index("tp")
    block_pos = lax.dynamic_slice_in_dim(positions, ctx_index * block_len, block_len, 1)
    cosine, sine = tables(block_pos)
    allowed = (positions[:, None, :] <= block_pos[:, :, None])[:, None]
    context_rows = (cosine, sine, allowed)
    zero_rows = jnp.zeros(tokens_in.shape[1:], jnp.bfloat16)

    def forward_step(carry, step_index):
        arriving = passed_along(carry, "section", 1)
        micro = jnp.clip(step_index, 0, micro_count - 1)
        fresh = lax.dynamic_index_in_dim(tokens_in, plan[micro], 0, keepdims=False)
        layer_in = jnp.where(section_index == 0, fresh, arriving).astype(jnp.float32)
        layer_out, stored = forward_layer(layer_in, weights, context_rows)
        sent = layer_out.astype(jnp.bfloat16)
        return (sent, (sent, stored))

    steps_all = jnp.arange(micro_count + 1, dtype=jnp.int32)
    unused, (outputs, stored_all) = lax.scan(forward_step, zero_rows, steps_all)
    share = width // ctx_count
    fine_share = width // (ctx_count * tp_count)
    totals = (
        (
            jnp.zeros((3, share, columns), jnp.float32),
            jnp.zeros((columns, share), jnp.float32),
            jnp.zeros((2, share, ff_local), jnp.float32),
            jnp.zeros((ff_local, share), jnp.float32),
        ),
        jnp.zeros((2, fine_share), jnp.float32),
        jnp.zeros((2, fine_share), jnp.float32),
        jnp.zeros((3, fine_share), jnp.float32),
    )

    def backward_step(carry, bundle):
        send_back, running = carry
        step_index, stored = bundle
        arriving = passed_along(send_back, "section", -1)
        micro = step_index - section_index
        valid_step = ((micro >= 0) & (micro < micro_count)).astype(jnp.float32)
        target = lax.dynamic_index_in_dim(
            cotangent, jnp.clip(micro, 0, micro_count - 1), 0, keepdims=False
        )
        grad_out = jnp.where(section_index == 1, target, arriving).astype(jnp.float32)
        input_grad, terms = backward_layer(grad_out, stored, weights, context_rows)
        terms = jax.tree.map(lambda tensor: tensor * valid_step, terms)
        terms = spread(terms, columns, tp_index)
        running = jax.tree.map(jnp.add, running, terms)
        sent = input_grad.astype(jnp.bfloat16)
        return ((sent, running), sent)

    (unused_back, totals), input_grads = lax.scan(
        backward_step, (zero_rows, totals), (steps_all, stored_all), reverse=True
    )
    weight_parts, gain_part, shift_part, bias_part = totals
    section_ends = jnp.where(section_index == 0, input_grads[:micro_count], outputs[1:])[None]
    return (
        section_ends,
        gain_part[None],
        shift_part[None],
        bias_part[None],
        weight_parts[0][None],
        weight_parts[1][None],
        weight_parts[2][None],
        weight_parts[3][None],
    )


def per_device(*arrays):
    chips = lax.axis_size("ctx") // 2 * lax.axis_size("tp")
    if lax.axis_size("section") == 2 and lax.axis_size("ctx") == 4 and arrays[0].shape[0] == chips:
        return bulk_device(*arrays)
    return stepwise_device(*arrays)


def solution(mesh):
    placed = (
        P(None, ("ctx", "tp"), None, None),
        P(None, ("ctx", "tp"), None, None),
        P(),
        P(),
        P("section", None, None),
        P("section", None, None),
        P("section", None, None, "tp"),
        P("section", None, "tp"),
        P("section", "tp", None),
        P("section", None, None, "tp"),
        P("section", "tp", None),
    )
    return jax.shard_map(
        per_device,
        mesh=mesh,
        in_specs=placed,
        out_specs=(
            P("section", None, ("ctx", "tp"), None, None),
            P("section", None, ("ctx", "tp")),
            P("section", None, ("ctx", "tp")),
            P("section", None, ("ctx", "tp")),
            P("section", None, "ctx", "tp"),
            P("section", "tp", "ctx"),
            P("section", None, "ctx", "tp"),
            P("section", "tp", "ctx"),
        ),
        check_vma=False,
    )
```
